32 devices in a mesh: groups: 2 (over x), tensor: 8 (over z, y), section: 2 (over core).
Axes of the slice: x: 2, y: 2, z: 4, core: 2. Of those that a mesh axis runs over, the one named last changes fastest.
Arguments:
- prompt_states: bfloat16 [4, 512, 8192], P(('groups', 'section'), 'tensor'), parts along dimension 0
- decode_states: bfloat16 [4, 32, 8192], P(('groups', 'section'), 'tensor'), parts along dimension 0
- norm_gain: bfloat16 [8192], replicated, may hold values from 0.099609375 to 1.8984375
- w_query: bfloat16 [8192, 4096], P(None, 'tensor'), may hold values from -0.0625 to 0.0625
- w_keyvalue: bfloat16 [8192, 2048], P(None, 'tensor'), may hold values from -0.0625 to 0.0625
- w_output: bfloat16 [4096, 8192], P('tensor'), may hold values from -0.09375 to 0.09375
- cache_pages: bfloat16 [4, 512, 16, 2048], P(('groups', 'section'), 'tensor'), parts along dimension 0
- page_table: int32 [4, 32, 16], P(('groups', 'section'), 'tensor'), parts along dimension 0, may hold values from 0 to 63, as said below
- cache_len: int32 [4, 32], P(('groups', 'section')), parts along dimension 0, may hold values from 1 to 252, as said below
- dest_rank: int32 [4, 4], P('groups'), parts along dimension 0, may hold values from 0 to 7, as said below
- dest_page: int32 [4, 4, 8], P('groups'), parts along dimension 0, may hold values from 0 to 63, as said below
Outputs:
- layer_outputs: bfloat16 [4, 4, 32, 8192], P(None, ('groups', 'section'), 'tensor'), parts along dimension 1
The draws below stay inside these ranges and needn't reach their ends.
There are 2 independent parts, one for each index of `groups`. The reference program is written for one: setup_inputs(seed, part) draws one part's arguments, and reference() takes and returns one part's arrays. A program takes and returns all parts, laid end to end along the dimension named above; an argument that names none is the same for every part. Nothing has to cross between parts.
Inputs may be any that keep to these rules, and one draw needn't show every extreme that they name: `page_table`: each device's table names each of its 64 local pages exactly once. `cache_len`: a request that receives a prompt has that prompt's length, 128 or fewer, and in each half one prompt has length 128; 252 is reached in every draw. `dest_rank`: distinct within a half. `dest_page`: the first 8 entries of the page table of one request of the receiving device.
All inputs are finite; a program needn't handle non-finite values.
Results may differ from the reference program's by a relative error of at most 0.03.
Values may be sent and summed in bfloat16 or wider, within the bound.
No kernel may reach another device: no remote copies, remote signals or barrier semaphores. Data moves between devices by JAX's collectives and lax.ppermute only.
A program may use at most 128 MiB of HBM per device.

```python
import math
import jax
import jax.numpy as jnp
from jax import lax

D = 8192
HEADS = 32
KVH = 8
HD = 128
PAGE = 16
MAXP = 16
PLEN = 128
STEPS = 4
REQ_DEV = 4
NP = 4
POOL = 64
PPG = 8
CAP = 252
N_TENSOR = 8
N_SECTION = 2


def layout(key):
    keys = jax.random.split(key, 8)
    halves = N_SECTION
    ranks = N_TENSOR
    orders = jax.vmap(lambda sub: jax.random.permutation(sub, POOL))(jax.random.split(keys[0], halves * ranks))
    tables = orders.reshape(halves, ranks, REQ_DEV, MAXP).astype(jnp.int32)
    ceilings = jax.random.randint(keys[1], (halves, ranks, 1), CAP // 4, CAP + 1) + 1
    lengths = jax.random.randint(keys[2], (halves, ranks, REQ_DEV), 1, ceilings).astype(jnp.int32)
    shuffled = jax.vmap(lambda sub: jax.random.permutation(sub, ranks))(jax.random.split(keys[3], halves)).astype(jnp.int32)
    targets = shuffled[:, :NP]
    spare = shuffled[:, NP]
    slots = jax.random.randint(keys[4], (halves, NP), 0, REQ_DEV).astype(jnp.int32)
    prompt_lengths = jax.random.randint(keys[5], (halves, NP), 1, PLEN + 1).astype(jnp.int32)
    longest = jax.random.randint(keys[6], (halves, 1), 0, NP)
    prompt_lengths = jnp.where(jnp.arange(NP)[None, :] == longest, PLEN, prompt_lengths).astype(jnp.int32)
    receiver = (jnp.arange(halves, dtype=jnp.int32) + 1) % halves
    lengths = lengths.at[receiver[:, None], targets, slots].set(prompt_lengths)
    full_slot = jax.random.randint(keys[7], (halves,), 0, REQ_DEV)
    lengths = lengths.at[receiver, spare, full_slot].set(CAP)
    landing = tables[receiver[:, None], targets, slots][:, :, :PPG]
    return (tables, lengths, targets, landing)


def draw_page_table(key, part):
    tables, lengths, targets, landing = layout(key)
    return tables.reshape(N_SECTION, N_TENSOR * REQ_DEV, MAXP).astype(jnp.int32)


def draw_cache_len(key, part):
    tables, lengths, targets, landing = layout(key)
    return lengths.reshape(N_SECTION, N_TENSOR * REQ_DEV).astype(jnp.int32)


def draw_dest_rank(key, part):
    tables, lengths, targets, landing = layout(key)
    return targets.astype(jnp.int32)


def draw_dest_page(key, part):
    tables, lengths, targets, landing = layout(key)
    return landing.astype(jnp.int32)


def draw_prompt_states(key, part):
    key = jax.random.fold_in(key, 11)
    first, second = jax.random.split(key, 2)
    count_rows = NP * PLEN
    scale = jnp.exp(jax.random.uniform(first, (N_SECTION, count_rows, 1), minval=math.log(0.3), maxval=math.log(3.0)))
    values = scale * jax.random.normal(second, (N_SECTION, count_rows, D))
    return values.astype(jnp.bfloat16)


def draw_decode_states(key, part):
    key = jax.random.fold_in(key, 12)
    first, second = jax.random.split(key, 2)
    count_rows = N_TENSOR * REQ_DEV
    scale = jnp.exp(jax.random.uniform(first, (N_SECTION, count_rows, 1), minval=math.log(0.05), maxval=math.log(0.5)))
    values = scale * jax.random.normal(second, (N_SECTION, count_rows, D))
    return values.astype(jnp.bfloat16)


def draw_cache_pages(key, part):
    key = jax.random.fold_in(key, 13)
    first = jax.random.fold_in(key, 0)
    total_pages = N_TENSOR * REQ_DEV * MAXP
    values = jax.random.normal(first, (N_SECTION, total_pages, PAGE, 2 * KVH, HD))
    return values.reshape(N_SECTION, total_pages, PAGE, 2 * KVH * HD).astype(jnp.bfloat16)


def level_of(own_key, shape, cuts, low, high):
    factor_of, own = 1.0, jax.random.fold_in(own_key, 6)
    for position, shards_of in cuts:
        draws = jnp.exp(jax.random.uniform(jax.random.fold_in(own, position), (shards_of,), jnp.float32, low / len(cuts), high / len(cuts)))
        factor_of = factor_of * jnp.repeat(draws, shape[position] // shards_of).reshape([-1 if axis == position else 1 for axis in range(len(shape))])
    return factor_of


def gaussian(stream_key, shape, scale, bound, cuts=(), kind=jnp.bfloat16):
    values = scale * jax.random.normal(stream_key, shape, jnp.float32)
    if cuts:
        values = values * level_of(stream_key, shape, cuts, -0.22, 0.18)
    return jnp.clip(values, -bound, bound).astype(kind)


def setup_inputs(seed: int = 0, part: int = 0) -> dict:
    key_of = jax.random.split(jax.random.key(seed), 12)
    part_splits = jax.random.split(jax.random.fold_in(key_of[11], part), 12)
    return {
        "prompt_states": draw_prompt_states(jax.random.fold_in(jax.random.fold_in(key_of[11], part), 71), part),
        "decode_states": draw_decode_states(jax.random.fold_in(jax.random.fold_in(key_of[11], part), 71), part),
        "norm_gain": jnp.clip(1.0 + 0.18 * jax.random.normal(key_of[2], (D,), jnp.float32), 0.099609375, 1.8984375).astype(jnp.bfloat16),
        "w_query": gaussian(key_of[3], (D, HEADS * HD), D ** -0.5, 0.0625, ((1, 8),)),
        "w_keyvalue": gaussian(key_of[4], (D, 2 * KVH * HD), D ** -0.5, 0.0625, ((1, 8),)),
        "w_output": gaussian(key_of[5], (HEADS * HD, D), (HEADS * HD) ** -0.5, 0.09375, ((0, 8),)),
        "cache_pages": draw_cache_pages(jax.random.fold_in(jax.random.fold_in(key_of[11], part), 71), part),
        "page_table": draw_page_table(jax.random.fold_in(jax.random.fold_in(key_of[11], part), 71), part),
        "cache_len": draw_cache_len(jax.random.fold_in(jax.random.fold_in(key_of[11], part), 71), part),
        "dest_rank": draw_dest_rank(jax.random.fold_in(jax.random.fold_in(key_of[11], part), 71), part),
        "dest_page": draw_dest_page(jax.random.fold_in(jax.random.fold_in(key_of[11], part), 71), part),
    }


EPS = 1e-05
ROPE_BASE = 500000.0

def normalize(rows, gain):
    values = rows.astype(jnp.float32)
    square = lax.optimization_barrier(jnp.mean(values * values, axis=-1, keepdims=True))
    return (values * lax.rsqrt(square + EPS) * gain.astype(jnp.float32)).astype(jnp.bfloat16)

def rotate(values, positions, head_dim):
    half_dim = head_dim // 2
    freqs = ROPE_BASE ** (-(jnp.arange(half_dim, dtype=jnp.float32) * 2.0 / head_dim))
    angles = positions.astype(jnp.float32)[:, None] * freqs[None, :]
    cosine = jnp.cos(angles)[:, None, :]
    sine = jnp.sin(angles)[:, None, :]
    first = values[..., :half_dim]
    second = values[..., half_dim:]
    return jnp.concatenate([first * cosine - second * sine, second * cosine + first * sine], axis=-1)

def rotate_keys(values, positions, first_col, head_dim):
    count_rows, columns = values.shape
    blocks = values.reshape(count_rows, columns // head_dim, head_dim)
    turned = rotate(blocks, positions, head_dim)
    block_index = first_col // head_dim + jnp.arange(columns // head_dim, dtype=jnp.int32)
    is_key = (block_index % 2 == 0)[None, :, None]
    return jnp.where(is_key, turned, blocks).reshape(count_rows, columns)

def attend(query, cache, positions, head_dim):
    count_rows, span, width = cache.shape
    kv_heads = width // (2 * head_dim)
    all_heads = query.shape[1] // head_dim
    paired = cache.astype(jnp.float32).reshape(count_rows, span, kv_heads, 2, head_dim)
    keys = paired[:, :, :, 0, :]
    values = paired[:, :, :, 1, :]
    grouped = query.astype(jnp.float32).reshape(count_rows, kv_heads, all_heads // kv_heads, head_dim)
    scores = jnp.einsum('rhgd,rlhd->rhgl', grouped, keys, precision=lax.Precision.HIGHEST) * head_dim ** (-0.5)
    visible = jnp.arange(span, dtype=jnp.int32)[None, :] <= positions[:, None]
    scores = jnp.where(visible[:, None, None, :], scores, -1e+30)
    top = lax.optimization_barrier(jnp.max(scores, axis=-1, keepdims=True))
    weights = jnp.exp(scores - top)
    weights = (weights / lax.optimization_barrier(jnp.sum(weights, axis=-1, keepdims=True))).astype(jnp.bfloat16)
    mixed = jnp.einsum('rhgl,rlhd->rhgd', weights.astype(jnp.float32), values, precision=lax.Precision.HIGHEST)
    return mixed.astype(jnp.bfloat16).reshape(count_rows, all_heads * head_dim)

def reference(prompt_states, decode_states, norm_gain, w_query, w_keyvalue, w_output, cache_pages, page_table, cache_len, dest_rank, dest_page):
    halves = N_SECTION
    ranks = N_TENSOR
    prompts = dest_rank.shape[1]
    kv_width = cache_pages.shape[3]
    flat_prompt = prompt_states.reshape(-1, D)
    normed_prompt = normalize(flat_prompt, norm_gain)
    values = jnp.dot(normed_prompt, w_keyvalue, preferred_element_type=jnp.float32)
    prompt_pos = jnp.arange(flat_prompt.shape[0], dtype=jnp.int32) % PLEN
    prompt_kv = rotate_keys(values, prompt_pos, 0, HD).astype(jnp.bfloat16)
    prompt_kv = prompt_kv.reshape(halves, prompts, PLEN // PAGE, PAGE, kv_width)
    page_pool = cache_pages.reshape(halves, ranks, -1, PAGE, kv_width)
    target_half = jnp.broadcast_to(((jnp.arange(halves, dtype=jnp.int32) + 1) % halves)[:, None, None], dest_page.shape)
    target_rank = jnp.broadcast_to(dest_rank[:, :, None], dest_page.shape)
    page_pool = page_pool.at[target_half, target_rank, dest_page].set(prompt_kv)
    tables = page_table.reshape(halves, ranks, -1, MAXP)
    lengths = cache_len.reshape(halves, ranks, -1)
    half_index = jnp.arange(halves, dtype=jnp.int32)[:, None, None]
    rank_index = jnp.arange(ranks, dtype=jnp.int32)[None, :, None]
    states = decode_states
    q_cols = w_query.shape[1] // ranks
    outputs = []
    for iteration in range(STEPS):
        positions = lengths + iteration
        flat_pos = positions.reshape(-1)
        normed = normalize(states.reshape(-1, D), norm_gain)
        query = jnp.dot(normed, w_query, preferred_element_type=jnp.float32)
        query = rotate(query.reshape(normed.shape[0], -1, HD), flat_pos, HD).reshape(normed.shape[0], -1).astype(jnp.bfloat16)
        new_kv = rotate_keys(jnp.dot(normed, w_keyvalue, preferred_element_type=jnp.float32), flat_pos, 0, HD).astype(jnp.bfloat16)
        slot_page = jnp.take_along_axis(tables, (positions // PAGE)[..., None], axis=3)[..., 0]
        page_pool = page_pool.at[half_index, rank_index, slot_page, positions % PAGE].set(new_kv.reshape(halves, ranks, -1, kv_width))
        cache = page_pool[half_index[..., None], rank_index[..., None], tables]
        mixed = attend(query, cache.reshape(flat_pos.shape[0], -1, kv_width), flat_pos, HD)
        shards = mixed.astype(jnp.float32).reshape(-1, ranks, q_cols)
        blocks = w_output.astype(jnp.float32).reshape(ranks, q_cols, D)
        partial_value = jnp.einsum('nrc,rcd->nrd', shards, blocks, precision=lax.Precision.HIGHEST)
        attention_out = lax.optimization_barrier(jnp.sum(partial_value.astype(jnp.bfloat16).astype(jnp.float32), axis=1))
        states = (states.astype(jnp.float32) + attention_out.reshape(halves, -1, D)).astype(jnp.bfloat16)
        outputs.append(states)
    return jnp.stack(outputs)
```

```python
import functools

import jax
import jax.numpy as jnp
from jax import lax
from jax.experimental import pallas as pl
from jax.experimental.pallas import tpu as pltpu
from jax.sharding import PartitionSpec as P

HD = 128
PLEN = 128
STEPS = 4
EPS = 1e-05
ROPE_BASE = 500000.0
LANES = 8
CHUNKS = 8
VMEM_LIMIT = 44 * 1024 * 1024


def ring_order(count):
    if count == 8:
        return [0, 2, 4, 6, 7, 5, 3, 1]
    return list(range(count))


def ring_shift(value, steps):
    count = lax.axis_size("tensor")
    order = ring_order(count)
    pairs = [(order[i], order[(i + steps) % count]) for i in range(count)]
    return lax.ppermute(value, "tensor", pairs)


def swap_xor(value, mask):
    count = lax.axis_size("tensor")
    return lax.ppermute(value, "tensor", [(s, s ^ mask) for s in range(count)])


def rope_tables(positions):
    half_dim = HD // 2
    freqs = ROPE_BASE ** (-(jnp.arange(half_dim, dtype=jnp.float32) * 2.0 / HD))
    angles = positions.astype(jnp.float32)[:, None] * freqs[None, :]
    cosine = jnp.cos(angles)
    sine = jnp.sin(angles)
    return (
        jnp.concatenate([cosine, cosine], axis=1),
        jnp.concatenate([-sine, sine], axis=1),
    )


def whole():
    return pl.BlockSpec(memory_space=pltpu.VMEM)


def normed_rows(values, gain):
    square = jnp.mean(values * values, axis=-1, keepdims=True)
    return values * lax.rsqrt(square + EPS) * gain


def prepare_kernel(prompt_ref, decode_ref, info_ref, gain_ref, first_ref, second_ref):
    half = first_ref.shape[0]
    gain = gain_ref[...].astype(jnp.float32)
    first_ref[...] = normed_rows(prompt_ref[:half, :].astype(jnp.float32), gain).astype(jnp.bfloat16)
    later = normed_rows(prompt_ref[half:, :].astype(jnp.float32), gain)
    states = normed_rows(decode_ref[...].astype(jnp.float32), gain)
    second_ref[...] = jnp.concatenate(
        [later, states, info_ref[...].astype(jnp.float32)], axis=0
    ).astype(jnp.bfloat16)


def prepare(prompts, decodes, info, gain):
    tokens, width = prompts.shape
    half = tokens // 2
    extra = decodes.shape[0] + info.shape[0]
    return pl.pallas_call(
        prepare_kernel,
        out_shape=(
            jax.ShapeDtypeStruct((half, width), jnp.bfloat16),
            jax.ShapeDtypeStruct((half + extra, width), jnp.bfloat16),
        ),
        in_specs=[whole()] * 4,
        out_specs=(whole(), whole()),
        compiler_params=pltpu.CompilerParams(vmem_limit_bytes=VMEM_LIMIT),
        name="prepare",
    )(prompts, decodes, info, gain)


def parcels_kernel(heads, table_ref, pool_ref, out_ref, held, load_sem, store_sem):
    pages = held.shape[0]
    width = out_ref.shape[-1]

    def load(index):
        return pltpu.make_async_copy(pool_ref.at[table_ref[index]], held.at[index], load_sem.at[index])

    for index in range(pages):
        load(index).start()
    for index in range(pages):
        load(index).wait()
    stores = []
    for target, head in enumerate(heads):
        copy = pltpu.make_async_copy(
            held.at[:, :, pl.ds(head * width, width)], out_ref.at[target], store_sem.at[target]
        )
        copy.start()
        stores.append(copy)
    for copy in stores:
        copy.wait()


def make_parcels(table, pool, heads, width):
    pages, rows, _ = pool.shape
    return pl.pallas_call(
        functools.partial(parcels_kernel, heads),
        out_shape=jax.ShapeDtypeStruct((len(heads), pages, rows, width), jnp.bfloat16),
        in_specs=[pl.BlockSpec(memory_space=pltpu.SMEM), pl.BlockSpec(memory_space=pl.ANY)],
        out_specs=pl.BlockSpec(memory_space=pl.ANY),
        scratch_shapes=[
            pltpu.VMEM(pool.shape, jnp.bfloat16),
            pltpu.SemaphoreType.DMA((pages,)),
            pltpu.SemaphoreType.DMA((len(heads),)),
        ],
        compiler_params=pltpu.CompilerParams(vmem_limit_bytes=VMEM_LIMIT),
        name="parcels",
    )(table, pool)


def patch_kernel(rows, request_ref, offset_ref, arrived_ref, _cache_in, cache_ref, sems):
    copies = []
    for piece in range(arrived_ref.shape[0] // rows):
        offset = pl.multiple_of(offset_ref[piece], rows)
        copy = pltpu.make_async_copy(
            arrived_ref.at[pl.ds(piece * rows, rows), :],
            cache_ref.at[request_ref[piece], pl.ds(offset, rows), :],
            sems.at[piece],
        )
        copy.start()
        copies.append(copy)
    for copy in copies:
        copy.wait()


def patch(requests, offsets, arrived, cache, rows):
    return pl.pallas_call(
        functools.partial(patch_kernel, rows),
        out_shape=jax.ShapeDtypeStruct(cache.shape, cache.dtype),
        in_specs=[
            pl.BlockSpec(memory_space=pltpu.SMEM),
            pl.BlockSpec(memory_space=pltpu.SMEM),
            pl.BlockSpec(memory_space=pl.ANY),
            pl.BlockSpec(memory_space=pl.ANY),
        ],
        out_specs=pl.BlockSpec(memory_space=pl.ANY),
        scratch_shapes=[pltpu.SemaphoreType.DMA((arrived.shape[0] // rows,))],
        input_output_aliases={3: 0},
        compiler_params=pltpu.CompilerParams(vmem_limit_bytes=VMEM_LIMIT),
        name="patch",
    )(requests, offsets, arrived, cache)


def turn(values, cosine, sine):
    return values * cosine + pltpu.roll(values, HD // 2, 1) * sine


def step_kernel(
    blocks,
    earlier,
    *refs,
):
    x_refs = refs[:blocks]
    refs = refs[blocks:]
    order_ref, wq, wkv, wo, cache, mask_ref, cos_ref, sin_ref = refs[:8]
    refs = refs[8:]
    new_refs = refs[:earlier]
    out_ref, fresh_ref = refs[earlier : earlier + 2]
    (x_rows, wq_s, wkv_s, wo_s, cache_s, q_s, score_s, mix_s, new_s, sems) = refs[earlier + 2 :]
    each, width = x_refs[0].shape
    count = blocks * each
    q_cols = wq_s.shape[1]
    heads = q_cols // HD
    depth = width // CHUNKS
    group = count // CHUNKS

    loads = []
    for c in range(CHUNKS):
        span = pl.ds(c * depth, depth)
        loads.append(pltpu.make_async_copy(wq.at[span, :], wq_s.at[span, :], sems.at[0, c]))
        loads.append(pltpu.make_async_copy(wkv.at[span, :], wkv_s.at[span, :], sems.at[1, c]))
    for c in range(CHUNKS):
        span = pl.ds(c * group, group)
        loads.append(pltpu.make_async_copy(cache.at[span], cache_s.at[span], sems.at[2, c]))
    for c in range(CHUNKS):
        span = pl.ds(c * depth, depth)
        loads.append(pltpu.make_async_copy(wo.at[:, span], wo_s.at[:, span], sems.at[3, c]))
    for copy in loads:
        copy.start()

    for k in range(blocks):
        x_rows[k * each : (k + 1) * each, :] = x_refs[k][...].astype(jnp.float32)
    order = order_ref[...]
    q_s[...] = jnp.zeros_like(q_s)

    query = jnp.zeros((count, q_cols), jnp.float32)
    keyvalue = jnp.zeros((count, 2 * HD), jnp.float32)
    for c in range(CHUNKS):
        span = slice(c * depth, (c + 1) * depth)
        x = jnp.dot(
            order, x_rows[:, span].astype(jnp.bfloat16), preferred_element_type=jnp.float32
        ).astype(jnp.bfloat16)
        loads[2 * c].wait()
        query += jnp.dot(x, wq_s[span, :], preferred_element_type=jnp.float32)
        loads[2 * c + 1].wait()
        keyvalue += jnp.dot(x, wkv_s[span, :], preferred_element_type=jnp.float32)

    cosine = cos_ref[...]
    sine = sin_ref[...]
    key = turn(keyvalue[:, :HD], cosine, sine).astype(jnp.bfloat16)
    value = keyvalue[:, HD:].astype(jnp.bfloat16)
    fresh_ref[:, :HD] = key
    fresh_ref[:, HD:] = value
    for j in range(heads):
        turned = turn(query[:, j * HD : (j + 1) * HD], cosine, sine).astype(jnp.bfloat16)
        lane = pl.ds(j, count, LANES)
        q_s[lane, :] = turned.astype(jnp.float32)
        for t in range(earlier):
            new_s[t, 0, lane, :] = new_refs[t][:, :HD].astype(jnp.float32)
            new_s[t, 1, lane, :] = new_refs[t][:, HD:].astype(jnp.float32)
        new_s[earlier, 0, lane, :] = key.astype(jnp.float32)
        new_s[earlier, 1, lane, :] = value.astype(jnp.float32)
    for j in range(heads, LANES):
        lane = pl.ds(j, count, LANES)
        for t in range(earlier + 1):
            for part in range(2):
                new_s[t, part, lane, :] = jnp.zeros((count, HD), jnp.float32)

    base = 2 * CHUNKS
    for r in range(count):
        if r % group == 0:
            loads[base + r // group].wait()
        rows = slice(r * LANES, (r + 1) * LANES)
        score_s[rows, :] = lax.dot_general(
            q_s[rows, :].astype(jnp.bfloat16),
            cache_s[r, :, :HD],
            (((1,), (1,)), ((), ())),
            preferred_element_type=jnp.float32,
        )

    scale = HD**-0.5
    span = score_s.shape[1]
    scores = score_s[...].reshape(count, LANES, span) * scale + mask_ref[...]
    queries = q_s[...]
    fresh_scores = [
        (jnp.sum(queries * new_s[t, 0], axis=-1, keepdims=True) * scale).reshape(count, LANES, 1)
        for t in range(earlier + 1)
    ]
    top = jnp.max(scores, axis=-1, keepdims=True)
    for s in fresh_scores:
        top = jnp.maximum(top, s)
    weights = jnp.exp(scores - top)
    fresh_weights = [jnp.exp(s - top) for s in fresh_scores]
    total = jnp.sum(weights, axis=-1, keepdims=True)
    for w in fresh_weights:
        total = total + w
    score_s[...] = (weights / total).reshape(count * LANES, span)
    fresh_weights = [
        (w / total).reshape(count * LANES, 1).astype(jnp.bfloat16).astype(jnp.float32)
        for w in fresh_weights
    ]
    for r in range(count):
        rows = slice(r * LANES, (r + 1) * LANES)
        mix_s[rows, :] = jnp.dot(
            score_s[rows, :].astype(jnp.bfloat16),
            cache_s[r, :, HD:],
            preferred_element_type=jnp.float32,
        )
    mixed = mix_s[...]
    for t in range(earlier + 1):
        mixed = mixed + fresh_weights[t] * new_s[t, 1]
    mix_s[...] = mixed
    columns = jnp.concatenate(
        [mix_s[pl.ds(j, count, LANES), :].astype(jnp.bfloat16) for j in range(heads)], axis=1
    )

    base = 3 * CHUNKS
    for c in range(CHUNKS):
        span = slice(c * depth, (c + 1) * depth)
        loads[base + c].wait()
        part = jnp.dot(columns, wo_s[:, span], preferred_element_type=jnp.float32)
        for d in range(blocks):
            out_ref[d, :, span] = part[d * each : (d + 1) * each, :].astype(jnp.bfloat16)


def step(x_blocks, order, wq, wkv, wo, cache, mask, cosine, sine, earlier):
    blocks = len(x_blocks)
    each, width = x_blocks[0].shape
    count = blocks * each
    span = cache.shape[1]
    anywhere = pl.BlockSpec(memory_space=pl.ANY)
    q_cols = wq.shape[1]
    return pl.pallas_call(
        functools.partial(step_kernel, blocks, len(earlier)),
        out_shape=(
            jax.ShapeDtypeStruct((blocks, each, width), jnp.bfloat16),
            jax.ShapeDtypeStruct((count, 2 * HD), jnp.bfloat16),
        ),
        in_specs=[whole()] * (blocks + 1) + [anywhere] * 4 + [whole()] * (3 + len(earlier)),
        out_specs=(whole(), whole()),
        scratch_shapes=[
            pltpu.VMEM((count, width), jnp.float32),
            pltpu.VMEM(wq.shape, jnp.bfloat16),
            pltpu.VMEM(wkv.shape, jnp.bfloat16),
            pltpu.VMEM(wo.shape, jnp.bfloat16),
            pltpu.VMEM(cache.shape, jnp.bfloat16),
            pltpu.VMEM((count * LANES, HD), jnp.float32),
            pltpu.VMEM((count * LANES, span), jnp.float32),
            pltpu.VMEM((count * LANES, HD), jnp.float32),
            pltpu.VMEM((len(earlier) + 1, 2, count * LANES, HD), jnp.float32),
            pltpu.SemaphoreType.DMA((4, CHUNKS)),
        ],
        compiler_params=pltpu.CompilerParams(vmem_limit_bytes=VMEM_LIMIT),
        cost_estimate=pl.CostEstimate(
            flops=2 * count * width * (2 * q_cols + 2 * HD),
            bytes_accessed=2 * (2 * wq.size + wkv.size + cache.size),
            transcendentals=count * LANES * span,
        ),
        name="decode_step",
    )(*x_blocks, order, wq, wkv, wo, cache, mask, cosine, sine, *earlier)


def settle_kernel(parts_ref, state_ref, gain_ref, next_ref, normed_ref):
    total = parts_ref[0].astype(jnp.float32)
    for d in range(1, parts_ref.shape[0]):
        total = total + parts_ref[d].astype(jnp.float32)
    state = (state_ref[...].astype(jnp.float32) + total).astype(jnp.bfloat16)
    next_ref[...] = state
    gain = gain_ref[...].astype(jnp.float32)
    normed_ref[...] = normed_rows(state.astype(jnp.float32), gain).astype(jnp.bfloat16)


def settle(parts, state, gain):
    shape = jax.ShapeDtypeStruct(state.shape, jnp.bfloat16)
    return pl.pallas_call(
        settle_kernel,
        out_shape=(shape, shape),
        in_specs=[whole()] * 3,
        out_specs=(whole(), whole()),
        compiler_params=pltpu.CompilerParams(vmem_limit_bytes=VMEM_LIMIT),
        name="settle",
    )(parts, state, gain)


def on_device(
    prompt_states,
    decode_states,
    norm_gain,
    w_query,
    w_keyvalue,
    w_output,
    cache_pages,
    page_table,
    cache_len,
    dest_rank,
    dest_page,
):
    rank = lax.axis_index("tensor")
    section = lax.axis_index("section")
    count = lax.axis_size("tensor")
    pool = cache_pages[0]
    page_size, kv_width = pool.shape[1:]
    own_table = page_table[0]
    lengths = cache_len[0]
    each, width = decode_states.shape[1:]
    tokens = prompt_states.shape[1]
    q_cols = w_query.shape[1]
    kv_heads = kv_width // (2 * HD)
    shared = count // kv_heads if count > kv_heads else 1
    gain = norm_gain[None, :]

    if w_keyvalue.shape[1] < 2 * HD:
        other = swap_xor(w_keyvalue, 1)
        is_key = rank % 2 == 0
        w_kv = jnp.concatenate(
            [jnp.where(is_key, w_keyvalue, other), jnp.where(is_key, other, w_keyvalue)], axis=1
        )
    else:
        w_kv = w_keyvalue

    heads = tuple(target // shared for target in range(count))
    parcels = make_parcels(own_table.reshape(-1), pool, heads, 2 * HD)
    span = own_table.shape[1] * page_size
    cache = lax.all_to_all(
        parcels.reshape(count, each * span, 2 * HD), "tensor", split_axis=0, concat_axis=0, tiled=True
    ).reshape(count * each, span, 2 * HD)

    info = jnp.zeros((LANES - each, width), jnp.bfloat16)
    info = info.at[0, :each].set(own_table[:, 0].astype(jnp.bfloat16))
    first, second = prepare(prompt_states[0], decode_states[0], info, gain)
    order = ring_order(count)
    place = jnp.array([order.index(r) for r in range(count)], jnp.int32)[rank]
    ring = jnp.array(order, jnp.int32)
    half = tokens // 2
    arrivals = [(rank, 0, first), (rank, 1, second)]
    going = [[first, first], [second, second]]
    for hop in range(1, count // 2 + 1):
        for piece in range(2):
            for way in range(2):
                if hop == count // 2 and piece != way:
                    continue
                sign = 1 if way == 0 else -1
                going[piece][way] = ring_shift(going[piece][way], sign)
                source = ring[(place - sign * hop) % count]
                arrivals.append((source, piece, going[piece][way]))
    products = [
        jnp.dot(rows, w_kv, preferred_element_type=jnp.float32)[:half] for _, _, rows in arrivals
    ]
    starts = jnp.stack([source * tokens + piece * half for source, piece, _ in arrivals])
    row_index = (starts[:, None] + jnp.arange(half, dtype=jnp.int32)[None, :]).reshape(-1)
    cosine, sine = rope_tables(row_index % PLEN)
    values = jnp.concatenate(products, axis=0)
    keys = values[:, :HD]
    keys = keys * cosine + jnp.roll(keys, HD // 2, axis=1) * sine
    prompt_kv = jnp.concatenate([keys, values[:, HD:]], axis=1).astype(jnp.bfloat16)
    sections = lax.axis_size("section")
    arrived = lax.ppermute(prompt_kv, "section", [(s, (s + 1) % sections) for s in range(sections)])

    seconds = [(source, rows) for source, piece, rows in arrivals if piece == 1]
    sources = jnp.stack([source for source, _ in seconds])
    first_pages = jnp.stack([rows[half + each, :each] for _, rows in seconds]).astype(jnp.int32)
    anchor = (section + 1) % sections
    targets = lax.dynamic_index_in_dim(dest_rank, anchor, 0, keepdims=False)
    landing = lax.dynamic_index_in_dim(dest_page, anchor, 0, keepdims=False)[:, 0]
    here = (sources[None, :, None] == targets[:, None, None]) & (
        first_pages[None] == landing[:, None, None]
    )
    numbers = sources[:, None] * each + jnp.arange(each, dtype=jnp.int32)[None, :]
    receivers = jnp.sum(jnp.where(here, numbers[None], 0), axis=(1, 2))
    cache = patch(receivers[starts // PLEN], starts % PLEN, arrived, cache, half)

    visible = jnp.arange(span, dtype=jnp.int32)[None, :] < lengths[:, None]
    mask = jnp.where(visible, 0.0, -1e30).astype(jnp.float32)[:, None, :]
    state = decode_states[0]
    blocks = [rows[half : half + each] for _, rows in seconds]
    outputs = []
    earlier = []
    for iteration in range(STEPS):
        rows_of = (sources[:, None] * each + jnp.arange(each, dtype=jnp.int32)[None, :]).reshape(-1)
        chosen = (jnp.arange(count * each, dtype=jnp.int32)[:, None] == rows_of[None, :]).astype(
            jnp.bfloat16
        )
        cosine, sine = rope_tables(lengths + iteration)
        parts, fresh = step(
            blocks, chosen, w_query, w_kv, w_output, cache, mask, cosine, sine, earlier
        )
        earlier.append(fresh)
        parts = lax.all_to_all(parts, "tensor", split_axis=0, concat_axis=0, tiled=True)
        state, normed = settle(parts, state, gain)
        outputs.append(state)
        if iteration + 1 < STEPS:
            blocks = [normed] + [swap_xor(normed, mask_bits) for mask_bits in range(1, count)]
            sources = rank ^ jnp.arange(count, dtype=jnp.int32)
    return jnp.stack(outputs)[:, None]


def solution(mesh):
    in_specs = (
        P(("groups", "section"), "tensor", None),
        P(("groups", "section"), "tensor", None),
        P(),
        P(None, "tensor"),
        P(None, "tensor"),
        P("tensor", None),
        P(("groups", "section"), "tensor", None, None),
        P(("groups", "section"), "tensor", None),
        P(("groups", "section"), None),
        P("groups", None),
        P("groups", None, None),
    )
    out_specs = P(None, ("groups", "section"), "tensor", None)
    return jax.shard_map(
        on_device, mesh=mesh, in_specs=in_specs, out_specs=out_specs, check_vma=False
    )
```

```python
import functools

import jax
import jax.numpy as jnp
from jax import lax
from jax.experimental import pallas as pl
from jax.experimental.pallas import tpu as pltpu
from jax.sharding import PartitionSpec as P

HD = 128
PLEN = 128
STEPS = 4
EPS = 1e-05
ROPE_BASE = 500000.0
LANES = 8
CHUNKS = 8
VMEM_LIMIT = 16 * 1024 * 1024


def ring_order(count):
    if count == 8:
        return [0, 2, 4, 6, 7, 5, 3, 1]
    return list(range(count))


def ring_shift(value, steps):
    count = lax.axis_size("tensor")
    order = ring_order(count)
    pairs = [(order[i], order[(i + steps) % count]) for i in range(count)]
    return lax.ppermute(value, "tensor", pairs)


def swap_xor(value, mask):
    count = lax.axis_size("tensor")
    return lax.ppermute(value, "tensor", [(s, s ^ mask) for s in range(count)])


def rope_tables(positions):
    half_dim = HD // 2
    freqs = ROPE_BASE ** (-(jnp.arange(half_dim, dtype=jnp.float32) * 2.0 / HD))
    angles = positions.astype(jnp.float32)[:, None] * freqs[None, :]
    cosine = jnp.cos(angles)
    sine = jnp.sin(angles)
    return (
        jnp.concatenate([cosine, cosine], axis=1),
        jnp.concatenate([-sine, sine], axis=1),
    )


def whole():
    return pl.BlockSpec(memory_space=pltpu.VMEM)


def normed_rows(values, gain):
    square = jnp.mean(values * values, axis=-1, keepdims=True)
    return values * lax.rsqrt(square + EPS) * gain


def normalize_kernel(rows_ref, gain_ref, out_ref):
    gain = gain_ref[...].astype(jnp.float32)
    out_ref[...] = normed_rows(rows_ref[...].astype(jnp.float32), gain).astype(jnp.bfloat16)


def normalize(rows, gain):
    return pl.pallas_call(
        normalize_kernel,
        out_shape=jax.ShapeDtypeStruct(rows.shape, jnp.bfloat16),
        in_specs=[whole()] * 2,
        out_specs=whole(),
        compiler_params=pltpu.CompilerParams(vmem_limit_bytes=VMEM_LIMIT),
        name="normalize",
    )(rows, gain)


def fetch_kernel(*refs):
    count = len(refs) // 2
    sems = refs[-1]
    copies = [pltpu.make_async_copy(refs[i], refs[count + i], sems.at[i]) for i in range(count)]
    for copy in copies:
        copy.start()
    for copy in copies:
        copy.wait()


def fetch(*arrays):
    return pl.pallas_call(
        fetch_kernel,
        out_shape=tuple(pltpu.VMEM(a.shape, a.dtype) for a in arrays),
        in_specs=[pl.BlockSpec(memory_space=pl.ANY)] * len(arrays),
        out_specs=tuple(whole() for _ in arrays),
        scratch_shapes=[pltpu.SemaphoreType.DMA((len(arrays),))],
        compiler_params=pltpu.CompilerParams(vmem_limit_bytes=VMEM_LIMIT),
        name="fetch",
    )(*arrays)


def parcels_kernel(heads, table_ref, pool_ref, out_ref, held, load_sem, store_sem):
    pages = held.shape[0]
    width = out_ref.shape[-1]

    def load(index):
        return pltpu.make_async_copy(pool_ref.at[table_ref[index]], held.at[index], load_sem.at[index])

    for index in range(pages):
        load(index).start()
    for index in range(pages):
        load(index).wait()
    stores = []
    for target, head in enumerate(heads):
        copy = pltpu.make_async_copy(
            held.at[:, :, pl.ds(head * width, width)], out_ref.at[target], store_sem.at[target]
        )
        copy.start()
        stores.append(copy)
    for copy in stores:
        copy.wait()


def make_parcels(table, pool, heads, width):
    pages, rows, _ = pool.shape
    return pl.pallas_call(
        functools.partial(parcels_kernel, heads),
        out_shape=jax.ShapeDtypeStruct((len(heads), pages, rows, width), jnp.bfloat16),
        in_specs=[pl.BlockSpec(memory_space=pltpu.SMEM), pl.BlockSpec(memory_space=pl.ANY)],
        out_specs=pl.BlockSpec(memory_space=pl.ANY),
        scratch_shapes=[
            pltpu.VMEM(pool.shape, jnp.bfloat16),
            pltpu.SemaphoreType.DMA((pages,)),
            pltpu.SemaphoreType.DMA((len(heads),)),
        ],
        compiler_params=pltpu.CompilerParams(vmem_limit_bytes=VMEM_LIMIT),
        name="parcels",
    )(table, pool)


def assemble_kernel(rows, request_ref, offset_ref, arrived_ref, cache_ref, out_ref, sems):
    fetched = pltpu.make_async_copy(cache_ref, out_ref, sems.at[0])
    fetched.start()
    fetched.wait()
    copies = []
    for piece in range(arrived_ref.shape[0] // rows):
        offset = pl.multiple_of(offset_ref[piece], rows)
        copy = pltpu.make_async_copy(
            arrived_ref.at[pl.ds(piece * rows, rows), :],
            out_ref.at[request_ref[piece], pl.ds(offset, rows), :],
            sems.at[piece + 1],
        )
        copy.start()
        copies.append(copy)
    for copy in copies:
        copy.wait()


def assemble(requests, offsets, arrived, cache, rows):
    smem = pl.BlockSpec(memory_space=pltpu.SMEM)
    anywhere = pl.BlockSpec(memory_space=pl.ANY)
    return pl.pallas_call(
        functools.partial(assemble_kernel, rows),
        out_shape=pltpu.VMEM(cache.shape, cache.dtype),
        in_specs=[smem, smem, anywhere, anywhere],
        out_specs=whole(),
        scratch_shapes=[pltpu.SemaphoreType.DMA((arrived.shape[0] // rows + 1,))],
        compiler_params=pltpu.CompilerParams(vmem_limit_bytes=VMEM_LIMIT),
        name="assemble",
    )(requests, offsets, arrived, cache)


def turn(values, cosine, sine):
    return values * cosine + pltpu.roll(values, HD // 2, 1) * sine


def step_kernel(blocks, iteration, *refs):
    x_refs = refs[:blocks]
    order_ref, lens_ref, wq, wkv, wo, cache, cos_ref, sin_ref = refs[blocks : blocks + 8]
    new_refs = refs[blocks + 8 : blocks + 8 + iteration]
    out_ref, fresh_ref, x_rows, q_s, score_s, mix_s, new_s = refs[blocks + 8 + iteration :]
    width, q_cols = wq.shape
    count, span = cache.shape[:2]
    each = count // out_ref.shape[0]
    heads = q_cols // HD
    depth = width // CHUNKS

    if blocks > 1:
        for k in range(blocks):
            x_rows[k * each : (k + 1) * each, :] = x_refs[k][...].astype(jnp.float32)
        order = order_ref[...]

    query = jnp.zeros((count, q_cols), jnp.float32)
    keyvalue = jnp.zeros((count, 2 * HD), jnp.float32)
    for c in range(CHUNKS):
        part = slice(c * depth, (c + 1) * depth)
        if blocks > 1:
            x = jnp.dot(
                order, x_rows[:, part].astype(jnp.bfloat16), preferred_element_type=jnp.float32
            ).astype(jnp.bfloat16)
        else:
            x = x_refs[0][:, part]
        query += jnp.dot(x, wq[part, :], preferred_element_type=jnp.float32)
        keyvalue += jnp.dot(x, wkv[part, :], preferred_element_type=jnp.float32)

    cosine = cos_ref[iteration]
    sine = sin_ref[iteration]
    key = turn(keyvalue[:, :HD], cosine, sine).astype(jnp.bfloat16)
    value = keyvalue[:, HD:].astype(jnp.bfloat16)
    fresh_ref[:, :HD] = key
    fresh_ref[:, HD:] = value
    news = [(ref[:, :HD], ref[:, HD:]) for ref in new_refs] + [(key, value)]
    for j in range(LANES):
        lane = pl.ds(j, count, LANES)
        if j < heads:
            turned = turn(query[:, j * HD : (j + 1) * HD], cosine, sine).astype(jnp.bfloat16)
            q_s[lane, :] = turned.astype(jnp.float32)
        else:
            q_s[lane, :] = jnp.zeros((count, HD), jnp.float32)
        for t, pair in enumerate(news):
            for half in range(2):
                new_s[t, half, lane, :] = pair[half].astype(jnp.float32)

    scale = HD**-0.5
    column = lax.broadcasted_iota(jnp.int32, (LANES, span), 1)
    for r in range(count):
        rows = slice(r * LANES, (r + 1) * LANES)
        found = lax.dot_general(
            q_s[rows, :].astype(jnp.bfloat16),
            cache[r, :, :HD],
            (((1,), (1,)), ((), ())),
            preferred_element_type=jnp.float32,
        )
        score_s[rows, :] = jnp.where(column < lens_ref[r], found * scale, -1e30)

    scores = score_s[...]
    queries = q_s[...]
    fresh_scores = [
        jnp.sum(queries * new_s[t, 0], axis=-1, keepdims=True) * scale for t in range(iteration + 1)
    ]
    top = jnp.max(scores, axis=-1, keepdims=True)
    for s in fresh_scores:
        top = jnp.maximum(top, s)
    weights = jnp.exp(scores - top)
    fresh_weights = [jnp.exp(s - top) for s in fresh_scores]
    total = jnp.sum(weights, axis=-1, keepdims=True)
    for w in fresh_weights:
        total = total + w
    score_s[...] = weights / total
    row = lax.broadcasted_iota(jnp.int32, (span, HD), 0)
    for r in range(count):
        rows = slice(r * LANES, (r + 1) * LANES)
        mix_s[rows, :] = jnp.dot(
            score_s[rows, :].astype(jnp.bfloat16),
            jnp.where(row < lens_ref[r], cache[r, :, HD:], jnp.zeros((), jnp.bfloat16)),
            preferred_element_type=jnp.float32,
        )
    mixed = mix_s[...]
    for t in range(iteration + 1):
        weight = (fresh_weights[t] / total).astype(jnp.bfloat16).astype(jnp.float32)
        mixed = mixed + weight * new_s[t, 1]
    mix_s[...] = mixed
    columns = jnp.concatenate(
        [mix_s[pl.ds(j, count, LANES), :].astype(jnp.bfloat16) for j in range(heads)], axis=1
    )
    for c in range(CHUNKS):
        part = slice(c * depth, (c + 1) * depth)
        product = jnp.dot(columns, wo[:, part], preferred_element_type=jnp.float32)
        for d in range(count // each):
            out_ref[d, :, part] = product[d * each : (d + 1) * each, :].astype(jnp.bfloat16)


def step(x_blocks, order, lengths, wq, wkv, wo, cache, cosine, sine, earlier, owners):
    width, q_cols = wq.shape
    count, span = cache.shape[:2]
    each = count // owners
    iteration = len(earlier)
    blocks = len(x_blocks)
    smem = pl.BlockSpec(memory_space=pltpu.SMEM)
    return pl.pallas_call(
        functools.partial(step_kernel, blocks, iteration),
        out_shape=(
            jax.ShapeDtypeStruct((owners, each, width), jnp.bfloat16),
            jax.ShapeDtypeStruct((count, 2 * HD), jnp.bfloat16),
        ),
        in_specs=[whole()] * (blocks + 1) + [smem] + [whole()] * (6 + iteration),
        out_specs=(whole(), whole()),
        scratch_shapes=[
            pltpu.VMEM((count, width), jnp.float32),
            pltpu.VMEM((count * LANES, HD), jnp.float32),
            pltpu.VMEM((count * LANES, span), jnp.float32),
            pltpu.VMEM((count * LANES, HD), jnp.float32),
            pltpu.VMEM((iteration + 1, 2, count * LANES, HD), jnp.float32),
        ],
        compiler_params=pltpu.CompilerParams(vmem_limit_bytes=VMEM_LIMIT),
        cost_estimate=pl.CostEstimate(
            flops=2 * count * width * (2 * q_cols + 2 * HD),
            bytes_accessed=2 * (2 * wq.size + wkv.size + cache.size),
            transcendentals=count * LANES * span,
        ),
        name="decode_step",
    )(*x_blocks, order, lengths, wq, wkv, wo, cache, cosine, sine, *earlier)


def settle_kernel(parts_ref, state_ref, gain_ref, next_ref, normed_ref):
    total = parts_ref[0].astype(jnp.float32)
    for d in range(1, parts_ref.shape[0]):
        total = total + parts_ref[d].astype(jnp.float32)
    state = (state_ref[...].astype(jnp.float32) + total).astype(jnp.bfloat16)
    next_ref[...] = state
    gain = gain_ref[...].astype(jnp.float32)
    normed_ref[...] = normed_rows(state.astype(jnp.float32), gain).astype(jnp.bfloat16)


def settle(parts, state, gain):
    shape = jax.ShapeDtypeStruct(state.shape, jnp.bfloat16)
    return pl.pallas_call(
        settle_kernel,
        out_shape=(shape, shape),
        in_specs=[whole()] * 3,
        out_specs=(whole(), whole()),
        compiler_params=pltpu.CompilerParams(vmem_limit_bytes=VMEM_LIMIT),
        name="settle",
    )(parts, state, gain)


def on_device(
    prompt_states,
    decode_states,
    norm_gain,
    w_query,
    w_keyvalue,
    w_output,
    cache_pages,
    page_table,
    cache_len,
    dest_rank,
    dest_page,
):
    rank = lax.axis_index("tensor")
    section = lax.axis_index("section")
    count = lax.axis_size("tensor")
    pool = cache_pages[0]
    page_size, kv_width = pool.shape[1:]
    own_table = page_table[0]
    lengths = cache_len[0]
    each, width = decode_states.shape[1:]
    tokens = prompt_states.shape[1]
    q_cols = w_query.shape[1]
    kv_heads = kv_width // (2 * HD)
    shared = count // kv_heads if count > kv_heads else 1
    gain = norm_gain[None, :]

    if w_keyvalue.shape[1] < 2 * HD:
        other = swap_xor(w_keyvalue, 1)
        is_key = rank % 2 == 0
        w_kv = jnp.concatenate(
            [jnp.where(is_key, w_keyvalue, other), jnp.where(is_key, other, w_keyvalue)], axis=1
        )
    else:
        w_kv = w_keyvalue

    w_q, w_kv, w_o = fetch(w_query, w_kv, w_output)
    first_pages = lax.all_gather(own_table[:, 0], "tensor", axis=0)
    states = lax.all_gather(normalize(decode_states[0], gain), "tensor", axis=0, tiled=True)

    heads = tuple(target // shared for target in range(count))
    parcels = make_parcels(own_table.reshape(-1), pool, heads, 2 * HD)
    span = own_table.shape[1] * page_size
    cache = lax.all_to_all(
        parcels.reshape(count, each * span, 2 * HD), "tensor", split_axis=0, concat_axis=0, tiled=True
    ).reshape(count * each, span, 2 * HD)

    half = tokens // 2
    ready = normalize(prompt_states[0], gain)
    pieces = [ready[:half], ready[half:]]
    order = ring_order(count)
    place = jnp.array([order.index(r) for r in range(count)], jnp.int32)[rank]
    ring = jnp.array(order, jnp.int32)
    arrivals = [(0, 0, pieces[0]), (0, 1, pieces[1])]
    going = [[piece, piece] for piece in pieces]
    for hop in range(1, count // 2 + 1):
        for piece in range(2):
            for way in range(2):
                if hop == count // 2 and piece != way:
                    continue
                sign = 1 if way == 0 else -1
                going[piece][way] = ring_shift(going[piece][way], sign)
                arrivals.append((-sign * hop, piece, going[piece][way]))
    products = [
        jnp.dot(rows, w_kv, preferred_element_type=jnp.float32) for _, _, rows in arrivals
    ]
    behind = jnp.array([steps for steps, _, _ in arrivals], jnp.int32)
    halves = jnp.array([piece for _, piece, _ in arrivals], jnp.int32)
    starts = ring[(place + behind) % count] * tokens + halves * half
    row_index = (starts[:, None] + jnp.arange(half, dtype=jnp.int32)[None, :]).reshape(-1)
    cosine, sine = rope_tables(row_index % PLEN)
    values = jnp.concatenate(products, axis=0)
    keys = values[:, :HD]
    keys = keys * cosine + jnp.roll(keys, HD // 2, axis=1) * sine
    prompt_kv = jnp.concatenate([keys, values[:, HD:]], axis=1).astype(jnp.bfloat16)
    sections = lax.axis_size("section")
    arrived = lax.ppermute(prompt_kv, "section", [(s, (s + 1) % sections) for s in range(sections)])

    anchor = (section + 1) % sections
    targets = lax.dynamic_index_in_dim(dest_rank, anchor, 0, keepdims=False)
    landing = lax.dynamic_index_in_dim(dest_page, anchor, 0, keepdims=False)[:, 0]
    numbers = jnp.arange(count * each, dtype=jnp.int32)
    here = (numbers[None, :] // each == targets[:, None]) & (
        first_pages.reshape(1, -1) == landing[:, None]
    )
    receivers = jnp.sum(jnp.where(here, numbers[None, :], 0), axis=1)
    cache = assemble(receivers[starts // PLEN], starts % PLEN, arrived, cache, half)

    times = lengths[None, :] + jnp.arange(STEPS, dtype=jnp.int32)[:, None]
    cosine, sine = rope_tables(times.reshape(-1))
    cosine = cosine.reshape(STEPS, count * each, HD)
    sine = sine.reshape(STEPS, count * each, HD)
    rows_of = ((rank ^ (numbers // each)) * each + numbers % each)[None, :]
    chosen = (numbers[:, None] == rows_of).astype(jnp.bfloat16)
    state = decode_states[0]
    blocks = [states]
    outputs = []
    earlier = []
    for iteration in range(STEPS):
        parts, fresh = step(
            blocks, chosen, lengths, w_q, w_kv, w_o, cache, cosine, sine, earlier, count
        )
        earlier.append(fresh)
        parts = lax.all_to_all(parts, "tensor", split_axis=0, concat_axis=0, tiled=True)
        state, normed = settle(parts, state, gain)
        outputs.append(state)
        if iteration + 1 < STEPS:
            blocks = [normed] + [swap_xor(normed, bits) for bits in range(1, count)]
    return jnp.stack(outputs)[:, None]


def solution(mesh):
    in_specs = (
        P(("groups", "section"), "tensor", None),
        P(("groups", "section"), "tensor", None),
        P(),
        P(None, "tensor"),
        P(None, "tensor"),
        P("tensor", None),
        P(("groups", "section"), "tensor", None, None),
        P(("groups", "section"), "tensor", None),
        P(("groups", "section"), None),
        P("groups", None),
        P("groups", None, None),
    )
    out_specs = P(None, ("groups", "section"), "tensor", None)
    return jax.shard_map(
        on_device, mesh=mesh, in_specs=in_specs, out_specs=out_specs, check_vma=False
    )
```

```python
import functools

import jax
import jax.numpy as jnp
from jax import lax
from jax.experimental import pallas as pl
from jax.experimental.pallas import tpu as pltpu
from jax.sharding import PartitionSpec as P

HD = 128
PLEN = 128
STEPS = 4
EPS = 1e-05
ROPE_BASE = 500000.0
LANES = 8
CHUNKS = 8
KEPT = (16, 24, 32, 36, 40, 44, 48, 52, 56)
VMEM_LIMIT = 16 * 1024 * 1024


def ring_order(count):
    if count == 8:
        return [0, 2, 4, 6, 7, 5, 3, 1]
    return list(range(count))


def ring_shift(value, steps):
    count = lax.axis_size("tensor")
    order = ring_order(count)
    pairs = [(order[i], order[(i + steps) % count]) for i in range(count)]
    return lax.ppermute(value, "tensor", pairs)


def swap_xor(value, mask):
    count = lax.axis_size("tensor")
    return lax.ppermute(value, "tensor", [(s, s ^ mask) for s in range(count)])


def rope_tables(positions):
    half_dim = HD // 2
    freqs = ROPE_BASE ** (-(jnp.arange(half_dim, dtype=jnp.float32) * 2.0 / HD))
    angles = positions.astype(jnp.float32)[:, None] * freqs[None, :]
    cosine = jnp.cos(angles)
    sine = jnp.sin(angles)
    return (
        jnp.concatenate([cosine, cosine], axis=1),
        jnp.concatenate([-sine, sine], axis=1),
    )


def whole():
    return pl.BlockSpec(memory_space=pltpu.VMEM)


def normed_rows(values, gain):
    square = jnp.mean(values * values, axis=-1, keepdims=True)
    return values * lax.rsqrt(square + EPS) * gain


def normalize_kernel(rows_ref, gain_ref, out_ref):
    gain = gain_ref[...].astype(jnp.float32)
    out_ref[...] = normed_rows(rows_ref[...].astype(jnp.float32), gain).astype(jnp.bfloat16)


def normalize(rows, gain):
    return pl.pallas_call(
        normalize_kernel,
        out_shape=jax.ShapeDtypeStruct(rows.shape, jnp.bfloat16),
        in_specs=[whole()] * 2,
        out_specs=whole(),
        compiler_params=pltpu.CompilerParams(vmem_limit_bytes=VMEM_LIMIT),
        name="normalize",
    )(rows, gain)


def opening_kernel(rows_ref, gain_ref, pages_ref, out_ref):
    width = rows_ref.shape[1]
    gain = gain_ref[...].astype(jnp.float32)
    out_ref[:, :width] = normed_rows(rows_ref[...].astype(jnp.float32), gain).astype(jnp.bfloat16)
    out_ref[:, width:] = pages_ref[...]


def opening(rows, gain, pages):
    shape = (rows.shape[0], rows.shape[1] + pages.shape[1])
    return pl.pallas_call(
        opening_kernel,
        out_shape=jax.ShapeDtypeStruct(shape, jnp.bfloat16),
        in_specs=[whole()] * 3,
        out_specs=whole(),
        compiler_params=pltpu.CompilerParams(vmem_limit_bytes=VMEM_LIMIT),
        name="opening",
    )(rows, gain, pages)


def fetch_kernel(*refs):
    count = len(refs) // 2
    sems = refs[-1]
    copies = [pltpu.make_async_copy(refs[i], refs[count + i], sems.at[i]) for i in range(count)]
    for copy in copies:
        copy.start()
    for copy in copies:
        copy.wait()


def fetch(*arrays):
    return pl.pallas_call(
        fetch_kernel,
        out_shape=tuple(pltpu.VMEM(a.shape, a.dtype) for a in arrays),
        in_specs=[pl.BlockSpec(memory_space=pl.ANY)] * len(arrays),
        out_specs=tuple(whole() for _ in arrays),
        scratch_shapes=[pltpu.SemaphoreType.DMA((len(arrays),))],
        compiler_params=pltpu.CompilerParams(vmem_limit_bytes=VMEM_LIMIT),
        name="fetch",
    )(*arrays)


def parcels_kernel(heads, kept, table_ref, used_ref, pool_ref, out_ref, held, load_sem, store_sem):
    width = out_ref.shape[-1]
    each, per_request = table_ref.shape
    total = used_ref[0]
    for r in range(1, each):
        total = total + used_ref[r]
    loads = []
    front, back = 0, total
    for r in range(each):
        used = used_ref[r]
        for p in range(per_request):
            spot = jnp.where(p < used, front + p, back + p - used)
            copy = pltpu.make_async_copy(
                pool_ref.at[table_ref[r, p]], held.at[spot], load_sem.at[r * per_request + p]
            )
            copy.start()
            loads.append(copy)
        front = front + used
        back = back + per_request - used
    for copy in loads:
        copy.wait()
    stores = []
    for target, head in enumerate(heads):
        copy = pltpu.make_async_copy(
            held.at[pl.ds(0, kept), :, pl.ds(head * width, width)],
            out_ref.at[target],
            store_sem.at[target],
        )
        copy.start()
        stores.append(copy)
    for copy in stores:
        copy.wait()


def make_parcels(table, used, pool, heads, width, kept):
    pages, rows, _ = pool.shape
    smem = pl.BlockSpec(memory_space=pltpu.SMEM)
    anywhere = pl.BlockSpec(memory_space=pl.ANY)
    return pl.pallas_call(
        functools.partial(parcels_kernel, heads, kept),
        out_shape=jax.ShapeDtypeStruct((len(heads), kept, rows, width), jnp.bfloat16),
        in_specs=[smem, smem, anywhere],
        out_specs=anywhere,
        scratch_shapes=[
            pltpu.VMEM(pool.shape, jnp.bfloat16),
            pltpu.SemaphoreType.DMA((pages,)),
            pltpu.SemaphoreType.DMA((len(heads),)),
        ],
        compiler_params=pltpu.CompilerParams(vmem_limit_bytes=VMEM_LIMIT),
        name="parcels",
    )(table, used, pool)


def unpack_kernel(used_ref, first_ref, packed_ref, out_ref, sems):
    count, per_request = out_ref.shape[:2]
    each = count // packed_ref.shape[0]
    sizes = []
    size = per_request
    while size:
        sizes.append(size)
        size //= 2

    def copies(r, action):
        used = used_ref[r]
        done = jnp.int32(0)
        for index, size in enumerate(sizes):
            present = (used // size) % 2 == 1

            @pl.when(present)
            def _():
                copy = pltpu.make_async_copy(
                    packed_ref.at[r // each, pl.ds(first_ref[r] + done, size)],
                    out_ref.at[r, pl.ds(done, size)],
                    sems.at[r, index],
                )
                action(copy)

            done = done + jnp.where(present, size, 0)

    for r in range(count):
        copies(r, lambda copy: copy.start())
    for r in range(count):
        copies(r, lambda copy: copy.wait())


def unpack(used, first, packed, count, per_request):
    smem = pl.BlockSpec(memory_space=pltpu.SMEM)
    anywhere = pl.BlockSpec(memory_space=pl.ANY)
    return pl.pallas_call(
        unpack_kernel,
        out_shape=jax.ShapeDtypeStruct((count, per_request) + packed.shape[2:], packed.dtype),
        in_specs=[smem, smem, anywhere],
        out_specs=anywhere,
        scratch_shapes=[pltpu.SemaphoreType.DMA((count, per_request.bit_length()))],
        compiler_params=pltpu.CompilerParams(vmem_limit_bytes=VMEM_LIMIT),
        name="unpack",
    )(used, first, packed)


def patch_kernel(rows, request_ref, offset_ref, arrived_ref, _cache_in, out_ref, sems):
    copies = []
    for piece in range(arrived_ref.shape[0] // rows):
        offset = pl.multiple_of(offset_ref[piece], rows)
        copy = pltpu.make_async_copy(
            arrived_ref.at[pl.ds(piece * rows, rows), :],
            out_ref.at[request_ref[piece], pl.ds(offset, rows), :],
            sems.at[piece],
        )
        copy.start()
        copies.append(copy)
    for copy in copies:
        copy.wait()


def patch(requests, offsets, arrived, cache, rows):
    smem = pl.BlockSpec(memory_space=pltpu.SMEM)
    return pl.pallas_call(
        functools.partial(patch_kernel, rows),
        out_shape=pltpu.VMEM(cache.shape, cache.dtype),
        in_specs=[smem, smem, pl.BlockSpec(memory_space=pl.ANY), whole()],
        out_specs=whole(),
        scratch_shapes=[pltpu.SemaphoreType.DMA((arrived.shape[0] // rows,))],
        input_output_aliases={3: 0},
        compiler_params=pltpu.CompilerParams(vmem_limit_bytes=VMEM_LIMIT),
        name="patch",
    )(requests, offsets, arrived, cache)


def turn(values, cosine, sine):
    return values * cosine + pltpu.roll(values, HD // 2, 1) * sine


def step_kernel(blocks, iteration, *refs):
    x_refs = refs[:blocks]
    order_ref, lens_ref, wq, wkv, wo, cache, cos_ref, sin_ref = refs[blocks : blocks + 8]
    new_refs = refs[blocks + 8 : blocks + 8 + iteration]
    out_ref, fresh_ref, x_rows, q_s, score_s, mix_s, new_s = refs[blocks + 8 + iteration :]
    width, q_cols = wq.shape
    count, span = cache.shape[:2]
    each = count // out_ref.shape[0]
    heads = q_cols // HD
    depth = width // CHUNKS

    for k in range(blocks):
        x_rows[k * each : (k + 1) * each, :] = x_refs[k][:, :width].astype(jnp.float32)
    order = order_ref[...]

    query = jnp.zeros((count, q_cols), jnp.float32)
    keyvalue = jnp.zeros((count, 2 * HD), jnp.float32)
    for c in range(CHUNKS):
        part = slice(c * depth, (c + 1) * depth)
        x = jnp.dot(
            order, x_rows[:, part].astype(jnp.bfloat16), preferred_element_type=jnp.float32
        ).astype(jnp.bfloat16)
        query += jnp.dot(x, wq[part, :], preferred_element_type=jnp.float32)
        keyvalue += jnp.dot(x, wkv[part, :], preferred_element_type=jnp.float32)

    cosine = cos_ref[iteration]
    sine = sin_ref[iteration]
    key = turn(keyvalue[:, :HD], cosine, sine).astype(jnp.bfloat16)
    value = keyvalue[:, HD:].astype(jnp.bfloat16)
    fresh_ref[:, :HD] = key
    fresh_ref[:, HD:] = value
    news = [(ref[:, :HD], ref[:, HD:]) for ref in new_refs] + [(key, value)]
    for j in range(LANES):
        lane = pl.ds(j, count, LANES)
        if j < heads:
            turned = turn(query[:, j * HD : (j + 1) * HD], cosine, sine).astype(jnp.bfloat16)
            q_s[lane, :] = turned.astype(jnp.float32)
        else:
            q_s[lane, :] = jnp.zeros((count, HD), jnp.float32)
        for t, pair in enumerate(news):
            for half in range(2):
                new_s[t, half, lane, :] = pair[half].astype(jnp.float32)

    scale = HD**-0.5
    column = lax.broadcasted_iota(jnp.int32, (LANES, span), 1)
    for r in range(count):
        rows = slice(r * LANES, (r + 1) * LANES)
        found = lax.dot_general(
            q_s[rows, :].astype(jnp.bfloat16),
            cache[r, :, :HD],
            (((1,), (1,)), ((), ())),
            preferred_element_type=jnp.float32,
        )
        score_s[rows, :] = jnp.where(column < lens_ref[r], found * scale, -1e30)

    scores = score_s[...]
    queries = q_s[...]
    fresh_scores = [
        jnp.sum(queries * new_s[t, 0], axis=-1, keepdims=True) * scale for t in range(iteration + 1)
    ]
    top = jnp.max(scores, axis=-1, keepdims=True)
    for s in fresh_scores:
        top = jnp.maximum(top, s)
    weights = jnp.exp(scores - top)
    fresh_weights = [jnp.exp(s - top) for s in fresh_scores]
    total = jnp.sum(weights, axis=-1, keepdims=True)
    for w in fresh_weights:
        total = total + w
    score_s[...] = weights / total
    row = lax.broadcasted_iota(jnp.int32, (span, HD), 0)
    for r in range(count):
        rows = slice(r * LANES, (r + 1) * LANES)
        mix_s[rows, :] = jnp.dot(
            score_s[rows, :].astype(jnp.bfloat16),
            jnp.where(row < lens_ref[r], cache[r, :, HD:], jnp.zeros((), jnp.bfloat16)),
            preferred_element_type=jnp.float32,
        )
    mixed = mix_s[...]
    for t in range(iteration + 1):
        weight = (fresh_weights[t] / total).astype(jnp.bfloat16).astype(jnp.float32)
        mixed = mixed + weight * new_s[t, 1]
    mix_s[...] = mixed
    columns = jnp.concatenate(
        [mix_s[pl.ds(j, count, LANES), :].astype(jnp.bfloat16) for j in range(heads)], axis=1
    )
    for c in range(CHUNKS):
        part = slice(c * depth, (c + 1) * depth)
        product = jnp.dot(columns, wo[:, part], preferred_element_type=jnp.float32)
        for d in range(count // each):
            out_ref[d, :, part] = product[d * each : (d + 1) * each, :].astype(jnp.bfloat16)


def step(x_blocks, order, lengths, wq, wkv, wo, cache, cosine, sine, earlier, owners):
    width, q_cols = wq.shape
    count, span = cache.shape[:2]
    each = count // owners
    iteration = len(earlier)
    blocks = len(x_blocks)
    smem = pl.BlockSpec(memory_space=pltpu.SMEM)
    return pl.pallas_call(
        functools.partial(step_kernel, blocks, iteration),
        out_shape=(
            jax.ShapeDtypeStruct((owners, each, width), jnp.bfloat16),
            jax.ShapeDtypeStruct((count, 2 * HD), jnp.bfloat16),
        ),
        in_specs=[whole()] * (blocks + 1) + [smem] + [whole()] * (6 + iteration),
        out_specs=(whole(), whole()),
        scratch_shapes=[
            pltpu.VMEM((count, width), jnp.float32),
            pltpu.VMEM((count * LANES, HD), jnp.float32),
            pltpu.VMEM((count * LANES, span), jnp.float32),
            pltpu.VMEM((count * LANES, HD), jnp.float32),
            pltpu.VMEM((iteration + 1, 2, count * LANES, HD), jnp.float32),
        ],
        compiler_params=pltpu.CompilerParams(vmem_limit_bytes=VMEM_LIMIT),
        cost_estimate=pl.CostEstimate(
            flops=2 * count * width * (2 * q_cols + 2 * HD),
            bytes_accessed=2 * (2 * wq.size + wkv.size + cache.size),
            transcendentals=count * LANES * span,
        ),
        name="decode_step",
    )(*x_blocks, order, lengths, wq, wkv, wo, cache, cosine, sine, *earlier)


def settle_kernel(parts_ref, state_ref, gain_ref, next_ref, normed_ref):
    total = parts_ref[0].astype(jnp.float32)
    for d in range(1, parts_ref.shape[0]):
        total = total + parts_ref[d].astype(jnp.float32)
    state = (state_ref[...].astype(jnp.float32) + total).astype(jnp.bfloat16)
    next_ref[...] = state
    gain = gain_ref[...].astype(jnp.float32)
    normed_ref[...] = normed_rows(state.astype(jnp.float32), gain).astype(jnp.bfloat16)


def settle(parts, state, gain):
    shape = jax.ShapeDtypeStruct(state.shape, jnp.bfloat16)
    return pl.pallas_call(
        settle_kernel,
        out_shape=(shape, shape),
        in_specs=[whole()] * 3,
        out_specs=(whole(), whole()),
        compiler_params=pltpu.CompilerParams(vmem_limit_bytes=VMEM_LIMIT),
        name="settle",
    )(parts, state, gain)


def on_device(
    prompt_states,
    decode_states,
    norm_gain,
    w_query,
    w_keyvalue,
    w_output,
    cache_pages,
    page_table,
    cache_len,
    dest_rank,
    dest_page,
):
    rank = lax.axis_index("tensor")
    section = lax.axis_index("section")
    count = lax.axis_size("tensor")
    pool = cache_pages[0]
    page_size, kv_width = pool.shape[1:]
    own_table = page_table[0]
    lengths = cache_len[0]
    each, width = decode_states.shape[1:]
    tokens = prompt_states.shape[1]
    q_cols = w_query.shape[1]
    kv_heads = kv_width // (2 * HD)
    shared = count // kv_heads if count > kv_heads else 1
    gain = norm_gain[None, :]

    if w_keyvalue.shape[1] < 2 * HD:
        other = swap_xor(w_keyvalue, 1)
        is_key = rank % 2 == 0
        w_pair = jnp.concatenate(
            [jnp.where(is_key, w_keyvalue, other), jnp.where(is_key, other, w_keyvalue)], axis=1
        )
    else:
        w_pair = w_keyvalue

    numbers = jnp.arange(count * each, dtype=jnp.int32)
    pages = jnp.broadcast_to(own_table[:, :1], (each, HD)).astype(jnp.bfloat16)
    opened = opening(decode_states[0], gain, pages)
    blocks = [opened] + [swap_xor(opened, bits) for bits in range(1, count)]
    first_pages = jnp.concatenate([block[:, width:] for block in blocks])[:, 0].astype(jnp.int32)

    heads = tuple(target // shared for target in range(count))
    per_request = own_table.shape[1]
    used = (lengths + page_size - 1) // page_size
    by_owner = used.reshape(count, each)
    most = jnp.max(jnp.sum(by_owner, axis=1, keepdims=True), keepdims=True)
    for axis in ("section", "groups"):
        for bit in range(lax.axis_size(axis).bit_length() - 1):
            pairs = [(s, s ^ (1 << bit)) for s in range(lax.axis_size(axis))]
            most = jnp.maximum(most, lax.ppermute(most, axis, pairs))
    first = (jnp.cumsum(by_owner, axis=1) - by_owner).reshape(-1)
    own_used = lax.dynamic_slice_in_dim(used, rank * each, each)
    limits = [limit for limit in KEPT if limit < pool.shape[0]] + [pool.shape[0]]

    def exchange(kept):
        def branch(table, own, used, first, pool):
            parcels = make_parcels(table, own, pool, heads, 2 * HD, kept)
            packed = lax.all_to_all(parcels, "tensor", split_axis=0, concat_axis=0, tiled=True)
            return unpack(used, first, packed, count * each, per_request)

        return branch

    choice = jnp.sum((most[0, 0] > jnp.array(limits[:-1], jnp.int32)).astype(jnp.int32))
    cache = lax.switch(
        choice, [exchange(limit) for limit in limits], own_table, own_used, used, first, pool
    ).reshape(count * each, per_request * page_size, 2 * HD)

    half = tokens // 2
    ready = normalize(prompt_states[0], gain)
    pieces = [ready[:half], ready[half:]]
    order = ring_order(count)
    place = jnp.array([order.index(r) for r in range(count)], jnp.int32)[rank]
    ring = jnp.array(order, jnp.int32)
    arrivals = [(0, 0, pieces[0]), (0, 1, pieces[1])]
    going = [[piece, piece] for piece in pieces]
    for hop in range(1, count // 2 + 1):
        for piece in range(2):
            for way in range(2):
                if hop == count // 2 and piece != way:
                    continue
                sign = 1 if way == 0 else -1
                going[piece][way] = ring_shift(going[piece][way], sign)
                arrivals.append((-sign * hop, piece, going[piece][way]))
    products = [
        jnp.dot(rows, w_pair, preferred_element_type=jnp.float32) for _, _, rows in arrivals
    ]
    behind = jnp.array([steps for steps, _, _ in arrivals], jnp.int32)
    halves = jnp.array([piece for _, piece, _ in arrivals], jnp.int32)
    starts = ring[(place + behind) % count] * tokens + halves * half
    row_index = (starts[:, None] + jnp.arange(half, dtype=jnp.int32)[None, :]).reshape(-1)
    cosine, sine = rope_tables(row_index % PLEN)
    values = jnp.concatenate(products, axis=0)
    keys = values[:, :HD]
    keys = keys * cosine + jnp.roll(keys, HD // 2, axis=1) * sine
    prompt_kv = jnp.concatenate([keys, values[:, HD:]], axis=1).astype(jnp.bfloat16)
    sections = lax.axis_size("section")
    arrived = lax.ppermute(prompt_kv, "section", [(s, (s + 1) % sections) for s in range(sections)])

    anchor = (section + 1) % sections
    targets = lax.dynamic_index_in_dim(dest_rank, anchor, 0, keepdims=False)
    landing = lax.dynamic_index_in_dim(dest_page, anchor, 0, keepdims=False)[:, 0]
    rows_of = (rank ^ (numbers // each)) * each + numbers % each
    here = (rows_of[None, :] // each == targets[:, None]) & (first_pages[None, :] == landing[:, None])
    receivers = jnp.sum(jnp.where(here, rows_of[None, :], 0), axis=1)
    w_q, w_kv, w_o, cache = fetch(w_query, w_pair, w_output, cache)
    cache = patch(receivers[starts // PLEN], starts % PLEN, arrived, cache, half)

    times = lengths[None, :] + jnp.arange(STEPS, dtype=jnp.int32)[:, None]
    cosine, sine = rope_tables(times.reshape(-1))
    cosine = cosine.reshape(STEPS, count * each, HD)
    sine = sine.reshape(STEPS, count * each, HD)
    chosen = (numbers[:, None] == rows_of[None, :]).astype(jnp.bfloat16)
    state = decode_states[0]
    outputs = []
    earlier = []
    for iteration in range(STEPS):
        parts, fresh = step(
            blocks, chosen, lengths, w_q, w_kv, w_o, cache, cosine, sine, earlier, count
        )
        earlier.append(fresh)
        parts = lax.all_to_all(parts, "tensor", split_axis=0, concat_axis=0, tiled=True)
        state, normed = settle(parts, state, gain)
        outputs.append(state)
        if iteration + 1 < STEPS:
            blocks = [normed] + [swap_xor(normed, bits) for bits in range(1, count)]
    return jnp.stack(outputs)[:, None]


def solution(mesh):
    in_specs = (
        P(("groups", "section"), "tensor", None),
        P(("groups", "section"), "tensor", None),
        P(),
        P(None, "tensor"),
        P(None, "tensor"),
        P("tensor", None),
        P(("groups", "section"), "tensor", None, None),
        P(("groups", "section"), "tensor", None),
        P(("groups", "section"), None),
        P("groups", None),
        P("groups", None, None),
    )
    out_specs = P(None, ("groups", "section"), "tensor", None)
    return jax.shard_map(
        on_device, mesh=mesh, in_specs=in_specs, out_specs=out_specs, check_vma=False
    )
```

```python
import functools

import jax
import jax.numpy as jnp
from jax import lax
from jax.experimental import pallas as pl
from jax.experimental.pallas import tpu as pltpu
from jax.sharding import PartitionSpec as P

HD = 128
PLEN = 128
STEPS = 4
EPS = 1e-05
ROPE_BASE = 500000.0
LANES = 8
CHUNKS = 8
VMEM_LIMIT = 16 * 1024 * 1024


def ring_shift(value, steps):
    count = lax.axis_size("tensor")
    return lax.ppermute(value, "tensor", [(s, (s + steps) % count) for s in range(count)])


def swap_xor(value, mask):
    count = lax.axis_size("tensor")
    return lax.ppermute(value, "tensor", [(s, s ^ mask) for s in range(count)])


def along_ring(pieces, opened, gate):
    count = lax.axis_size("tensor")
    rank = lax.axis_index("tensor")
    arrivals = [(rank, piece, rows) for piece, rows in enumerate(pieces)]
    going = [[rows, rows] for rows in pieces]
    middle = None
    for hop in range(1, count // 2 + 1):
        for piece in range(2):
            for way in range(2):
                if hop == count // 2 and piece != way:
                    continue
                sign = 1 if way == 0 else -1
                going[piece][way] = ring_shift(going[piece][way], sign)
                arrivals.append(((rank - sign * hop) % count, piece, going[piece][way]))
        if hop == 1:
            going, opened, gate = lax.optimization_barrier((going, opened, gate))
        if hop == count // 4:
            middle = going[1][1]
    return arrivals, opened, gate, middle


def along_grid(pieces, opened, gate):
    rank = lax.axis_index("tensor")
    z, y = rank // 2, rank % 2

    def shift(rows, steps, starts):
        pairs = [(2 * s + c, 2 * (s + steps) + c) for s in starts for c in range(2)]
        return lax.ppermute(rows, "tensor", pairs)

    def cross(rows):
        return lax.ppermute(rows, "tensor", [(r, r ^ 1) for r in range(8)])

    def pick(*rows):
        return jnp.where(z == 0, rows[0], jnp.where(z == 1, rows[1], jnp.where(z == 2, rows[2], rows[3])))

    origin = [z, z ^ 1, jnp.where(z < 2, 2, 1), jnp.where(z < 2, 3, 0)]
    state = []
    for rows in pieces:
        state.append((rows, shift(rows, 1, (0, 1, 2)), shift(rows, -1, (1, 2, 3)), cross(rows)))
    state, opened, gate = lax.optimization_barrier((state, opened, gate))
    arrivals = []
    middle = None
    for piece, (rows, up, down, crossed) in enumerate(state):
        second = pick(down, up, down, up)
        up2, down2, crossed2 = lax.optimization_barrier(
            (shift(up, 1, (1, 2)), shift(down, -1, (1, 2)), cross(second))
        )
        middle = up2
        third = pick(down2, down, up, up2)
        up3, down3, crossed3 = lax.optimization_barrier(
            (shift(up2, 1, (2,)), shift(down2, -1, (1,)), cross(third))
        )
        fourth = pick(down3, down2, up2, up3)
        crossed4 = cross(fourth)
        straight = (rows, second, third, fourth)
        for source, block in zip(origin, straight):
            arrivals.append((2 * source + y, piece, block))
        for source, block in zip(origin, (crossed, crossed2, crossed3, crossed4)):
            arrivals.append((2 * source + 1 - y, piece, block))
    return arrivals, opened, gate, middle


def rope_tables(positions):
    half_dim = HD // 2
    freqs = ROPE_BASE ** (-(jnp.arange(half_dim, dtype=jnp.float32) * 2.0 / HD))
    angles = positions.astype(jnp.float32)[:, None] * freqs[None, :]
    cosine = jnp.cos(angles)
    sine = jnp.sin(angles)
    return (
        jnp.concatenate([cosine, cosine], axis=1),
        jnp.concatenate([-sine, sine], axis=1),
    )


def whole():
    return pl.BlockSpec(memory_space=pltpu.VMEM)


def normed_rows(values, gain):
    square = jnp.mean(values * values, axis=-1, keepdims=True)
    return values * lax.rsqrt(square + EPS) * gain


def normalize_kernel(rows_ref, gain_ref, out_ref):
    gain = gain_ref[...].astype(jnp.float32)
    out_ref[...] = normed_rows(rows_ref[...].astype(jnp.float32), gain).astype(jnp.bfloat16)


def normalize(rows, gain):
    return pl.pallas_call(
        normalize_kernel,
        out_shape=jax.ShapeDtypeStruct(rows.shape, jnp.bfloat16),
        in_specs=[whole()] * 2,
        out_specs=whole(),
        compiler_params=pltpu.CompilerParams(vmem_limit_bytes=VMEM_LIMIT),
        name="normalize",
    )(rows, gain)


def opening_kernel(rows_ref, gain_ref, pages_ref, out_ref):
    width = rows_ref.shape[1]
    gain = gain_ref[...].astype(jnp.float32)
    out_ref[:, :width] = normed_rows(rows_ref[...].astype(jnp.float32), gain).astype(jnp.bfloat16)
    out_ref[:, width:] = pages_ref[...]


def opening(rows, gain, pages):
    shape = (rows.shape[0], rows.shape[1] + pages.shape[1])
    return pl.pallas_call(
        opening_kernel,
        out_shape=jax.ShapeDtypeStruct(shape, jnp.bfloat16),
        in_specs=[whole()] * 3,
        out_specs=whole(),
        compiler_params=pltpu.CompilerParams(vmem_limit_bytes=VMEM_LIMIT),
        name="opening",
    )(rows, gain, pages)


def parcels_kernel(heads, table_ref, pool_ref, out_ref, held, load_sem, store_sem):
    width = out_ref.shape[-1]
    each, per_request = table_ref.shape
    loads = []
    for r in range(each):
        for p in range(per_request):
            index = r * per_request + p
            copy = pltpu.make_async_copy(
                pool_ref.at[table_ref[r, p]], held.at[index], load_sem.at[index]
            )
            copy.start()
            loads.append(copy)
    for copy in loads:
        copy.wait()
    stores = []
    for target, head in enumerate(heads):
        copy = pltpu.make_async_copy(
            held.at[:, :, pl.ds(head * width, width)], out_ref.at[target], store_sem.at[target]
        )
        copy.start()
        stores.append(copy)
    for copy in stores:
        copy.wait()


def make_parcels(table, pool, heads, width):
    pages, rows, _ = pool.shape
    hbm = pl.BlockSpec(memory_space=pltpu.HBM)
    return pl.pallas_call(
        functools.partial(parcels_kernel, heads),
        out_shape=pltpu.HBM((len(heads), pages, rows, width), jnp.bfloat16),
        in_specs=[pl.BlockSpec(memory_space=pltpu.SMEM), hbm],
        out_specs=hbm,
        scratch_shapes=[
            pltpu.VMEM(pool.shape, jnp.bfloat16),
            pltpu.SemaphoreType.DMA((pages,)),
            pltpu.SemaphoreType.DMA((len(heads),)),
        ],
        compiler_params=pltpu.CompilerParams(vmem_limit_bytes=VMEM_LIMIT),
        name="parcels",
    )(table, pool)


def turn(values, cosine, sine):
    return values * cosine + pltpu.roll(values, HD // 2, 1) * sine


def step_kernel(blocks, iteration, *refs):
    x_refs = refs[:blocks]
    order_ref, lens_ref, cos_ref, sin_ref = refs[blocks : blocks + 4]
    new_refs = refs[blocks + 4 : blocks + 4 + iteration]
    refs = refs[blocks + 4 + iteration :]
    if iteration == 0:
        request_ref, offset_ref, arrived_ref, wq_in, wkv_in, wo_in, cache_in = refs[:7]
        out_ref, fresh_ref, wq, wkv, wo, cache = refs[7:13]
        x_rows, q_s, score_s, mix_s, new_s, sems = refs[13:]
    else:
        wq, wkv, wo, cache = refs[:4]
        out_ref, fresh_ref, x_rows, q_s, score_s, mix_s, new_s = refs[4:]
    width, q_cols = wq.shape
    count, span = cache.shape[:2]
    each = count // out_ref.shape[0]
    heads = q_cols // HD
    depth = width // CHUNKS

    waits = {}
    if iteration == 0:
        for c in range(CHUNKS):
            part = pl.ds(c * depth, depth)
            waits[c] = [
                pltpu.make_async_copy(wq_in.at[part, :], wq.at[part, :], sems.at[0, c]),
                pltpu.make_async_copy(wkv_in.at[part, :], wkv.at[part, :], sems.at[1, c]),
            ]
            waits["out", c] = [pltpu.make_async_copy(wo_in.at[:, part], wo.at[:, part], sems.at[2, c])]
        waits["cache"] = [pltpu.make_async_copy(cache_in, cache, sems.at[3, 0])]
        for name in [0, 1, 2, 3, "cache", 4, 5, 6, 7] + [("out", c) for c in range(CHUNKS)]:
            for copy in waits[name]:
                copy.start()

    def wait(name):
        for copy in waits.get(name, ()):
            copy.wait()

    def patch(action):
        pieces = offset_ref.shape[0]
        rows = arrived_ref.shape[0] // pieces
        for piece in range(pieces):
            offset = pl.multiple_of(offset_ref[piece], rows)
            copy = pltpu.make_async_copy(
                arrived_ref.at[pl.ds(piece * rows, rows), :],
                cache.at[request_ref[piece], pl.ds(offset, rows), :],
                sems.at[4 + piece // CHUNKS, piece % CHUNKS],
            )
            action(copy)

    for k in range(blocks):
        x_rows[k * each : (k + 1) * each, :] = x_refs[k][:, :width].astype(jnp.float32)
    order = order_ref[...]

    query = jnp.zeros((count, q_cols), jnp.float32)
    keyvalue = jnp.zeros((count, 2 * HD), jnp.float32)
    for c in range(CHUNKS):
        part = slice(c * depth, (c + 1) * depth)
        x = jnp.dot(
            order, x_rows[:, part].astype(jnp.bfloat16), preferred_element_type=jnp.float32
        ).astype(jnp.bfloat16)
        wait(c)
        query += jnp.dot(x, wq[part, :], preferred_element_type=jnp.float32)
        keyvalue += jnp.dot(x, wkv[part, :], preferred_element_type=jnp.float32)
        if iteration == 0 and c == CHUNKS - 2:
            wait("cache")
            patch(lambda copy: copy.start())

    cosine = cos_ref[iteration]
    sine = sin_ref[iteration]
    key = turn(keyvalue[:, :HD], cosine, sine).astype(jnp.bfloat16)
    value = keyvalue[:, HD:].astype(jnp.bfloat16)
    fresh_ref[:, :HD] = key
    fresh_ref[:, HD:] = value
    news = [(ref[:, :HD], ref[:, HD:]) for ref in new_refs] + [(key, value)]
    for j in range(LANES):
        lane = pl.ds(j, count, LANES)
        if j < heads:
            turned = turn(query[:, j * HD : (j + 1) * HD], cosine, sine).astype(jnp.bfloat16)
            q_s[lane, :] = turned.astype(jnp.float32)
        else:
            q_s[lane, :] = jnp.zeros((count, HD), jnp.float32)
        for t, pair in enumerate(news):
            for half in range(2):
                new_s[t, half, lane, :] = pair[half].astype(jnp.float32)

    if iteration == 0:
        patch(lambda copy: copy.wait())
    scale = HD**-0.5
    column = lax.broadcasted_iota(jnp.int32, (LANES, span), 1)
    for r in range(count):
        rows = slice(r * LANES, (r + 1) * LANES)
        found = lax.dot_general(
            q_s[rows, :].astype(jnp.bfloat16),
            cache[r, :, :HD],
            (((1,), (1,)), ((), ())),
            preferred_element_type=jnp.float32,
        )
        score_s[rows, :] = jnp.where(column < lens_ref[r], found * scale, -1e30)

    scores = score_s[...]
    queries = q_s[...]
    fresh_scores = [
        jnp.sum(queries * new_s[t, 0], axis=-1, keepdims=True) * scale for t in range(iteration + 1)
    ]
    top = jnp.max(scores, axis=-1, keepdims=True)
    for s in fresh_scores:
        top = jnp.maximum(top, s)
    weights = jnp.exp(scores - top)
    fresh_weights = [jnp.exp(s - top) for s in fresh_scores]
    total = jnp.sum(weights, axis=-1, keepdims=True)
    for w in fresh_weights:
        total = total + w
    score_s[...] = weights / total
    row = lax.broadcasted_iota(jnp.int32, (span, HD), 0)
    for r in range(count):
        rows = slice(r * LANES, (r + 1) * LANES)
        mix_s[rows, :] = jnp.dot(
            score_s[rows, :].astype(jnp.bfloat16),
            jnp.where(row < lens_ref[r], cache[r, :, HD:], jnp.zeros((), jnp.bfloat16)),
            preferred_element_type=jnp.float32,
        )
    mixed = mix_s[...]
    for t in range(iteration + 1):
        weight = (fresh_weights[t] / total).astype(jnp.bfloat16).astype(jnp.float32)
        mixed = mixed + weight * new_s[t, 1]
    mix_s[...] = mixed
    columns = jnp.concatenate(
        [mix_s[pl.ds(j, count, LANES), :].astype(jnp.bfloat16) for j in range(heads)], axis=1
    )
    for c in range(CHUNKS):
        part = slice(c * depth, (c + 1) * depth)
        wait(("out", c))
        product = jnp.dot(columns, wo[:, part], preferred_element_type=jnp.float32)
        for d in range(count // each):
            out_ref[d, :, part] = product[d * each : (d + 1) * each, :].astype(jnp.bfloat16)


def step(x_blocks, order, lengths, cosine, sine, earlier, held, owners, prompts=()):
    width, q_cols = held[0].shape
    count, span = held[3].shape[:2]
    each = count // owners
    iteration = len(earlier)
    blocks = len(x_blocks)
    smem = pl.BlockSpec(memory_space=pltpu.SMEM)
    hbm = pl.BlockSpec(memory_space=pltpu.HBM)
    out_shape = [
        jax.ShapeDtypeStruct((owners, each, width), jnp.bfloat16),
        jax.ShapeDtypeStruct((count, 2 * HD), jnp.bfloat16),
    ]
    in_specs = [whole()] * (blocks + 1) + [smem] + [whole()] * (2 + iteration)
    scratch = [
        pltpu.VMEM((count, width), jnp.float32),
        pltpu.VMEM((count * LANES, HD), jnp.float32),
        pltpu.VMEM((count * LANES, span), jnp.float32),
        pltpu.VMEM((count * LANES, HD), jnp.float32),
        pltpu.VMEM((iteration + 1, 2, count * LANES, HD), jnp.float32),
    ]
    if iteration == 0:
        in_specs += [smem, smem, whole()] + [hbm] * 4
        out_shape += [pltpu.VMEM(a.shape, a.dtype) for a in held]
        banks = -(-prompts[1].shape[0] // CHUNKS)
        scratch.append(pltpu.SemaphoreType.DMA((4 + banks, CHUNKS)))
    else:
        in_specs += [whole()] * 4
    return pl.pallas_call(
        functools.partial(step_kernel, blocks, iteration),
        out_shape=tuple(out_shape),
        in_specs=in_specs,
        out_specs=tuple(whole() for _ in out_shape),
        scratch_shapes=scratch,
        compiler_params=pltpu.CompilerParams(vmem_limit_bytes=VMEM_LIMIT),
        cost_estimate=pl.CostEstimate(
            flops=2 * count * width * (2 * q_cols + 2 * HD),
            bytes_accessed=2 * sum(a.size for a in held),
            transcendentals=count * LANES * span,
        ),
        name="decode_step",
    )(*x_blocks, order, lengths, cosine, sine, *earlier, *prompts, *held)


def settle_kernel(parts_ref, state_ref, gain_ref, next_ref, normed_ref):
    total = parts_ref[0].astype(jnp.float32)
    for d in range(1, parts_ref.shape[0]):
        total = total + parts_ref[d].astype(jnp.float32)
    state = (state_ref[...].astype(jnp.float32) + total).astype(jnp.bfloat16)
    next_ref[...] = state
    gain = gain_ref[...].astype(jnp.float32)
    normed_ref[...] = normed_rows(state.astype(jnp.float32), gain).astype(jnp.bfloat16)


def settle(parts, state, gain):
    shape = jax.ShapeDtypeStruct(state.shape, jnp.bfloat16)
    return pl.pallas_call(
        settle_kernel,
        out_shape=(shape, shape),
        in_specs=[whole()] * 3,
        out_specs=(whole(), whole()),
        compiler_params=pltpu.CompilerParams(vmem_limit_bytes=VMEM_LIMIT),
        name="settle",
    )(parts, state, gain)


def on_device(
    prompt_states,
    decode_states,
    norm_gain,
    w_query,
    w_keyvalue,
    w_output,
    cache_pages,
    page_table,
    cache_len,
    dest_rank,
    dest_page,
):
    rank = lax.axis_index("tensor")
    section = lax.axis_index("section")
    count = lax.axis_size("tensor")
    pool = cache_pages[0]
    page_size, kv_width = pool.shape[1:]
    own_table = page_table[0]
    lengths = cache_len[0]
    each, width = decode_states.shape[1:]
    tokens = prompt_states.shape[1]
    q_cols = w_query.shape[1]
    kv_heads = kv_width // (2 * HD)
    shared = count // kv_heads if count > kv_heads else 1
    gain = norm_gain[None, :]

    if w_keyvalue.shape[1] < 2 * HD:
        other = swap_xor(w_keyvalue, 1)
        is_key = rank % 2 == 0
        w_pair = jnp.concatenate(
            [jnp.where(is_key, w_keyvalue, other), jnp.where(is_key, other, w_keyvalue)], axis=1
        )
    else:
        w_pair = w_keyvalue

    half = tokens // 2
    ready = normalize(prompt_states[0], gain)
    pieces = [ready[:half], ready[half:]]
    pages = jnp.broadcast_to(own_table[:, :1], (each, HD)).astype(jnp.bfloat16)
    opened = opening(decode_states[0], gain, pages)
    heads = tuple(target // shared for target in range(count))
    parcels = make_parcels(own_table, pool, heads, 2 * HD)
    spread = along_grid if count == 8 else along_ring
    arrivals, opened, parcels, middle = spread(pieces, opened, parcels)
    blocks = [opened] + [swap_xor(opened, bits) for bits in range(1, count)]
    numbers = jnp.arange(count * each, dtype=jnp.int32)

    span = own_table.shape[1] * page_size
    parcels, blocks, _ = lax.optimization_barrier((parcels, blocks, middle))
    first_pages = jnp.concatenate([block[:, width:] for block in blocks])[:, 0].astype(jnp.int32)
    cache = lax.all_to_all(
        parcels.reshape(count, each * span, 2 * HD), "tensor", split_axis=0, concat_axis=0, tiled=True
    ).reshape(count * each, span, 2 * HD)

    products = [
        jnp.dot(rows, w_pair, preferred_element_type=jnp.float32) for _, _, rows in arrivals
    ]
    starts = jnp.stack([source * tokens + piece * half for source, piece, _ in arrivals])
    row_index = (starts[:, None] + jnp.arange(half, dtype=jnp.int32)[None, :]).reshape(-1)
    cosine, sine = rope_tables(row_index % PLEN)
    values = jnp.concatenate(products, axis=0)
    keys = values[:, :HD]
    keys = keys * cosine + jnp.roll(keys, HD // 2, axis=1) * sine
    prompt_kv = jnp.concatenate([keys, values[:, HD:]], axis=1).astype(jnp.bfloat16)
    sections = lax.axis_size("section")
    arrived = lax.ppermute(prompt_kv, "section", [(s, (s + 1) % sections) for s in range(sections)])

    anchor = (section + 1) % sections
    targets = lax.dynamic_index_in_dim(dest_rank, anchor, 0, keepdims=False)
    landing = lax.dynamic_index_in_dim(dest_page, anchor, 0, keepdims=False)[:, 0]
    rows_of = (rank ^ (numbers // each)) * each + numbers % each
    here = (rows_of[None, :] // each == targets[:, None]) & (first_pages[None, :] == landing[:, None])
    receivers = jnp.sum(jnp.where(here, rows_of[None, :], 0), axis=1)
    prompts = (receivers[starts // PLEN], starts % PLEN, arrived)
    held = (w_query, w_pair, w_output, cache)

    times = lengths[None, :] + jnp.arange(STEPS, dtype=jnp.int32)[:, None]
    cosine, sine = rope_tables(times.reshape(-1))
    cosine = cosine.reshape(STEPS, count * each, HD)
    sine = sine.reshape(STEPS, count * each, HD)
    chosen = (numbers[:, None] == rows_of[None, :]).astype(jnp.bfloat16)
    state = decode_states[0]
    outputs = []
    earlier = []
    for iteration in range(STEPS):
        parts, fresh, *fetched = step(
            blocks, chosen, lengths, cosine, sine, earlier, held, count, prompts
        )
        if iteration == 0:
            held, prompts = fetched, ()
        earlier.append(fresh)
        parts = lax.all_to_all(parts, "tensor", split_axis=0, concat_axis=0, tiled=True)
        state, normed = settle(parts, state, gain)
        outputs.append(state)
        if iteration + 1 < STEPS:
            blocks = [normed] + [swap_xor(normed, bits) for bits in range(1, count)]
    return jnp.stack(outputs)[:, None]


def solution(mesh):
    in_specs = (
        P(("groups", "section"), "tensor", None),
        P(("groups", "section"), "tensor", None),
        P(),
        P(None, "tensor"),
        P(None, "tensor"),
        P("tensor", None),
        P(("groups", "section"), "tensor", None, None),
        P(("groups", "section"), "tensor", None),
        P(("groups", "section"), None),
        P("groups", None),
        P("groups", None, None),
    )
    out_specs = P(None, ("groups", "section"), "tensor", None)
    return jax.shard_map(
        on_device, mesh=mesh, in_specs=in_specs, out_specs=out_specs, check_vma=False
    )
```

```python
import functools

import jax
import jax.numpy as jnp
import numpy as np
from jax import lax
from jax.experimental import pallas as pl
from jax.experimental.pallas import tpu as pltpu
from jax.sharding import PartitionSpec as P

HD = 128
PLEN = 128
STEPS = 4
EPS = 1e-05
ROPE_BASE = 500000.0
LANES = 8
CHUNKS = 8
PAGE = 16
SURE = 24
MORE = (0, 4, 8, 12, 16, 20, 24, 28, 32)
VMEM_LIMIT = 10 * 1024 * 1024


def ring_shift(value, steps):
    count = lax.axis_size("tensor")
    return lax.ppermute(value, "tensor", [(s, (s + steps) % count) for s in range(count)])


def swap_xor(value, mask):
    count = lax.axis_size("tensor")
    return lax.ppermute(value, "tensor", [(s, s ^ mask) for s in range(count)])


def ring_arrivals(count):
    table, halves = [np.arange(count)] * 2, [0, 1]
    for hop in range(1, count // 2 + 1):
        for piece in range(2):
            for way in range(2):
                if hop < count // 2 or piece == way:
                    table.append((np.arange(count) - (1 - 2 * way) * hop) % count)
                    halves.append(piece)
    return np.stack(table, axis=1), halves


def along_ring(pieces, ready):
    count = lax.axis_size("tensor")
    blocks = list(pieces)
    going = [[rows, rows] for rows in pieces]
    for hop in range(1, count // 2 + 1):
        for piece in range(2):
            for way in range(2):
                if hop < count // 2 or piece == way:
                    going[piece][way] = ring_shift(going[piece][way], 1 - 2 * way)
                    blocks.append(going[piece][way])
        if hop == 1:
            going, ready = lax.optimization_barrier((going, ready))
    return [blocks[at : at + 8] for at in range(0, len(blocks), 8)], (), lambda pending: [], ready


def grid_arrivals():
    table = []
    for origin in ((0, 1, 2, 3), (1, 0, 3, 2), (2, 2, 1, 1), (3, 3, 0, 0)):
        table.append(np.array([2 * origin[r // 2] + r % 2 for r in range(8)]))
        table.append(table[-1] ^ 1)
    return np.stack(table, axis=1), [0] * 8


def along_grid(pieces, ready):
    z = lax.axis_index("tensor") // 2

    def shift(rows, steps, starts):
        pairs = [(2 * s + c, 2 * (s + steps) + c) for s in starts for c in range(2)]
        return lax.ppermute(rows, "tensor", pairs)

    def cross(rows):
        return lax.ppermute(rows, "tensor", [(r, r ^ 1) for r in range(8)])

    def pick(*rows):
        return jnp.where(z == 0, rows[0], jnp.where(z == 1, rows[1], jnp.where(z == 2, rows[2], rows[3])))

    (rows,) = pieces
    up, down, crossed = shift(rows, 1, (0, 1, 2)), shift(rows, -1, (1, 2, 3)), cross(rows)
    up, down, crossed, parcels = lax.optimization_barrier((up, down, crossed, ready[0]))
    ready = (parcels, *ready[1:])
    second = pick(down, up, down, up)
    up2, down2, crossed2 = lax.optimization_barrier(
        (shift(up, 1, (1, 2)), shift(down, -1, (1, 2)), cross(second))
    )
    up2, down2, crossed2, ready = lax.optimization_barrier((up2, down2, crossed2, ready))
    third = pick(down2, down, up, up2)
    outward = jnp.where(z == 1, down2, up2)
    ends = lax.ppermute(outward, "tensor", [(2, 0), (3, 1), (4, 6), (5, 7)])
    crossed3 = cross(third)

    def finish(pending):
        up2, down2, ends = pending
        fourth = pick(ends, down2, up2, ends)
        return [[fourth, cross(fourth)]]

    groups = [[rows, crossed, second, crossed2, third, crossed3]]
    return groups, (up2, down2, ends), finish, ready


def rope_tables(positions, lib=jnp):
    half_dim = HD // 2
    freqs = ROPE_BASE ** (-(lib.arange(half_dim, dtype=lib.float32) * 2.0 / HD))
    angles = positions.astype(lib.float32)[:, None] * freqs[None, :].astype(lib.float32)
    cosine = lib.cos(angles)
    sine = lib.sin(angles)
    return (
        lib.concatenate([cosine, cosine], axis=1).astype(lib.float32),
        lib.concatenate([-sine, sine], axis=1).astype(lib.float32),
    )


def whole():
    return pl.BlockSpec(memory_space=pltpu.VMEM)


def normed_rows(values, gain):
    square = jnp.mean(values * values, axis=-1, keepdims=True)
    return values * lax.rsqrt(square + EPS) * gain


def prepare_kernel(prompt_ref, state_ref, gain_ref, *out_refs):
    tokens, width = prompt_ref.shape
    rows = tokens // len(out_refs)
    gain = gain_ref[...].astype(jnp.float32)
    for index, out_ref in enumerate(out_refs):
        part = prompt_ref[index * rows : (index + 1) * rows, :].astype(jnp.float32)
        out_ref[:rows, :] = normed_rows(part, gain).astype(jnp.bfloat16)
    states = normed_rows(state_ref[...].astype(jnp.float32), gain)
    filling = jnp.zeros((out_refs[-1].shape[0] - rows - states.shape[0], width), jnp.float32)
    out_refs[-1][rows:, :] = jnp.concatenate([states, filling], axis=0).astype(jnp.bfloat16)


def prepare(prompts, states, gain, pieces):
    tokens, width = prompts.shape
    rows = [tokens // pieces] * pieces
    rows[-1] += -(-states.shape[0] // LANES) * LANES
    return pl.pallas_call(
        prepare_kernel,
        out_shape=tuple(jax.ShapeDtypeStruct((count, width), jnp.bfloat16) for count in rows),
        in_specs=[whole()] * 3,
        out_specs=tuple(whole() for _ in rows),
        compiler_params=pltpu.CompilerParams(vmem_limit_bytes=VMEM_LIMIT),
        name="prepare",
    )(prompts, states, gain)


def project_kernel(rows, each, skipped, *refs):
    blocks, (starts_ref, weight_ref, cos_ref, sin_ref, out_ref, states_ref) = refs[:-6], refs[-6:]
    depth = weight_ref.shape[0] // CHUNKS
    total = jnp.zeros(out_ref.shape, jnp.float32)
    for c in range(CHUNKS):
        part = slice(c * depth, (c + 1) * depth)
        x = jnp.concatenate([block[:rows, part] for block in blocks], axis=0)
        total += jnp.dot(x, weight_ref[part, :], preferred_element_type=jnp.float32)
    out_ref[:, HD:] = total[:, HD:].astype(jnp.bfloat16)
    found = 0
    for index, block in enumerate(blocks):
        begin = starts_ref[skipped + index] % PLEN
        span = pl.ds(pl.multiple_of(begin, rows), rows)
        here = slice(index * rows, (index + 1) * rows)
        keys = turn(total[here, :HD], cos_ref[span, :], sin_ref[span, :])
        out_ref[here, :HD] = keys.astype(jnp.bfloat16)
        if block.shape[0] > rows:
            states_ref[found] = block[rows:, :].astype(jnp.float32)[:each, :].astype(jnp.bfloat16)
            found += 1


def project(blocks, weight, starts, skipped, rows, each):
    width = weight.shape[0]
    cosine, sine = rope_tables(np.arange(PLEN), np)
    carrying = sum(block.shape[0] > rows for block in blocks)
    return pl.pallas_call(
        functools.partial(project_kernel, rows, each, skipped),
        out_shape=(
            jax.ShapeDtypeStruct((len(blocks) * rows, 2 * HD), jnp.bfloat16),
            jax.ShapeDtypeStruct((carrying, each, width), jnp.bfloat16),
        ),
        in_specs=[whole()] * len(blocks) + [pl.BlockSpec(memory_space=pltpu.SMEM)] + [whole()] * 3,
        out_specs=(whole(), whole()),
        compiler_params=pltpu.CompilerParams(vmem_limit_bytes=VMEM_LIMIT),
        cost_estimate=pl.CostEstimate(
            flops=2 * len(blocks) * rows * weight.size,
            bytes_accessed=2 * weight.size,
            transcendentals=0,
        ),
        name="project",
    )(*blocks, starts, weight, cosine, sine)


def parcels_kernel(heads, table_ref, used_ref, info_ref, pool_ref, sure_ref, more_ref, held, load_sem, store_sem):
    width = sure_ref.shape[-1]
    each, per_request = table_ref.shape
    pages = each * per_request
    sure = sure_ref.shape[1] - 1
    stores = []
    for target in range(len(heads)):
        copy = pltpu.make_async_copy(info_ref, sure_ref.at[target, 0], store_sem.at[0, target])
        copy.start()
        stores.append(copy)
    front = jnp.int32(0)
    back = used_ref[0]
    for r in range(1, each):
        back = back + used_ref[r]
    loads = []
    for r in range(each):
        used = used_ref[r]
        for p in range(per_request):
            spot = jnp.where(p < used, front + p, back + p - used)
            copy = pltpu.make_async_copy(
                pool_ref.at[table_ref[r, p]], held.at[spot], load_sem.at[r * per_request + p]
            )
            copy.start()
            loads.append(copy)
        front = front + used
        back = back + per_request - used
    for copy in loads:
        copy.wait()
    for target, head in enumerate(heads):
        columns = pl.ds(head * width, width)
        for bank, source, goal in (
            (1, held.at[pl.ds(0, sure), :, columns], sure_ref.at[target, pl.ds(1, sure)]),
            (2, held.at[pl.ds(sure, pages - sure), :, columns], more_ref.at[target]),
        ):
            copy = pltpu.make_async_copy(source, goal, store_sem.at[bank, target])
            copy.start()
            stores.append(copy)
    for copy in stores:
        copy.wait()


def make_parcels(table, used, info, pool, heads, width):
    pages, rows, _ = pool.shape
    hbm = pl.BlockSpec(memory_space=pltpu.HBM)
    smem = pl.BlockSpec(memory_space=pltpu.SMEM)
    return pl.pallas_call(
        functools.partial(parcels_kernel, heads),
        out_shape=(
            pltpu.HBM((len(heads), SURE + 1, rows, width), jnp.bfloat16),
            pltpu.HBM((len(heads), pages - SURE, rows, width), jnp.bfloat16),
        ),
        in_specs=[smem, smem, whole(), hbm],
        out_specs=(hbm, hbm),
        scratch_shapes=[
            pltpu.VMEM(pool.shape, jnp.bfloat16),
            pltpu.SemaphoreType.DMA((pages,)),
            pltpu.SemaphoreType.DMA((3, len(heads))),
        ],
        compiler_params=pltpu.CompilerParams(vmem_limit_bytes=VMEM_LIMIT),
        name="parcels",
    )(table, used, info, pltpu.with_memory_space_constraint(pool, pltpu.HBM))


def turn(values, cosine, sine):
    return values * cosine + pltpu.roll(values, HD // 2, 1) * sine


def step_kernel(blocks, iteration, groups, each, *refs):
    x_refs = refs[:blocks]
    order_ref, lens_ref, used_ref, first_ref, cos_ref, sin_ref = refs[blocks : blocks + 6]
    new_refs = refs[blocks + 6 : blocks + 6 + iteration]
    refs = refs[blocks + 6 + iteration :]
    if iteration == 0:
        target_ref, landing_ref, prompt_ref, offset_ref = refs[:4]
        arrived_refs = refs[4 : 4 + groups]
        refs = refs[4 + groups :]
        wq_in, wkv_in, wo_in, sure_in, more_in, out_ref, fresh_ref, wq, wkv, wo, cache = refs[:11]
        x_rows, q_s, score_s, mix_s, new_s, sems, patch_sems = refs[11:]
    else:
        wq, wkv, wo, cache = refs[:4]
        out_ref, fresh_ref, x_rows, q_s, score_s, mix_s, new_s = refs[4:]
    width, q_cols = wq.shape
    owners = cache.shape[0]
    count = owners * each
    span = (cache.shape[1] // PAGE - 1) // each * PAGE
    heads = q_cols // HD
    depth = width // CHUNKS

    waits = {}
    if iteration == 0:
        for c in range(CHUNKS):
            part = pl.ds(c * depth, depth)
            waits[c] = [
                pltpu.make_async_copy(wq_in.at[part, :], wq.at[part, :], sems.at[0, c]),
                pltpu.make_async_copy(wkv_in.at[part, :], wkv.at[part, :], sems.at[1, c]),
            ]
            waits["out", c] = [pltpu.make_async_copy(wo_in.at[:, part], wo.at[:, part], sems.at[2, c])]
        sure = sure_in.shape[1]
        waits["cache"] = [
            pltpu.make_async_copy(sure_in, cache.at[:, pl.ds(0, sure), :], sems.at[3, 0]),
            pltpu.make_async_copy(
                more_in, cache.at[:, pl.ds(sure, more_in.shape[1]), :], sems.at[3, 1]
            ),
        ]
        for name in [0, 1, 2, 3, "cache", 4, 5, 6, 7] + [("out", c) for c in range(CHUNKS)]:
            for copy in waits[name]:
                copy.start()

    def wait(name):
        for copy in waits.get(name, ()):
            copy.wait()

    def receivers():
        lines = [
            cache[owner, :PAGE, :HD].astype(jnp.float32)[:1, :] for owner in range(owners)
        ]
        firsts = jnp.concatenate(lines, axis=0)
        owner = lax.broadcasted_iota(jnp.int32, firsts.shape, 0)
        slot = lax.broadcasted_iota(jnp.int32, firsts.shape, 1)
        numbers = (owner * each + slot).astype(jnp.float32)
        found = []
        for k in range(target_ref.shape[0]):
            here = (owner == target_ref[k]) & (slot < each)
            here = here & (firsts == landing_ref[k].astype(jnp.float32))
            found.append(jnp.sum(jnp.where(here, numbers, 0.0)).astype(jnp.int32))
        return found

    def window(r, size, page=0):
        return pl.ds(pl.multiple_of((first_ref[r] + page + 1) * PAGE, PAGE), size)

    def patch(requests, action):
        pieces = offset_ref.shape[0]
        rows = sum(ref.shape[0] for ref in arrived_refs) // pieces
        piece = 0
        for ref in arrived_refs:
            for local in range(ref.shape[0] // rows):
                request = jnp.int32(0)
                for k, number in enumerate(requests):
                    request = jnp.where(prompt_ref[piece] == k, number, request)
                for p in range(rows // PAGE):
                    page = offset_ref[piece] // PAGE + p

                    @pl.when(page < used_ref[request])
                    def _():
                        copy = pltpu.make_async_copy(
                            ref.at[pl.ds(local * rows + p * PAGE, PAGE), :],
                            cache.at[request // each, window(request, PAGE, page), :],
                            patch_sems.at[piece, p],
                        )
                        action(copy)

                piece += 1

    place = 0
    for ref in x_refs:
        for rows in [ref[...]] if ref.ndim == 2 else [ref[k] for k in range(ref.shape[0])]:
            x_rows[place : place + each, :] = rows.astype(jnp.float32)
            place += each
    order = order_ref[...]

    query = jnp.zeros((count, q_cols), jnp.float32)
    keyvalue = jnp.zeros((count, 2 * HD), jnp.float32)
    for c in range(CHUNKS):
        part = slice(c * depth, (c + 1) * depth)
        x = jnp.dot(
            order, x_rows[:, part].astype(jnp.bfloat16), preferred_element_type=jnp.float32
        ).astype(jnp.bfloat16)
        wait(c)
        query += jnp.dot(x, wq[part, :], preferred_element_type=jnp.float32)
        keyvalue += jnp.dot(x, wkv[part, :], preferred_element_type=jnp.float32)
        if iteration == 0 and c == CHUNKS - 2:
            wait("cache")
            requests = receivers()
            patch(requests, lambda copy: copy.start())

    cosine = cos_ref[iteration]
    sine = sin_ref[iteration]
    key = turn(keyvalue[:, :HD], cosine, sine).astype(jnp.bfloat16)
    value = keyvalue[:, HD:].astype(jnp.bfloat16)
    fresh_ref[:, :HD] = key
    fresh_ref[:, HD:] = value
    news = [(ref[:, :HD], ref[:, HD:]) for ref in new_refs] + [(key, value)]
    for j in range(LANES):
        lane = pl.ds(j, count, LANES)
        if j < heads:
            turned = turn(query[:, j * HD : (j + 1) * HD], cosine, sine).astype(jnp.bfloat16)
            q_s[lane, :] = turned.astype(jnp.float32)
        else:
            q_s[lane, :] = jnp.zeros((count, HD), jnp.float32)
        for t, pair in enumerate(news):
            for half in range(2):
                new_s[t, half, lane, :] = pair[half].astype(jnp.float32)

    if iteration == 0:
        patch(requests, lambda copy: copy.wait())
    scale = HD**-0.5
    column = lax.broadcasted_iota(jnp.int32, (LANES, span), 1)
    for r in range(count):
        rows = slice(r * LANES, (r + 1) * LANES)
        found = lax.dot_general(
            q_s[rows, :].astype(jnp.bfloat16),
            cache[r // each, window(r, span), :HD],
            (((1,), (1,)), ((), ())),
            preferred_element_type=jnp.float32,
        )
        score_s[rows, :] = jnp.where(column < lens_ref[r], found * scale, -1e30)

    scores = score_s[...]
    queries = q_s[...]
    fresh_scores = [
        jnp.sum(queries * new_s[t, 0], axis=-1, keepdims=True) * scale for t in range(iteration + 1)
    ]
    top = jnp.max(scores, axis=-1, keepdims=True)
    for s in fresh_scores:
        top = jnp.maximum(top, s)
    weights = jnp.exp(scores - top)
    fresh_weights = [jnp.exp(s - top) for s in fresh_scores]
    total = jnp.sum(weights, axis=-1, keepdims=True)
    for w in fresh_weights:
        total = total + w
    score_s[...] = weights / total
    row = lax.broadcasted_iota(jnp.int32, (span, HD), 0)
    for r in range(count):
        rows = slice(r * LANES, (r + 1) * LANES)
        mix_s[rows, :] = jnp.dot(
            score_s[rows, :].astype(jnp.bfloat16),
            jnp.where(
                row < lens_ref[r],
                cache[r // each, window(r, span), HD:],
                jnp.zeros((), jnp.bfloat16),
            ),
            preferred_element_type=jnp.float32,
        )
    mixed = mix_s[...]
    for t in range(iteration + 1):
        weight = (fresh_weights[t] / total).astype(jnp.bfloat16).astype(jnp.float32)
        mixed = mixed + weight * new_s[t, 1]
    mix_s[...] = mixed
    columns = jnp.concatenate(
        [mix_s[pl.ds(j, count, LANES), :].astype(jnp.bfloat16) for j in range(heads)], axis=1
    )
    for c in range(CHUNKS):
        part = slice(c * depth, (c + 1) * depth)
        wait(("out", c))
        product = jnp.dot(columns, wo[:, part], preferred_element_type=jnp.float32)
        for d in range(owners):
            out_ref[d, :, part] = product[d * each : (d + 1) * each, :].astype(jnp.bfloat16)


def step(x_blocks, order, lengths, used, first, cosine, sine, earlier, held, each, prompts=()):
    width, q_cols = held[0].shape
    owners = held[3].shape[0]
    count = owners * each
    cached = sum(a.shape[1] for a in held[3:])
    span = (cached // PAGE - 1) // each * PAGE
    iteration = len(earlier)
    blocks = len(x_blocks)
    groups = max(len(prompts) - 4, 0)
    smem = pl.BlockSpec(memory_space=pltpu.SMEM)
    hbm = pl.BlockSpec(memory_space=pltpu.HBM)
    out_shape = [
        jax.ShapeDtypeStruct((owners, each, width), jnp.bfloat16),
        jax.ShapeDtypeStruct((count, 2 * HD), jnp.bfloat16),
    ]
    in_specs = [whole()] * (blocks + 1) + [smem] * 3 + [whole()] * (2 + iteration)
    scratch = [
        pltpu.VMEM((count, width), jnp.float32),
        pltpu.VMEM((count * LANES, HD), jnp.float32),
        pltpu.VMEM((count * LANES, span), jnp.float32),
        pltpu.VMEM((count * LANES, HD), jnp.float32),
        pltpu.VMEM((iteration + 1, 2, count * LANES, HD), jnp.float32),
    ]
    if iteration == 0:
        in_specs += [smem] * 4 + [whole()] * groups + [hbm] * 5
        out_shape += [pltpu.VMEM(a.shape, a.dtype) for a in held[:3]]
        out_shape.append(pltpu.VMEM((owners, cached, 2 * HD), jnp.bfloat16))
        held = [pltpu.with_memory_space_constraint(a, pltpu.HBM) for a in held]
        pieces = prompts[3].shape[0]
        pages = sum(a.shape[0] for a in prompts[4:]) // pieces // PAGE
        scratch.append(pltpu.SemaphoreType.DMA((4, CHUNKS)))
        scratch.append(pltpu.SemaphoreType.DMA((pieces, pages)))
    else:
        in_specs += [whole()] * 4
    return pl.pallas_call(
        functools.partial(step_kernel, blocks, iteration, groups, each),
        out_shape=tuple(out_shape),
        in_specs=in_specs,
        out_specs=tuple(whole() for _ in out_shape),
        scratch_shapes=scratch,
        compiler_params=pltpu.CompilerParams(vmem_limit_bytes=VMEM_LIMIT),
        cost_estimate=pl.CostEstimate(
            flops=2 * count * width * (2 * q_cols + 2 * HD),
            bytes_accessed=2 * sum(a.size for a in held),
            transcendentals=count * LANES * span,
        ),
        name="decode_step",
    )(*x_blocks, order, lengths, used, first, cosine, sine, *earlier, *prompts, *held)


def settle_kernel(parts_ref, state_ref, gain_ref, next_ref, normed_ref):
    total = parts_ref[0].astype(jnp.float32)
    for d in range(1, parts_ref.shape[0]):
        total = total + parts_ref[d].astype(jnp.float32)
    state = (state_ref[...].astype(jnp.float32) + total).astype(jnp.bfloat16)
    next_ref[...] = state
    gain = gain_ref[...].astype(jnp.float32)
    normed_ref[...] = normed_rows(state.astype(jnp.float32), gain).astype(jnp.bfloat16)


def settle(parts, state, gain):
    shape = jax.ShapeDtypeStruct(state.shape, jnp.bfloat16)
    return pl.pallas_call(
        settle_kernel,
        out_shape=(shape, shape),
        in_specs=[whole()] * 3,
        out_specs=(whole(), whole()),
        compiler_params=pltpu.CompilerParams(vmem_limit_bytes=VMEM_LIMIT),
        name="settle",
    )(parts, state, gain)


def on_device(
    prompt_states,
    decode_states,
    norm_gain,
    w_query,
    w_keyvalue,
    w_output,
    cache_pages,
    page_table,
    cache_len,
    dest_rank,
    dest_page,
):
    rank = lax.axis_index("tensor")
    section = lax.axis_index("section")
    count = lax.axis_size("tensor")
    pool = cache_pages[0]
    page_size, kv_width = pool.shape[1:]
    own_table = page_table[0]
    lengths = cache_len[0]
    each, width = decode_states.shape[1:]
    tokens = prompt_states.shape[1]
    q_cols = w_query.shape[1]
    kv_heads = kv_width // (2 * HD)
    shared = count // kv_heads if count > kv_heads else 1
    gain = norm_gain[None, :]

    if w_keyvalue.shape[1] < 2 * HD:
        other = swap_xor(w_keyvalue, 1)
        is_key = rank % 2 == 0
        w_pair = jnp.concatenate(
            [jnp.where(is_key, w_keyvalue, other), jnp.where(is_key, other, w_keyvalue)], axis=1
        )
    else:
        w_pair = w_keyvalue

    numbers = jnp.arange(count * each, dtype=jnp.int32)
    per_request = own_table.shape[1]
    used = (lengths + page_size - 1) // page_size
    by_owner = used.reshape(count, each)
    first = (jnp.cumsum(by_owner, axis=1) - by_owner).reshape(-1)
    most = jnp.max(jnp.sum(by_owner, axis=1, keepdims=True), keepdims=True)
    for axis in ("section", "groups"):
        for bit in range(lax.axis_size(axis).bit_length() - 1):
            pairs = [(s, s ^ (1 << bit)) for s in range(lax.axis_size(axis))]
            most = jnp.maximum(most, lax.ppermute(most, axis, pairs))
    own_used = lax.dynamic_slice_in_dim(used, rank * each, each)
    heads = tuple(target // shared for target in range(count))
    info = jnp.zeros((page_size, 2 * HD), jnp.bfloat16)
    info = info.at[0, :each].set(own_table[:, 0].astype(jnp.bfloat16))
    ready = make_parcels(own_table, own_used, info, pool, heads, 2 * HD)

    grid = count == 8
    table, halves = grid_arrivals() if grid else ring_arrivals(count)
    parts = 1 if grid else 2
    rows = tokens // parts
    carried = np.array([index for index, piece in enumerate(halves) if piece == parts - 1])
    senders = jnp.asarray(table, jnp.int32)[rank]
    starts = senders * tokens + jnp.asarray(halves, jnp.int32) * rows
    orders = []
    for owners in (senders[carried], rank ^ jnp.arange(count, dtype=jnp.int32)):
        rows_of = jnp.repeat(owners * each, each) + numbers % each
        orders.append((numbers[:, None] == rows_of[None, :]).astype(jnp.bfloat16))
    times = lengths[None, :] + jnp.arange(STEPS, dtype=jnp.int32)[:, None]
    cosine, sine = rope_tables(times.reshape(-1))
    cosine = cosine.reshape(STEPS, count * each, HD)
    sine = sine.reshape(STEPS, count * each, HD)
    sizes = [size for size in MORE if size < pool.shape[0] - SURE] + [pool.shape[0] - SURE]
    wanted = most[0, 0] - SURE
    choice = jnp.sum((wanted > jnp.array(sizes[:-1], jnp.int32)).astype(jnp.int32))
    ready = (ready, choice, starts, orders, cosine, sine)
    pieces = prepare(prompt_states[0], decode_states[0], gain, parts)
    known, pending, finish, ready = (along_grid if grid else along_ring)(pieces, ready)
    ready, choice, starts, orders, cosine, sine = ready

    sure, more = ready

    def exchange(pages):
        return lax.all_to_all(
            pages.reshape(count, -1, 2 * HD), "tensor", split_axis=0, concat_axis=0, tiled=True
        )

    extra = more.shape[1]

    def branch(size):
        def run(more):
            if size == 0:
                return jnp.zeros((count, extra * page_size, 2 * HD), jnp.bfloat16)
            pages = exchange(more[:, :size])
            return jnp.pad(pages, ((0, 0), (0, (extra - size) * page_size), (0, 0)))

        return run

    more = lax.switch(choice, [branch(size) for size in sizes], more)
    known, pending, more = lax.optimization_barrier((known, pending, more))
    final = finish(pending)
    if final:
        small = final[0][0][:LANES, :HD] * 2.0
        sure, _ = lax.optimization_barrier((sure, small))
    else:
        sure, _ = lax.optimization_barrier((sure, more))
    sure = exchange(sure)

    prompt_kv = []
    blocks = []
    skipped = 0
    for group in known + final:
        values, states = project(group, w_pair, starts, skipped, rows, each)
        prompt_kv.append(values)
        blocks.append(states)
        skipped += len(group)
    sections = lax.axis_size("section")
    onward = [(s, (s + 1) % sections) for s in range(sections)]
    arrived = tuple(lax.ppermute(part, "section", onward) for part in prompt_kv)

    anchor = (section + 1) % sections
    targets = lax.dynamic_index_in_dim(dest_rank, anchor, 0, keepdims=False)
    landing = lax.dynamic_index_in_dim(dest_page, anchor, 0, keepdims=False)[:, 0]
    prompts = (targets, landing, starts // PLEN, starts % PLEN, *arrived)
    held = (w_query, w_pair, w_output, sure, more)

    blocks, cosine, sine, state = lax.optimization_barrier((blocks, cosine, sine, decode_states[0]))
    outputs = []
    earlier = []
    for iteration in range(STEPS):
        chosen = orders[min(iteration, 1)]
        parts, fresh, *fetched = step(
            blocks, chosen, lengths, used, first, cosine, sine, earlier, held, each, prompts
        )
        if iteration == 0:
            held, prompts = fetched, ()
        earlier.append(fresh)
        parts = lax.all_to_all(parts, "tensor", split_axis=0, concat_axis=0, tiled=True)
        state, normed = settle(parts, state, gain)
        outputs.append(state)
        if iteration + 1 < STEPS:
            blocks = [normed] + [swap_xor(normed, bits) for bits in range(1, count)]
    return jnp.stack(outputs)[:, None]


def solution(mesh):
    in_specs = (
        P(("groups", "section"), "tensor", None),
        P(("groups", "section"), "tensor", None),
        P(),
        P(None, "tensor"),
        P(None, "tensor"),
        P("tensor", None),
        P(("groups", "section"), "tensor", None, None),
        P(("groups", "section"), "tensor", None),
        P(("groups", "section"), None),
        P("groups", None),
        P("groups", None, None),
    )
    out_specs = P(None, ("groups", "section"), "tensor", None)
    return jax.shard_map(
        on_device, mesh=mesh, in_specs=in_specs, out_specs=out_specs, check_vma=False
    )
```

```python
import functools

import jax
import jax.numpy as jnp
import numpy as np
from jax import lax
from jax.experimental import pallas as pl
from jax.experimental.pallas import tpu as pltpu
from jax.sharding import PartitionSpec as P

HD = 128
PLEN = 128
STEPS = 4
EPS = 1e-05
ROPE_BASE = 500000.0
LANES = 8
CHUNKS = 8
PAGE = 16
SURE = 24
MORE = (0, 4, 8, 12, 16, 20, 24, 28, 32)
VMEM_LIMIT = 10 * 1024 * 1024


def ring_shift(value, steps):
    count = lax.axis_size("tensor")
    return lax.ppermute(value, "tensor", [(s, (s + steps) % count) for s in range(count)])


def swap_xor(value, mask):
    count = lax.axis_size("tensor")
    return lax.ppermute(value, "tensor", [(s, s ^ mask) for s in range(count)])


def ring_arrivals(count):
    table, halves = [np.arange(count)] * 2, [0, 1]
    for hop in range(1, count // 2 + 1):
        for piece in range(2):
            for way in range(2):
                if hop < count // 2 or piece == way:
                    table.append((np.arange(count) - (1 - 2 * way) * hop) % count)
                    halves.append(piece)
    return np.stack(table, axis=1), halves


def along_ring(pieces, ready):
    count = lax.axis_size("tensor")
    blocks = list(pieces)
    going = [[rows, rows] for rows in pieces]
    for hop in range(1, count // 2 + 1):
        for piece in range(2):
            for way in range(2):
                if hop < count // 2 or piece == way:
                    going[piece][way] = ring_shift(going[piece][way], 1 - 2 * way)
                    blocks.append(going[piece][way])
        if hop == 1:
            going, ready = lax.optimization_barrier((going, ready))
    return [blocks[at : at + 8] for at in range(0, len(blocks), 8)], (), lambda pending: [], ready


def cross(value):
    return lax.ppermute(value, "tensor", [(r, r ^ 1) for r in range(8)])


def grid_arrivals():
    table = []
    for across in (0, 1):
        for origin in ((0, 1, 2, 3), (1, 0, 3, 2), (2, 2, 1, 1), (3, 3, 0, 0)):
            table.append(np.array([(2 * origin[r // 2] + r % 2) ^ across for r in range(8)]))
    return np.stack(table, axis=1), [0] * 8


def along_grid(pieces, ready):
    z = lax.axis_index("tensor") // 2

    def shift(rows, steps, starts):
        pairs = [(2 * s + c, 2 * (s + steps) + c) for s in starts for c in range(2)]
        return lax.ppermute(rows, "tensor", pairs)

    def pick(*rows):
        return jnp.where(z == 0, rows[0], jnp.where(z == 1, rows[1], jnp.where(z == 2, rows[2], rows[3])))

    (rows,) = pieces
    up, down = shift(rows, 1, (0, 1, 2)), shift(rows, -1, (1, 2, 3))
    up, down, parcels, weight = lax.optimization_barrier((up, down, *ready[:2]))
    section = lax.axis_index("section")
    half = weight.shape[0] // 2
    brought = cross(lax.dynamic_slice_in_dim(weight, section * half, half))
    ready = (parcels, *ready[2:])
    up2, down2 = shift(up, 1, (1, 2)), shift(down, -1, (1, 2))
    up2, down2, ready = lax.optimization_barrier((up2, down2, ready))
    outward = jnp.where(z == 1, down2, up2)
    ends = lax.ppermute(outward, "tensor", [(2, 0), (3, 1), (4, 6), (5, 7)])

    def finish(pending):
        up, down, up2, down2, ends, brought = pending
        given = lax.ppermute(brought, "section", [(0, 1), (1, 0)])
        other = jnp.where(
            section == 0,
            jnp.concatenate([brought, given], axis=0),
            jnp.concatenate([given, brought], axis=0),
        )
        second = pick(down, up, down, up)
        third = pick(down2, down, up, up2)
        fourth = pick(ends, down2, up2, ends)
        return [second, third, fourth], other

    return [[rows]], (up, down, up2, down2, ends, brought), finish, ready


def rope_tables(positions, lib=jnp):
    half_dim = HD // 2
    freqs = ROPE_BASE ** (-(lib.arange(half_dim, dtype=lib.float32) * 2.0 / HD))
    angles = positions.astype(lib.float32)[:, None] * freqs[None, :].astype(lib.float32)
    cosine = lib.cos(angles)
    sine = lib.sin(angles)
    return (
        lib.concatenate([cosine, cosine], axis=1).astype(lib.float32),
        lib.concatenate([-sine, sine], axis=1).astype(lib.float32),
    )


def whole():
    return pl.BlockSpec(memory_space=pltpu.VMEM)


def normed_rows(values, gain):
    square = jnp.mean(values * values, axis=-1, keepdims=True)
    return values * lax.rsqrt(square + EPS) * gain


def prepare_kernel(prompt_ref, state_ref, gain_ref, *out_refs):
    tokens, width = prompt_ref.shape
    rows = tokens // len(out_refs)
    gain = gain_ref[...].astype(jnp.float32)
    for index, out_ref in enumerate(out_refs):
        part = prompt_ref[index * rows : (index + 1) * rows, :].astype(jnp.float32)
        out_ref[:rows, :] = normed_rows(part, gain).astype(jnp.bfloat16)
    states = normed_rows(state_ref[...].astype(jnp.float32), gain)
    filling = jnp.zeros((out_refs[-1].shape[0] - rows - states.shape[0], width), jnp.float32)
    out_refs[-1][rows:, :] = jnp.concatenate([states, filling], axis=0).astype(jnp.bfloat16)


def prepare(prompts, states, gain, pieces):
    tokens, width = prompts.shape
    rows = [tokens // pieces] * pieces
    rows[-1] += -(-states.shape[0] // LANES) * LANES
    return pl.pallas_call(
        prepare_kernel,
        out_shape=tuple(jax.ShapeDtypeStruct((count, width), jnp.bfloat16) for count in rows),
        in_specs=[whole()] * 3,
        out_specs=tuple(whole() for _ in rows),
        compiler_params=pltpu.CompilerParams(vmem_limit_bytes=VMEM_LIMIT),
        name="prepare",
    )(prompts, states, gain)


def project_kernel(rows, each, skipped, heads, *refs):
    blocks, refs = refs[: -2 * heads - 4], refs[-2 * heads - 4 :]
    starts_ref, cos_ref, sin_ref = refs[:3]
    weight_refs, out_refs, states_ref = refs[3 : 3 + heads], refs[3 + heads : -1], refs[-1]
    depth = weight_refs[0].shape[0] // CHUNKS
    totals = [jnp.zeros(out_ref.shape, jnp.float32) for out_ref in out_refs]
    for c in range(CHUNKS):
        part = slice(c * depth, (c + 1) * depth)
        x = jnp.concatenate([block[:rows, part] for block in blocks], axis=0)
        for head in range(heads):
            totals[head] += jnp.dot(
                x, weight_refs[head][part, :], preferred_element_type=jnp.float32
            )
    for total, out_ref in zip(totals, out_refs):
        out_ref[:, HD:] = total[:, HD:].astype(jnp.bfloat16)
        for index in range(len(blocks)):
            begin = starts_ref[skipped + index] % PLEN
            span = pl.ds(pl.multiple_of(begin, rows), rows)
            here = slice(index * rows, (index + 1) * rows)
            keys = turn(total[here, :HD], cos_ref[span, :], sin_ref[span, :])
            out_ref[here, :HD] = keys.astype(jnp.bfloat16)
    found = 0
    for block in blocks:
        if block.shape[0] > rows:
            states_ref[found] = block[rows:, :].astype(jnp.float32)[:each, :].astype(jnp.bfloat16)
            found += 1


def project(blocks, weights, starts, skipped, rows, each):
    width = weights[0].shape[0]
    cosine, sine = rope_tables(np.arange(PLEN), np)
    carrying = sum(block.shape[0] > rows for block in blocks)
    values = jax.ShapeDtypeStruct((len(blocks) * rows, 2 * HD), jnp.bfloat16)
    out_shape = [values] * len(weights)
    out_shape.append(jax.ShapeDtypeStruct((carrying, each, width), jnp.bfloat16))
    smem = pl.BlockSpec(memory_space=pltpu.SMEM)
    return pl.pallas_call(
        functools.partial(project_kernel, rows, each, skipped, len(weights)),
        out_shape=tuple(out_shape),
        in_specs=[whole()] * len(blocks) + [smem] + [whole()] * (2 + len(weights)),
        out_specs=tuple(whole() for _ in out_shape),
        compiler_params=pltpu.CompilerParams(vmem_limit_bytes=VMEM_LIMIT),
        cost_estimate=pl.CostEstimate(
            flops=2 * len(blocks) * rows * weights[0].size * len(weights),
            bytes_accessed=2 * weights[0].size * len(weights),
            transcendentals=0,
        ),
        name="project",
    )(*blocks, starts, cosine, sine, *weights)


def parcels_kernel(heads, table_ref, used_ref, info_ref, pool_ref, sure_ref, more_ref, held, load_sem, store_sem):
    width = sure_ref.shape[-1]
    each, per_request = table_ref.shape
    pages = each * per_request
    sure = sure_ref.shape[1] - 1
    stores = []
    for target in range(len(heads)):
        copy = pltpu.make_async_copy(info_ref, sure_ref.at[target, 0], store_sem.at[0, target])
        copy.start()
        stores.append(copy)
    front = jnp.int32(0)
    back = used_ref[0]
    for r in range(1, each):
        back = back + used_ref[r]
    loads = []
    for r in range(each):
        used = used_ref[r]
        for p in range(per_request):
            spot = jnp.where(p < used, front + p, back + p - used)
            copy = pltpu.make_async_copy(
                pool_ref.at[table_ref[r, p]], held.at[spot], load_sem.at[r * per_request + p]
            )
            copy.start()
            loads.append(copy)
        front = front + used
        back = back + per_request - used
    for copy in loads:
        copy.wait()
    for target, head in enumerate(heads):
        columns = pl.ds(head * width, width)
        for bank, source, goal in (
            (1, held.at[pl.ds(0, sure), :, columns], sure_ref.at[target, pl.ds(1, sure)]),
            (2, held.at[pl.ds(sure, pages - sure), :, columns], more_ref.at[target]),
        ):
            copy = pltpu.make_async_copy(source, goal, store_sem.at[bank, target])
            copy.start()
            stores.append(copy)
    for copy in stores:
        copy.wait()


def make_parcels(table, used, info, pool, heads, width):
    pages, rows, _ = pool.shape
    hbm = pl.BlockSpec(memory_space=pltpu.HBM)
    smem = pl.BlockSpec(memory_space=pltpu.SMEM)
    return pl.pallas_call(
        functools.partial(parcels_kernel, heads),
        out_shape=(
            pltpu.HBM((len(heads), SURE + 1, rows, width), jnp.bfloat16),
            pltpu.HBM((len(heads), pages - SURE, rows, width), jnp.bfloat16),
        ),
        in_specs=[smem, smem, whole(), hbm],
        out_specs=(hbm, hbm),
        scratch_shapes=[
            pltpu.VMEM(pool.shape, jnp.bfloat16),
            pltpu.SemaphoreType.DMA((pages,)),
            pltpu.SemaphoreType.DMA((3, len(heads))),
        ],
        compiler_params=pltpu.CompilerParams(vmem_limit_bytes=VMEM_LIMIT),
        name="parcels",
    )(table, used, info, pltpu.with_memory_space_constraint(pool, pltpu.HBM))


def turn(values, cosine, sine):
    return values * cosine + pltpu.roll(values, HD // 2, 1) * sine


def step_kernel(blocks, iteration, groups, each, *refs):
    x_refs = refs[:blocks]
    order_ref, lens_ref, used_ref, first_ref, cos_ref, sin_ref = refs[blocks : blocks + 6]
    new_refs = refs[blocks + 6 : blocks + 6 + iteration]
    refs = refs[blocks + 6 + iteration :]
    if iteration == 0:
        target_ref, landing_ref, prompt_ref, offset_ref = refs[:4]
        arrived_refs = refs[4 : 4 + groups]
        refs = refs[4 + groups :]
        wq_in, wkv_in, wo_in, sure_in, more_in, out_ref, fresh_ref, wq, wkv, wo, cache = refs[:11]
        x_rows, q_s, score_s, mix_s, new_s, sems, patch_sems = refs[11:]
    else:
        wq, wkv, wo, cache = refs[:4]
        out_ref, fresh_ref, x_rows, q_s, score_s, mix_s, new_s = refs[4:]
    width, q_cols = wq.shape
    owners = cache.shape[0]
    count = owners * each
    span = (cache.shape[1] // PAGE - 1) // each * PAGE
    heads = q_cols // HD
    depth = width // CHUNKS

    waits = {}
    if iteration == 0:
        for c in range(CHUNKS):
            part = pl.ds(c * depth, depth)
            waits[c] = [
                pltpu.make_async_copy(wq_in.at[part, :], wq.at[part, :], sems.at[0, c]),
                pltpu.make_async_copy(wkv_in.at[part, :], wkv.at[part, :], sems.at[1, c]),
            ]
            waits["out", c] = [pltpu.make_async_copy(wo_in.at[:, part], wo.at[:, part], sems.at[2, c])]
        sure = sure_in.shape[1]
        waits["cache"] = [
            pltpu.make_async_copy(sure_in, cache.at[:, pl.ds(0, sure), :], sems.at[3, 0]),
            pltpu.make_async_copy(
                more_in, cache.at[:, pl.ds(sure, more_in.shape[1]), :], sems.at[3, 1]
            ),
        ]
        for name in [0, 1, 2, 3, "cache", 4, 5, 6, 7]:
            for copy in waits[name]:
                copy.start()

    def wait(name):
        for copy in waits.get(name, ()):
            copy.wait()

    def receivers():
        lines = [
            cache[owner, :PAGE, :HD].astype(jnp.float32)[:1, :] for owner in range(owners)
        ]
        firsts = jnp.concatenate(lines, axis=0)
        owner = lax.broadcasted_iota(jnp.int32, firsts.shape, 0)
        slot = lax.broadcasted_iota(jnp.int32, firsts.shape, 1)
        numbers = (owner * each + slot).astype(jnp.float32)
        found = []
        for k in range(target_ref.shape[0]):
            here = (owner == target_ref[k]) & (slot < each)
            here = here & (firsts == landing_ref[k].astype(jnp.float32))
            found.append(jnp.sum(jnp.where(here, numbers, 0.0)).astype(jnp.int32))
        return found

    def window(r, size, page=0):
        return pl.ds(pl.multiple_of((first_ref[r] + page + 1) * PAGE, PAGE), size)

    def patch(requests, action):
        pieces = offset_ref.shape[0]
        rows = sum(ref.shape[0] for ref in arrived_refs) // pieces
        piece = 0
        for ref in arrived_refs:
            for local in range(ref.shape[0] // rows):
                request = jnp.int32(0)
                for k, number in enumerate(requests):
                    request = jnp.where(prompt_ref[piece] == k, number, request)
                for p in range(rows // PAGE):
                    page = offset_ref[piece] // PAGE + p

                    @pl.when(page < used_ref[request])
                    def _():
                        copy = pltpu.make_async_copy(
                            ref.at[pl.ds(local * rows + p * PAGE, PAGE), :],
                            cache.at[request // each, window(request, PAGE, page), :],
                            patch_sems.at[piece, p],
                        )
                        action(copy)

                piece += 1

    place = 0
    for ref in x_refs:
        for rows in [ref[...]] if ref.ndim == 2 else [ref[k] for k in range(ref.shape[0])]:
            x_rows[place : place + each, :] = rows.astype(jnp.float32)
            place += each
    order = order_ref[...]

    query = jnp.zeros((count, q_cols), jnp.float32)
    keyvalue = jnp.zeros((count, 2 * HD), jnp.float32)
    for c in range(CHUNKS):
        part = slice(c * depth, (c + 1) * depth)
        x = jnp.dot(
            order, x_rows[:, part].astype(jnp.bfloat16), preferred_element_type=jnp.float32
        ).astype(jnp.bfloat16)
        wait(c)
        if iteration == 0:
            for copy in waits["out", c]:
                copy.start()
        query += jnp.dot(x, wq[part, :], preferred_element_type=jnp.float32)
        keyvalue += jnp.dot(x, wkv[part, :], preferred_element_type=jnp.float32)
        if iteration == 0 and c == CHUNKS - 2:
            wait("cache")
            requests = receivers()
            patch(requests, lambda copy: copy.start())

    cosine = cos_ref[iteration]
    sine = sin_ref[iteration]
    key = turn(keyvalue[:, :HD], cosine, sine).astype(jnp.bfloat16)
    value = keyvalue[:, HD:].astype(jnp.bfloat16)
    fresh_ref[:, :HD] = key
    fresh_ref[:, HD:] = value
    news = [(ref[:, :HD], ref[:, HD:]) for ref in new_refs] + [(key, value)]
    for j in range(LANES):
        lane = pl.ds(j, count, LANES)
        if j < heads:
            turned = turn(query[:, j * HD : (j + 1) * HD], cosine, sine).astype(jnp.bfloat16)
            q_s[lane, :] = turned.astype(jnp.float32)
        else:
            q_s[lane, :] = jnp.zeros((count, HD), jnp.float32)
        for t, pair in enumerate(news):
            for half in range(2):
                new_s[t, half, lane, :] = pair[half].astype(jnp.float32)

    if iteration == 0:
        patch(requests, lambda copy: copy.wait())
    scale = HD**-0.5
    column = lax.broadcasted_iota(jnp.int32, (LANES, span), 1)
    for r in range(count):
        rows = slice(r * LANES, (r + 1) * LANES)
        found = lax.dot_general(
            q_s[rows, :].astype(jnp.bfloat16),
            cache[r // each, window(r, span), :HD],
            (((1,), (1,)), ((), ())),
            preferred_element_type=jnp.float32,
        )
        score_s[rows, :] = jnp.where(column < lens_ref[r], found * scale, -1e30)

    scores = score_s[...]
    queries = q_s[...]
    fresh_scores = [
        jnp.sum(queries * new_s[t, 0], axis=-1, keepdims=True) * scale for t in range(iteration + 1)
    ]
    top = jnp.max(scores, axis=-1, keepdims=True)
    for s in fresh_scores:
        top = jnp.maximum(top, s)
    weights = jnp.exp(scores - top)
    fresh_weights = [jnp.exp(s - top) for s in fresh_scores]
    total = jnp.sum(weights, axis=-1, keepdims=True)
    for w in fresh_weights:
        total = total + w
    score_s[...] = weights / total
    row = lax.broadcasted_iota(jnp.int32, (span, HD), 0)
    for r in range(count):
        rows = slice(r * LANES, (r + 1) * LANES)
        mix_s[rows, :] = jnp.dot(
            score_s[rows, :].astype(jnp.bfloat16),
            jnp.where(
                row < lens_ref[r],
                cache[r // each, window(r, span), HD:],
                jnp.zeros((), jnp.bfloat16),
            ),
            preferred_element_type=jnp.float32,
        )
    mixed = mix_s[...]
    for t in range(iteration + 1):
        weight = (fresh_weights[t] / total).astype(jnp.bfloat16).astype(jnp.float32)
        mixed = mixed + weight * new_s[t, 1]
    mix_s[...] = mixed
    columns = jnp.concatenate(
        [mix_s[pl.ds(j, count, LANES), :].astype(jnp.bfloat16) for j in range(heads)], axis=1
    )
    for c in range(CHUNKS):
        part = slice(c * depth, (c + 1) * depth)
        wait(("out", c))
        product = jnp.dot(columns, wo[:, part], preferred_element_type=jnp.float32)
        for d in range(owners):
            out_ref[d, :, part] = product[d * each : (d + 1) * each, :].astype(jnp.bfloat16)


def step(x_blocks, order, lengths, used, first, cosine, sine, earlier, held, each, prompts=()):
    width, q_cols = held[0].shape
    owners = held[3].shape[0]
    count = owners * each
    cached = sum(a.shape[1] for a in held[3:])
    span = (cached // PAGE - 1) // each * PAGE
    iteration = len(earlier)
    blocks = len(x_blocks)
    groups = max(len(prompts) - 4, 0)
    smem = pl.BlockSpec(memory_space=pltpu.SMEM)
    hbm = pl.BlockSpec(memory_space=pltpu.HBM)
    out_shape = [
        jax.ShapeDtypeStruct((owners, each, width), jnp.bfloat16),
        jax.ShapeDtypeStruct((count, 2 * HD), jnp.bfloat16),
    ]
    in_specs = [whole()] * (blocks + 1) + [smem] * 3 + [whole()] * (2 + iteration)
    scratch = [
        pltpu.VMEM((count, width), jnp.float32),
        pltpu.VMEM((count * LANES, HD), jnp.float32),
        pltpu.VMEM((count * LANES, span), jnp.float32),
        pltpu.VMEM((count * LANES, HD), jnp.float32),
        pltpu.VMEM((iteration + 1, 2, count * LANES, HD), jnp.float32),
    ]
    if iteration == 0:
        in_specs += [smem] * 4 + [whole()] * groups + [hbm] * 5
        out_shape += [pltpu.VMEM(a.shape, a.dtype) for a in held[:3]]
        out_shape.append(pltpu.VMEM((owners, cached, 2 * HD), jnp.bfloat16))
        held = [pltpu.with_memory_space_constraint(a, pltpu.HBM) for a in held]
        pieces = prompts[3].shape[0]
        pages = sum(a.shape[0] for a in prompts[4:]) // pieces // PAGE
        scratch.append(pltpu.SemaphoreType.DMA((4, CHUNKS)))
        scratch.append(pltpu.SemaphoreType.DMA((pieces, pages)))
    else:
        in_specs += [whole()] * 4
    return pl.pallas_call(
        functools.partial(step_kernel, blocks, iteration, groups, each),
        out_shape=tuple(out_shape),
        in_specs=in_specs,
        out_specs=tuple(whole() for _ in out_shape),
        scratch_shapes=scratch,
        compiler_params=pltpu.CompilerParams(vmem_limit_bytes=VMEM_LIMIT),
        cost_estimate=pl.CostEstimate(
            flops=2 * count * width * (2 * q_cols + 2 * HD),
            bytes_accessed=2 * sum(a.size for a in held),
            transcendentals=count * LANES * span,
        ),
        name="decode_step",
    )(*x_blocks, order, lengths, used, first, cosine, sine, *earlier, *prompts, *held)


def settle_kernel(parts_ref, state_ref, gain_ref, next_ref, normed_ref):
    total = parts_ref[0].astype(jnp.float32)
    for d in range(1, parts_ref.shape[0]):
        total = total + parts_ref[d].astype(jnp.float32)
    state = (state_ref[...].astype(jnp.float32) + total).astype(jnp.bfloat16)
    next_ref[...] = state
    gain = gain_ref[...].astype(jnp.float32)
    normed_ref[...] = normed_rows(state.astype(jnp.float32), gain).astype(jnp.bfloat16)


def last_kernel(parts_ref, *refs):
    state_refs, out_ref = refs[:-1], refs[-1]
    total = parts_ref[0].astype(jnp.float32)
    for d in range(1, parts_ref.shape[0]):
        total = total + parts_ref[d].astype(jnp.float32)
    for index, state_ref in enumerate(state_refs):
        out_ref[index] = state_ref[...]
    out_ref[len(state_refs)] = (state_refs[-1][...].astype(jnp.float32) + total).astype(jnp.bfloat16)


def last(parts, states):
    return pl.pallas_call(
        last_kernel,
        out_shape=jax.ShapeDtypeStruct((len(states) + 1, *states[0].shape), jnp.bfloat16),
        in_specs=[whole()] * (1 + len(states)),
        out_specs=whole(),
        compiler_params=pltpu.CompilerParams(vmem_limit_bytes=VMEM_LIMIT),
        name="last",
    )(parts, *states)


def settle(parts, state, gain):
    shape = jax.ShapeDtypeStruct(state.shape, jnp.bfloat16)
    return pl.pallas_call(
        settle_kernel,
        out_shape=(shape, shape),
        in_specs=[whole()] * 3,
        out_specs=(whole(), whole()),
        compiler_params=pltpu.CompilerParams(vmem_limit_bytes=VMEM_LIMIT),
        name="settle",
    )(parts, state, gain)


def on_device(
    prompt_states,
    decode_states,
    norm_gain,
    w_query,
    w_keyvalue,
    w_output,
    cache_pages,
    page_table,
    cache_len,
    dest_rank,
    dest_page,
):
    rank = lax.axis_index("tensor")
    section = lax.axis_index("section")
    count = lax.axis_size("tensor")
    pool = cache_pages[0]
    page_size, kv_width = pool.shape[1:]
    own_table = page_table[0]
    lengths = cache_len[0]
    each, width = decode_states.shape[1:]
    tokens = prompt_states.shape[1]
    q_cols = w_query.shape[1]
    kv_heads = kv_width // (2 * HD)
    shared = count // kv_heads if count > kv_heads else 1
    gain = norm_gain[None, :]

    if w_keyvalue.shape[1] < 2 * HD:
        other = swap_xor(w_keyvalue, 1)
        is_key = rank % 2 == 0
        w_pair = jnp.concatenate(
            [jnp.where(is_key, w_keyvalue, other), jnp.where(is_key, other, w_keyvalue)], axis=1
        )
    else:
        w_pair = w_keyvalue

    sections = lax.axis_size("section")
    onward = [(s, (s + 1) % sections) for s in range(sections)]
    grid = count == 8 and sections == 2

    numbers = jnp.arange(count * each, dtype=jnp.int32)
    per_request = own_table.shape[1]
    used = (lengths + page_size - 1) // page_size
    by_owner = used.reshape(count, each)
    first = (jnp.cumsum(by_owner, axis=1) - by_owner).reshape(-1)
    most = jnp.max(jnp.sum(by_owner, axis=1, keepdims=True), keepdims=True)
    for axis in ("section", "groups"):
        for bit in range(lax.axis_size(axis).bit_length() - 1):
            pairs = [(s, s ^ (1 << bit)) for s in range(lax.axis_size(axis))]
            most = jnp.maximum(most, lax.ppermute(most, axis, pairs))
    own_used = lax.dynamic_slice_in_dim(used, rank * each, each)
    heads = tuple(target // shared for target in range(count))
    info = jnp.zeros((page_size, 2 * HD), jnp.bfloat16)
    info = info.at[0, :each].set(own_table[:, 0].astype(jnp.bfloat16))
    ready = make_parcels(own_table, own_used, info, pool, heads, 2 * HD)

    table, halves = grid_arrivals() if grid else ring_arrivals(count)
    parts = 1 if grid else 2
    rows = tokens // parts
    carried = np.array([index for index, piece in enumerate(halves) if piece == parts - 1])
    senders = jnp.asarray(table, jnp.int32)[rank]
    starts = senders * tokens + jnp.asarray(halves, jnp.int32) * rows
    orders = []
    for owners in (senders[carried], rank ^ jnp.arange(count, dtype=jnp.int32)):
        rows_of = jnp.repeat(owners * each, each) + numbers % each
        orders.append((numbers[:, None] == rows_of[None, :]).astype(jnp.bfloat16))
    times = lengths[None, :] + jnp.arange(STEPS, dtype=jnp.int32)[:, None]
    cosine, sine = rope_tables(times.reshape(-1))
    cosine = cosine.reshape(STEPS, count * each, HD)
    sine = sine.reshape(STEPS, count * each, HD)
    sizes = [size for size in MORE if size < pool.shape[0] - SURE] + [pool.shape[0] - SURE]
    wanted = most[0, 0] - SURE
    choice = jnp.sum((wanted > jnp.array(sizes[:-1], jnp.int32)).astype(jnp.int32))
    ready = (ready, w_pair, choice, starts, orders, cosine, sine)
    pieces = prepare(prompt_states[0], decode_states[0], gain, parts)
    known, pending, finish, ready = (along_grid if grid else along_ring)(pieces, ready)
    ready, *_, choice, starts, orders, cosine, sine = ready

    sure, more = ready

    def exchange(pages):
        return lax.all_to_all(
            pages.reshape(count, -1, 2 * HD), "tensor", split_axis=0, concat_axis=0, tiled=True
        )

    extra = more.shape[1]

    def branch(size):
        def run(more):
            if size == 0:
                return jnp.zeros((count, extra * page_size, 2 * HD), jnp.bfloat16)
            pages = exchange(more[:, :size])
            return jnp.pad(pages, ((0, 0), (0, (extra - size) * page_size), (0, 0)))

        return run

    more = lax.switch(choice, [branch(size) for size in sizes], more)
    known, pending, more = lax.optimization_barrier((known, pending, more))
    sure, _ = lax.optimization_barrier((sure, more))
    sure = exchange(sure)

    prompt_kv = []
    blocks = []
    if grid:
        rest, w_other = finish(pending)
        own, other, states = project(known[0] + rest, [w_pair, w_other], starts, 0, rows, each)
        prompt_kv = [own, cross(other)]
        blocks = [states, cross(states)]
    else:
        skipped = 0
        for group in known:
            values, states = project(group, [w_pair], starts, skipped, rows, each)
            prompt_kv.append(values)
            blocks.append(states)
            skipped += len(group)
    arrived = tuple(lax.ppermute(part, "section", onward) for part in prompt_kv)
    anchor = (section + 1) % sections
    targets = lax.dynamic_index_in_dim(dest_rank, anchor, 0, keepdims=False)
    landing = lax.dynamic_index_in_dim(dest_page, anchor, 0, keepdims=False)[:, 0]
    prompts = (targets, landing, starts // PLEN, starts % PLEN, *arrived)
    held = (w_query, w_pair, w_output, sure, more)

    blocks, cosine, sine, state = lax.optimization_barrier((blocks, cosine, sine, decode_states[0]))
    outputs = []
    earlier = []
    for iteration in range(STEPS):
        chosen = orders[min(iteration, 1)]
        parts, fresh, *fetched = step(
            blocks, chosen, lengths, used, first, cosine, sine, earlier, held, each, prompts
        )
        if iteration == 0:
            held, prompts = fetched, ()
        earlier.append(fresh)
        parts = lax.all_to_all(parts, "tensor", split_axis=0, concat_axis=0, tiled=True)
        if iteration + 1 < STEPS:
            state, normed = settle(parts, state, gain)
            outputs.append(state)
            blocks = [normed] + [swap_xor(normed, bits) for bits in range(1, count)]
    return last(parts, outputs)[:, None]


def solution(mesh):
    in_specs = (
        P(("groups", "section"), "tensor", None),
        P(("groups", "section"), "tensor", None),
        P(),
        P(None, "tensor"),
        P(None, "tensor"),
        P("tensor", None),
        P(("groups", "section"), "tensor", None, None),
        P(("groups", "section"), "tensor", None),
        P(("groups", "section"), None),
        P("groups", None),
        P("groups", None, None),
    )
    out_specs = P(None, ("groups", "section"), "tensor", None)
    return jax.shard_map(
        on_device, mesh=mesh, in_specs=in_specs, out_specs=out_specs, check_vma=False
    )
```

```python
import functools

import jax
import jax.numpy as jnp
import numpy as np
from jax import lax
from jax.experimental import pallas as pl
from jax.experimental.pallas import tpu as pltpu
from jax.sharding import PartitionSpec as P

HD = 128
PLEN = 128
STEPS = 4
EPS = 1e-05
ROPE_BASE = 500000.0
LANES = 8
CHUNKS = 8
PAGE = 16
SURE = 24
MORE = (0, 4, 8, 10, 12, 14, 16, 18, 20, 22, 24, 26, 28, 30, 32, 36)
VMEM_LIMIT = 10 * 1024 * 1024


def ring_shift(value, steps):
    count = lax.axis_size("tensor")
    return lax.ppermute(value, "tensor", [(s, (s + steps) % count) for s in range(count)])


def swap_xor(value, mask):
    count = lax.axis_size("tensor")
    return lax.ppermute(value, "tensor", [(s, s ^ mask) for s in range(count)])


def ring_arrivals(count):
    table, halves = [np.arange(count)] * 2, [0, 1]
    for hop in range(1, count // 2 + 1):
        for piece in range(2):
            for way in range(2):
                if hop < count // 2 or piece == way:
                    table.append((np.arange(count) - (1 - 2 * way) * hop) % count)
                    halves.append(piece)
    return np.stack(table, axis=1), halves


def along_ring(pieces, ready):
    count = lax.axis_size("tensor")
    blocks = list(pieces)
    going = [[rows, rows] for rows in pieces]
    for hop in range(1, count // 2 + 1):
        for piece in range(2):
            for way in range(2):
                if hop < count // 2 or piece == way:
                    going[piece][way] = ring_shift(going[piece][way], 1 - 2 * way)
                    blocks.append(going[piece][way])
        if hop == 1:
            going, ready = lax.optimization_barrier((going, ready))
    return [blocks[at : at + 8] for at in range(0, len(blocks), 8)], (), lambda pending: [], ready


def cross(value):
    return lax.ppermute(value, "tensor", [(r, r ^ 1) for r in range(8)])


def grid_arrivals():
    table = []
    for across in (0, 1):
        for origin in ((0, 1, 2, 3), (1, 0, 3, 2), (2, 2, 1, 1), (3, 3, 0, 0)):
            table.append(np.array([(2 * origin[r // 2] + r % 2) ^ across for r in range(8)]))
    return np.stack(table, axis=1), [0] * 8


def along_grid(pieces, ready):
    z = lax.axis_index("tensor") // 2

    def shift(rows, steps, starts):
        pairs = [(2 * s + c, 2 * (s + steps) + c) for s in starts for c in range(2)]
        return lax.ppermute(rows, "tensor", pairs)

    def pick(*rows):
        return jnp.where(z == 0, rows[0], jnp.where(z == 1, rows[1], jnp.where(z == 2, rows[2], rows[3])))

    (rows,) = pieces
    up, down = shift(rows, 1, (0, 1, 2)), shift(rows, -1, (1, 2, 3))
    up, down, parcels, weight = lax.optimization_barrier((up, down, *ready[:2]))
    section = lax.axis_index("section")
    half = weight.shape[0] // 2
    brought = cross(lax.dynamic_slice_in_dim(weight, section * half, half))
    ready = (parcels, *ready[2:])
    up2, down2 = shift(up, 1, (1, 2)), shift(down, -1, (1, 2))
    up2, down2, ready = lax.optimization_barrier((up2, down2, ready))
    outward = jnp.where(z == 1, down2, up2)
    ends = lax.ppermute(outward, "tensor", [(2, 0), (3, 1), (4, 6), (5, 7)])

    def finish(pending):
        up, down, up2, down2, ends, brought = pending
        given = lax.ppermute(brought, "section", [(0, 1), (1, 0)])
        other = jnp.where(
            section == 0,
            jnp.concatenate([brought, given], axis=0),
            jnp.concatenate([given, brought], axis=0),
        )
        second = pick(down, up, down, up)
        third = pick(down2, down, up, up2)
        fourth = pick(ends, down2, up2, ends)
        return [second, third, fourth], other

    return [[rows]], (up, down, up2, down2, ends, brought), finish, ready


def rope_tables(positions, lib=jnp):
    half_dim = HD // 2
    freqs = ROPE_BASE ** (-(lib.arange(half_dim, dtype=lib.float32) * 2.0 / HD))
    angles = positions.astype(lib.float32)[:, None] * freqs[None, :].astype(lib.float32)
    cosine = lib.cos(angles)
    sine = lib.sin(angles)
    return (
        lib.concatenate([cosine, cosine], axis=1).astype(lib.float32),
        lib.concatenate([-sine, sine], axis=1).astype(lib.float32),
    )


def whole():
    return pl.BlockSpec(memory_space=pltpu.VMEM)


def normed_rows(values, gain):
    square = jnp.mean(values * values, axis=-1, keepdims=True)
    return values * lax.rsqrt(square + EPS) * gain


def prepare_kernel(prompt_ref, state_ref, gain_ref, *out_refs):
    tokens, width = prompt_ref.shape
    rows = tokens // len(out_refs)
    gain = gain_ref[...].astype(jnp.float32)
    for index, out_ref in enumerate(out_refs):
        part = prompt_ref[index * rows : (index + 1) * rows, :].astype(jnp.float32)
        out_ref[:rows, :] = normed_rows(part, gain).astype(jnp.bfloat16)
    states = normed_rows(state_ref[...].astype(jnp.float32), gain)
    filling = jnp.zeros((out_refs[-1].shape[0] - rows - states.shape[0], width), jnp.float32)
    out_refs[-1][rows:, :] = jnp.concatenate([states, filling], axis=0).astype(jnp.bfloat16)


def prepare(prompts, states, gain, pieces):
    tokens, width = prompts.shape
    rows = [tokens // pieces] * pieces
    rows[-1] += -(-states.shape[0] // LANES) * LANES
    return pl.pallas_call(
        prepare_kernel,
        out_shape=tuple(jax.ShapeDtypeStruct((count, width), jnp.bfloat16) for count in rows),
        in_specs=[whole()] * 3,
        out_specs=tuple(whole() for _ in rows),
        compiler_params=pltpu.CompilerParams(vmem_limit_bytes=VMEM_LIMIT),
        name="prepare",
    )(prompts, states, gain)


def project_kernel(rows, each, skipped, heads, *refs):
    blocks, refs = refs[: -2 * heads - 4], refs[-2 * heads - 4 :]
    starts_ref, cos_ref, sin_ref = refs[:3]
    weight_refs, out_refs, states_ref = refs[3 : 3 + heads], refs[3 + heads : -1], refs[-1]
    depth = weight_refs[0].shape[0] // CHUNKS
    totals = [jnp.zeros(out_ref.shape, jnp.float32) for out_ref in out_refs]
    for c in range(CHUNKS):
        part = slice(c * depth, (c + 1) * depth)
        x = jnp.concatenate([block[:rows, part] for block in blocks], axis=0)
        for head in range(heads):
            totals[head] += jnp.dot(
                x, weight_refs[head][part, :], preferred_element_type=jnp.float32
            )
    for total, out_ref in zip(totals, out_refs):
        out_ref[:, HD:] = total[:, HD:].astype(jnp.bfloat16)
        for index in range(len(blocks)):
            begin = starts_ref[skipped + index] % PLEN
            span = pl.ds(pl.multiple_of(begin, rows), rows)
            here = slice(index * rows, (index + 1) * rows)
            keys = turn(total[here, :HD], cos_ref[span, :], sin_ref[span, :])
            out_ref[here, :HD] = keys.astype(jnp.bfloat16)
    found = 0
    for block in blocks:
        if block.shape[0] > rows:
            states_ref[found] = block[rows:, :].astype(jnp.float32)[:each, :].astype(jnp.bfloat16)
            found += 1


def project(blocks, weights, starts, skipped, rows, each):
    width = weights[0].shape[0]
    cosine, sine = rope_tables(np.arange(PLEN), np)
    carrying = sum(block.shape[0] > rows for block in blocks)
    values = jax.ShapeDtypeStruct((len(blocks) * rows, 2 * HD), jnp.bfloat16)
    out_shape = [values] * len(weights)
    out_shape.append(jax.ShapeDtypeStruct((carrying, each, width), jnp.bfloat16))
    smem = pl.BlockSpec(memory_space=pltpu.SMEM)
    return pl.pallas_call(
        functools.partial(project_kernel, rows, each, skipped, len(weights)),
        out_shape=tuple(out_shape),
        in_specs=[whole()] * len(blocks) + [smem] + [whole()] * (2 + len(weights)),
        out_specs=tuple(whole() for _ in out_shape),
        compiler_params=pltpu.CompilerParams(vmem_limit_bytes=VMEM_LIMIT),
        cost_estimate=pl.CostEstimate(
            flops=2 * len(blocks) * rows * weights[0].size * len(weights),
            bytes_accessed=2 * weights[0].size * len(weights),
            transcendentals=0,
        ),
        name="project",
    )(*blocks, starts, cosine, sine, *weights)


def parcels_kernel(heads, table_ref, used_ref, info_ref, pool_ref, sure_ref, more_ref, held, load_sem, store_sem):
    width = sure_ref.shape[-1]
    each, per_request = table_ref.shape
    pages = each * per_request
    sure = sure_ref.shape[1] - 1
    stores = []
    for target in range(len(heads)):
        copy = pltpu.make_async_copy(info_ref, sure_ref.at[target, 0], store_sem.at[0, target])
        copy.start()
        stores.append(copy)
    front = jnp.int32(0)
    back = used_ref[0]
    for r in range(1, each):
        back = back + used_ref[r]
    loads = []
    for r in range(each):
        used = used_ref[r]
        for p in range(per_request):
            spot = jnp.where(p < used, front + p, back + p - used)
            copy = pltpu.make_async_copy(
                pool_ref.at[table_ref[r, p]], held.at[spot], load_sem.at[r * per_request + p]
            )
            copy.start()
            loads.append(copy)
        front = front + used
        back = back + per_request - used
    for copy in loads:
        copy.wait()
    for target, head in enumerate(heads):
        columns = pl.ds(head * width, width)
        for bank, source, goal in (
            (1, held.at[pl.ds(0, sure), :, columns], sure_ref.at[target, pl.ds(1, sure)]),
            (2, held.at[pl.ds(sure, pages - sure), :, columns], more_ref.at[target]),
        ):
            copy = pltpu.make_async_copy(source, goal, store_sem.at[bank, target])
            copy.start()
            stores.append(copy)
    for copy in stores:
        copy.wait()


def make_parcels(table, used, info, pool, heads, width):
    pages, rows, _ = pool.shape
    hbm = pl.BlockSpec(memory_space=pltpu.HBM)
    smem = pl.BlockSpec(memory_space=pltpu.SMEM)
    return pl.pallas_call(
        functools.partial(parcels_kernel, heads),
        out_shape=(
            pltpu.HBM((len(heads), SURE + 1, rows, width), jnp.bfloat16),
            pltpu.HBM((len(heads), pages - SURE, rows, width), jnp.bfloat16),
        ),
        in_specs=[smem, smem, whole(), hbm],
        out_specs=(hbm, hbm),
        scratch_shapes=[
            pltpu.VMEM(pool.shape, jnp.bfloat16),
            pltpu.SemaphoreType.DMA((pages,)),
            pltpu.SemaphoreType.DMA((3, len(heads))),
        ],
        compiler_params=pltpu.CompilerParams(vmem_limit_bytes=VMEM_LIMIT),
        name="parcels",
    )(table, used, info, pltpu.with_memory_space_constraint(pool, pltpu.HBM))


def turn(values, cosine, sine):
    return values * cosine + pltpu.roll(values, HD // 2, 1) * sine


def step_kernel(blocks, iteration, groups, each, *refs):
    x_refs = refs[:blocks]
    order_ref, lens_ref, used_ref, first_ref, cos_ref, sin_ref = refs[blocks : blocks + 6]
    new_refs = refs[blocks + 6 : blocks + 6 + iteration]
    refs = refs[blocks + 6 + iteration :]
    if iteration == 0:
        target_ref, landing_ref, prompt_ref, offset_ref = refs[:4]
        arrived_refs = refs[4 : 4 + groups]
        refs = refs[4 + groups :]
        wq_in, wkv_in, wo_in, sure_in, more_in, out_ref, fresh_ref, wq, wkv, wo, cache = refs[:11]
        x_rows, q_s, score_s, mix_s, new_s, sems, patch_sems = refs[11:]
    else:
        wq, wkv, wo, cache = refs[:4]
        out_ref, fresh_ref, x_rows, q_s, score_s, mix_s, new_s = refs[4:]
    width, q_cols = wq.shape
    owners = cache.shape[0]
    count = owners * each
    span = (cache.shape[1] // PAGE - 1) // each * PAGE
    heads = q_cols // HD
    depth = width // CHUNKS

    waits = {}
    if iteration == 0:
        for c in range(CHUNKS):
            part = pl.ds(c * depth, depth)
            waits[c] = [
                pltpu.make_async_copy(wq_in.at[part, :], wq.at[part, :], sems.at[0, c]),
                pltpu.make_async_copy(wkv_in.at[part, :], wkv.at[part, :], sems.at[1, c]),
            ]
            waits["out", c] = [pltpu.make_async_copy(wo_in.at[:, part], wo.at[:, part], sems.at[2, c])]
        sure = sure_in.shape[1]
        waits["cache"] = [
            pltpu.make_async_copy(sure_in, cache.at[:, pl.ds(0, sure), :], sems.at[3, 0]),
            pltpu.make_async_copy(
                more_in, cache.at[:, pl.ds(sure, more_in.shape[1]), :], sems.at[3, 1]
            ),
        ]
        for name in [0, 1, 2, 3, "cache", 4, 5, 6, 7]:
            for copy in waits[name]:
                copy.start()

    def wait(name):
        for copy in waits.get(name, ()):
            copy.wait()

    def receivers():
        lines = [
            cache[owner, :PAGE, :HD].astype(jnp.float32)[:1, :] for owner in range(owners)
        ]
        firsts = jnp.concatenate(lines, axis=0)
        owner = lax.broadcasted_iota(jnp.int32, firsts.shape, 0)
        slot = lax.broadcasted_iota(jnp.int32, firsts.shape, 1)
        numbers = (owner * each + slot).astype(jnp.float32)
        found = []
        for k in range(target_ref.shape[0]):
            here = (owner == target_ref[k]) & (slot < each)
            here = here & (firsts == landing_ref[k].astype(jnp.float32))
            found.append(jnp.sum(jnp.where(here, numbers, 0.0)).astype(jnp.int32))
        return found

    def window(r, size, page=0):
        return pl.ds(pl.multiple_of((first_ref[r] + page + 1) * PAGE, PAGE), size)

    def patch(requests, action):
        pieces = offset_ref.shape[0]
        rows = sum(ref.shape[0] for ref in arrived_refs) // pieces
        piece = 0
        for ref in arrived_refs:
            for local in range(ref.shape[0] // rows):
                request = jnp.int32(0)
                for k, number in enumerate(requests):
                    request = jnp.where(prompt_ref[piece] == k, number, request)
                for p in range(rows // PAGE):
                    page = offset_ref[piece] // PAGE + p

                    @pl.when(page < used_ref[request])
                    def _():
                        copy = pltpu.make_async_copy(
                            ref.at[pl.ds(local * rows + p * PAGE, PAGE), :],
                            cache.at[request // each, window(request, PAGE, page), :],
                            patch_sems.at[piece, p],
                        )
                        action(copy)

                piece += 1

    place = 0
    for ref in x_refs:
        for rows in [ref[...]] if ref.ndim == 2 else [ref[k] for k in range(ref.shape[0])]:
            x_rows[place : place + each, :] = rows.astype(jnp.float32)
            place += each
    order = order_ref[...]

    query = jnp.zeros((count, q_cols), jnp.float32)
    keyvalue = jnp.zeros((count, 2 * HD), jnp.float32)
    for c in range(CHUNKS):
        part = slice(c * depth, (c + 1) * depth)
        x = jnp.dot(
            order, x_rows[:, part].astype(jnp.bfloat16), preferred_element_type=jnp.float32
        ).astype(jnp.bfloat16)
        wait(c)
        if iteration == 0:
            for copy in waits["out", c]:
                copy.start()
        query += jnp.dot(x, wq[part, :], preferred_element_type=jnp.float32)
        keyvalue += jnp.dot(x, wkv[part, :], preferred_element_type=jnp.float32)
        if iteration == 0 and c == CHUNKS - 2:
            wait("cache")
            requests = receivers()
            patch(requests, lambda copy: copy.start())

    cosine = cos_ref[iteration]
    sine = sin_ref[iteration]
    key = turn(keyvalue[:, :HD], cosine, sine).astype(jnp.bfloat16)
    value = keyvalue[:, HD:].astype(jnp.bfloat16)
    fresh_ref[:, :HD] = key
    fresh_ref[:, HD:] = value
    news = [(ref[:, :HD], ref[:, HD:]) for ref in new_refs] + [(key, value)]
    for j in range(LANES):
        lane = pl.ds(j, count, LANES)
        if j < heads:
            turned = turn(query[:, j * HD : (j + 1) * HD], cosine, sine).astype(jnp.bfloat16)
            q_s[lane, :] = turned.astype(jnp.float32)
        else:
            q_s[lane, :] = jnp.zeros((count, HD), jnp.float32)
        for t, pair in enumerate(news):
            for half in range(2):
                new_s[t, half, lane, :] = pair[half].astype(jnp.float32)

    if iteration == 0:
        patch(requests, lambda copy: copy.wait())
    scale = HD**-0.5
    column = lax.broadcasted_iota(jnp.int32, (LANES, span), 1)
    for r in range(count):
        rows = slice(r * LANES, (r + 1) * LANES)
        found = lax.dot_general(
            q_s[rows, :].astype(jnp.bfloat16),
            cache[r // each, window(r, span), :HD],
            (((1,), (1,)), ((), ())),
            preferred_element_type=jnp.float32,
        )
        score_s[rows, :] = jnp.where(column < lens_ref[r], found * scale, -1e30)

    scores = score_s[...]
    queries = q_s[...]
    fresh_scores = [
        jnp.sum(queries * new_s[t, 0], axis=-1, keepdims=True) * scale for t in range(iteration + 1)
    ]
    top = jnp.max(scores, axis=-1, keepdims=True)
    for s in fresh_scores:
        top = jnp.maximum(top, s)
    weights = jnp.exp(scores - top)
    fresh_weights = [jnp.exp(s - top) for s in fresh_scores]
    total = jnp.sum(weights, axis=-1, keepdims=True)
    for w in fresh_weights:
        total = total + w
    score_s[...] = weights / total
    row = lax.broadcasted_iota(jnp.int32, (span, HD), 0)
    for r in range(count):
        rows = slice(r * LANES, (r + 1) * LANES)
        mix_s[rows, :] = jnp.dot(
            score_s[rows, :].astype(jnp.bfloat16),
            jnp.where(
                row < lens_ref[r],
                cache[r // each, window(r, span), HD:],
                jnp.zeros((), jnp.bfloat16),
            ),
            preferred_element_type=jnp.float32,
        )
    mixed = mix_s[...]
    for t in range(iteration + 1):
        weight = (fresh_weights[t] / total).astype(jnp.bfloat16).astype(jnp.float32)
        mixed = mixed + weight * new_s[t, 1]
    mix_s[...] = mixed
    columns = jnp.concatenate(
        [mix_s[pl.ds(j, count, LANES), :].astype(jnp.bfloat16) for j in range(heads)], axis=1
    )
    for c in range(CHUNKS):
        part = slice(c * depth, (c + 1) * depth)
        wait(("out", c))
        product = jnp.dot(columns, wo[:, part], preferred_element_type=jnp.float32)
        for d in range(owners):
            out_ref[d, :, part] = product[d * each : (d + 1) * each, :].astype(jnp.bfloat16)


def step(x_blocks, order, lengths, used, first, cosine, sine, earlier, held, each, prompts=()):
    width, q_cols = held[0].shape
    owners = held[3].shape[0]
    count = owners * each
    cached = sum(a.shape[1] for a in held[3:])
    span = (cached // PAGE - 1) // each * PAGE
    iteration = len(earlier)
    blocks = len(x_blocks)
    groups = max(len(prompts) - 4, 0)
    smem = pl.BlockSpec(memory_space=pltpu.SMEM)
    hbm = pl.BlockSpec(memory_space=pltpu.HBM)
    anywhere = pl.BlockSpec(memory_space=pl.ANY)
    out_shape = [
        jax.ShapeDtypeStruct((owners, each, width), jnp.bfloat16),
        jax.ShapeDtypeStruct((count, 2 * HD), jnp.bfloat16),
    ]
    in_specs = [whole()] * (blocks + 1) + [smem] * 3 + [whole()] * (2 + iteration)
    scratch = [
        pltpu.VMEM((count, width), jnp.float32),
        pltpu.VMEM((count * LANES, HD), jnp.float32),
        pltpu.VMEM((count * LANES, span), jnp.float32),
        pltpu.VMEM((count * LANES, HD), jnp.float32),
        pltpu.VMEM((iteration + 1, 2, count * LANES, HD), jnp.float32),
    ]
    if iteration == 0:
        in_specs += [smem] * 4 + [whole()] * groups + [hbm] * 3 + [anywhere] * 2
        out_shape += [pltpu.VMEM(a.shape, a.dtype) for a in held[:3]]
        out_shape.append(pltpu.VMEM((owners, cached, 2 * HD), jnp.bfloat16))
        held = [pltpu.with_memory_space_constraint(a, pltpu.HBM) for a in held[:3]] + list(held[3:])
        pieces = prompts[3].shape[0]
        pages = sum(a.shape[0] for a in prompts[4:]) // pieces // PAGE
        scratch.append(pltpu.SemaphoreType.DMA((4, CHUNKS)))
        scratch.append(pltpu.SemaphoreType.DMA((pieces, pages)))
    else:
        in_specs += [whole()] * 4
    return pl.pallas_call(
        functools.partial(step_kernel, blocks, iteration, groups, each),
        out_shape=tuple(out_shape),
        in_specs=in_specs,
        out_specs=tuple(whole() for _ in out_shape),
        scratch_shapes=scratch,
        compiler_params=pltpu.CompilerParams(vmem_limit_bytes=VMEM_LIMIT),
        cost_estimate=pl.CostEstimate(
            flops=2 * count * width * (2 * q_cols + 2 * HD),
            bytes_accessed=2 * sum(a.size for a in held),
            transcendentals=count * LANES * span,
        ),
        name="decode_step",
    )(*x_blocks, order, lengths, used, first, cosine, sine, *earlier, *prompts, *held)


def settle_kernel(parts_ref, state_ref, gain_ref, next_ref, normed_ref):
    total = parts_ref[0].astype(jnp.float32)
    for d in range(1, parts_ref.shape[0]):
        total = total + parts_ref[d].astype(jnp.float32)
    state = (state_ref[...].astype(jnp.float32) + total).astype(jnp.bfloat16)
    next_ref[...] = state
    gain = gain_ref[...].astype(jnp.float32)
    normed_ref[...] = normed_rows(state.astype(jnp.float32), gain).astype(jnp.bfloat16)


def last_kernel(parts_ref, *refs):
    state_refs, out_ref = refs[:-1], refs[-1]
    total = parts_ref[0].astype(jnp.float32)
    for d in range(1, parts_ref.shape[0]):
        total = total + parts_ref[d].astype(jnp.float32)
    for index, state_ref in enumerate(state_refs):
        out_ref[index] = state_ref[...]
    out_ref[len(state_refs)] = (state_refs[-1][...].astype(jnp.float32) + total).astype(jnp.bfloat16)


def last(parts, states):
    return pl.pallas_call(
        last_kernel,
        out_shape=jax.ShapeDtypeStruct((len(states) + 1, *states[0].shape), jnp.bfloat16),
        in_specs=[whole()] * (1 + len(states)),
        out_specs=whole(),
        compiler_params=pltpu.CompilerParams(vmem_limit_bytes=VMEM_LIMIT),
        name="last",
    )(parts, *states)


def settle(parts, state, gain):
    shape = jax.ShapeDtypeStruct(state.shape, jnp.bfloat16)
    return pl.pallas_call(
        settle_kernel,
        out_shape=(shape, shape),
        in_specs=[whole()] * 3,
        out_specs=(whole(), whole()),
        compiler_params=pltpu.CompilerParams(vmem_limit_bytes=VMEM_LIMIT),
        name="settle",
    )(parts, state, gain)


def on_device(
    prompt_states,
    decode_states,
    norm_gain,
    w_query,
    w_keyvalue,
    w_output,
    cache_pages,
    page_table,
    cache_len,
    dest_rank,
    dest_page,
):
    rank = lax.axis_index("tensor")
    section = lax.axis_index("section")
    count = lax.axis_size("tensor")
    pool = cache_pages[0]
    page_size, kv_width = pool.shape[1:]
    own_table = page_table[0]
    lengths = cache_len[0]
    each, width = decode_states.shape[1:]
    tokens = prompt_states.shape[1]
    q_cols = w_query.shape[1]
    kv_heads = kv_width // (2 * HD)
    shared = count // kv_heads if count > kv_heads else 1
    gain = norm_gain[None, :]

    if w_keyvalue.shape[1] < 2 * HD:
        other = swap_xor(w_keyvalue, 1)
        is_key = rank % 2 == 0
        w_pair = jnp.concatenate(
            [jnp.where(is_key, w_keyvalue, other), jnp.where(is_key, other, w_keyvalue)], axis=1
        )
    else:
        w_pair = w_keyvalue

    sections = lax.axis_size("section")
    onward = [(s, (s + 1) % sections) for s in range(sections)]
    grid = count == 8 and sections == 2

    numbers = jnp.arange(count * each, dtype=jnp.int32)
    per_request = own_table.shape[1]
    used = (lengths + page_size - 1) // page_size
    by_owner = used.reshape(count, each)
    first = (jnp.cumsum(by_owner, axis=1) - by_owner).reshape(-1)
    most = jnp.max(jnp.sum(by_owner, axis=1, keepdims=True), keepdims=True)
    for axis in ("section", "groups"):
        for bit in range(lax.axis_size(axis).bit_length() - 1):
            pairs = [(s, s ^ (1 << bit)) for s in range(lax.axis_size(axis))]
            most = jnp.maximum(most, lax.ppermute(most, axis, pairs))
    own_used = lax.dynamic_slice_in_dim(used, rank * each, each)
    heads = tuple(target // shared for target in range(count))
    info = jnp.zeros((page_size, 2 * HD), jnp.bfloat16)
    info = info.at[0, :each].set(own_table[:, 0].astype(jnp.bfloat16))
    ready = make_parcels(own_table, own_used, info, pool, heads, 2 * HD)

    table, halves = grid_arrivals() if grid else ring_arrivals(count)
    parts = 1 if grid else 2
    rows = tokens // parts
    carried = np.array([index for index, piece in enumerate(halves) if piece == parts - 1])
    senders = jnp.asarray(table, jnp.int32)[rank]
    starts = senders * tokens + jnp.asarray(halves, jnp.int32) * rows
    orders = []
    masks = jnp.array([0, 1, 6, 4, 2, 7, 5, 3] if grid else range(count), jnp.int32)
    for owners in (senders[carried], rank ^ masks):
        rows_of = jnp.repeat(owners * each, each) + numbers % each
        orders.append((numbers[:, None] == rows_of[None, :]).astype(jnp.bfloat16))
    times = lengths[None, :] + jnp.arange(STEPS, dtype=jnp.int32)[:, None]
    cosine, sine = rope_tables(times.reshape(-1))
    cosine = cosine.reshape(STEPS, count * each, HD)
    sine = sine.reshape(STEPS, count * each, HD)
    sizes = [size for size in MORE if size < pool.shape[0] - SURE] + [pool.shape[0] - SURE]
    wanted = most[0, 0] - SURE
    choice = jnp.sum((wanted > jnp.array(sizes[:-1], jnp.int32)).astype(jnp.int32))
    ready = (ready, w_pair, choice, starts, orders, cosine, sine)
    pieces = prepare(prompt_states[0], decode_states[0], gain, parts)
    known, pending, finish, ready = (along_grid if grid else along_ring)(pieces, ready)
    ready, *_, choice, starts, orders, cosine, sine = ready

    sure, more = ready

    def exchange(pages):
        return lax.all_to_all(
            pages.reshape(count, -1, 2 * HD), "tensor", split_axis=0, concat_axis=0, tiled=True
        )

    extra = more.shape[1]

    def branch(size):
        def run(more):
            if size == 0:
                return jnp.zeros((count, extra * page_size, 2 * HD), jnp.bfloat16)
            pages = exchange(more[:, :size])
            return jnp.pad(pages, ((0, 0), (0, (extra - size) * page_size), (0, 0)))

        return run

    more = lax.switch(choice, [branch(size) for size in sizes], more)
    known, pending, more = lax.optimization_barrier((known, pending, more))
    sure, _ = lax.optimization_barrier((sure, more))
    sure = exchange(sure)

    prompt_kv = []
    blocks = []
    if grid:
        rest, w_other = finish(pending)
        own, other, states = project(known[0] + rest, [w_pair, w_other], starts, 0, rows, each)
        prompt_kv = [own, cross(other)]
        blocks = [states, cross(states)]
    else:
        skipped = 0
        for group in known:
            values, states = project(group, [w_pair], starts, skipped, rows, each)
            prompt_kv.append(values)
            blocks.append(states)
            skipped += len(group)
    arrived = tuple(lax.ppermute(part, "section", onward) for part in prompt_kv)
    anchor = (section + 1) % sections
    targets = lax.dynamic_index_in_dim(dest_rank, anchor, 0, keepdims=False)
    landing = lax.dynamic_index_in_dim(dest_page, anchor, 0, keepdims=False)[:, 0]
    prompts = (targets, landing, starts // PLEN, starts % PLEN, *arrived)
    held = (w_query, w_pair, w_output, sure, more)

    blocks, cosine, sine, state = lax.optimization_barrier((blocks, cosine, sine, decode_states[0]))
    outputs = []
    earlier = []
    for iteration in range(STEPS):
        chosen = orders[min(iteration, 1)]
        parts, fresh, *fetched = step(
            blocks, chosen, lengths, used, first, cosine, sine, earlier, held, each, prompts
        )
        if iteration == 0:
            held, prompts = fetched, ()
        earlier.append(fresh)
        parts = lax.all_to_all(parts, "tensor", split_axis=0, concat_axis=0, tiled=True)
        if iteration + 1 < STEPS:
            state, normed = settle(parts, state, gain)
            outputs.append(state)
            if grid:
                along = [swap_xor(normed, bits) for bits in (6, 4, 2)]
                blocks = [normed, cross(normed), *along, *(cross(block) for block in along)]
            else:
                blocks = [normed] + [swap_xor(normed, bits) for bits in range(1, count)]
    return last(parts, outputs)[:, None]


def solution(mesh):
    in_specs = (
        P(("groups", "section"), "tensor", None),
        P(("groups", "section"), "tensor", None),
        P(),
        P(None, "tensor"),
        P(None, "tensor"),
        P("tensor", None),
        P(("groups", "section"), "tensor", None, None),
        P(("groups", "section"), "tensor", None),
        P(("groups", "section"), None),
        P("groups", None),
        P("groups", None, None),
    )
    out_specs = P(None, ("groups", "section"), "tensor", None)
    return jax.shard_map(
        on_device, mesh=mesh, in_specs=in_specs, out_specs=out_specs, check_vma=False
    )
```

```python
import functools

import jax
import jax.numpy as jnp
import numpy as np
from jax import lax
from jax.experimental import pallas as pl
from jax.experimental.pallas import tpu as pltpu
from jax.sharding import PartitionSpec as P

HD = 128
PLEN = 128
STEPS = 4
EPS = 1e-05
ROPE_BASE = 500000.0
LANES = 8
CHUNKS = 8
PAGE = 16
SURE = 16
MORE = (0, 8, 12, 16, 18, 20, 22, 24, 26, 28, 30, 32, 34, 36, 40)
VMEM_LIMIT = 10 * 1024 * 1024


def ring_shift(value, steps):
    count = lax.axis_size("tensor")
    return lax.ppermute(value, "tensor", [(s, (s + steps) % count) for s in range(count)])


def swap_xor(value, mask):
    count = lax.axis_size("tensor")
    return lax.ppermute(value, "tensor", [(s, s ^ mask) for s in range(count)])


def ring_arrivals(count):
    table, halves = [np.arange(count)] * 2, [0, 1]
    for hop in range(1, count // 2 + 1):
        for piece in range(2):
            for way in range(2):
                if hop < count // 2 or piece == way:
                    table.append((np.arange(count) - (1 - 2 * way) * hop) % count)
                    halves.append(piece)
    return np.stack(table, axis=1), halves


def along_ring(pieces, ready):
    count = lax.axis_size("tensor")
    blocks = list(pieces)
    going = [[rows, rows] for rows in pieces]
    for hop in range(1, count // 2 + 1):
        for piece in range(2):
            for way in range(2):
                if hop < count // 2 or piece == way:
                    going[piece][way] = ring_shift(going[piece][way], 1 - 2 * way)
                    blocks.append(going[piece][way])
        if hop == 1:
            going, ready = lax.optimization_barrier((going, ready))
    return [blocks[at : at + 8] for at in range(0, len(blocks), 8)], (), lambda pending: [], ready


def cross(value):
    return lax.ppermute(value, "tensor", [(r, r ^ 1) for r in range(8)])


def grid_arrivals():
    table = []
    for across in (0, 1):
        for origin in ((0, 1, 2, 3), (1, 0, 3, 2), (2, 2, 1, 1), (3, 3, 0, 0)):
            table.append(np.array([(2 * origin[r // 2] + r % 2) ^ across for r in range(8)]))
    return np.stack(table, axis=1), [0] * 8


def along_grid(pieces, ready):
    z = lax.axis_index("tensor") // 2

    def shift(rows, steps, starts):
        pairs = [(2 * s + c, 2 * (s + steps) + c) for s in starts for c in range(2)]
        return lax.ppermute(rows, "tensor", pairs)

    def pick(*rows):
        return jnp.where(z == 0, rows[0], jnp.where(z == 1, rows[1], jnp.where(z == 2, rows[2], rows[3])))

    (rows,) = pieces
    up, down = shift(rows, 1, (0, 1, 2)), shift(rows, -1, (1, 2, 3))
    up, down, parcels, weight = lax.optimization_barrier((up, down, *ready[:2]))
    section = lax.axis_index("section")
    half = weight.shape[0] // 2
    brought = cross(lax.dynamic_slice_in_dim(weight, section * half, half))
    ready = (parcels, *ready[2:])
    up2, down2 = shift(up, 1, (1, 2)), shift(down, -1, (1, 2))
    up2, down2, ready = lax.optimization_barrier((up2, down2, ready))
    outward = jnp.where(z == 1, down2, up2)
    ends = lax.ppermute(outward, "tensor", [(2, 0), (3, 1), (4, 6), (5, 7)])

    def finish(pending):
        up, down, up2, down2, ends, brought = pending
        given = lax.ppermute(brought, "section", [(0, 1), (1, 0)])
        begins = jnp.stack([section * half, (1 - section) * half]).astype(jnp.int32)
        second = pick(down, up, down, up)
        third = pick(down2, down, up, up2)
        fourth = pick(ends, down2, up2, ends)
        return [second, third, fourth], (brought, given), begins

    return [[rows]], (up, down, up2, down2, ends, brought), finish, ready


def rope_tables(positions, lib=jnp):
    half_dim = HD // 2
    freqs = ROPE_BASE ** (-(lib.arange(half_dim, dtype=lib.float32) * 2.0 / HD))
    angles = positions.astype(lib.float32)[:, None] * freqs[None, :].astype(lib.float32)
    cosine = lib.cos(angles)
    sine = lib.sin(angles)
    return (
        lib.concatenate([cosine, cosine], axis=1).astype(lib.float32),
        lib.concatenate([-sine, sine], axis=1).astype(lib.float32),
    )


def whole():
    return pl.BlockSpec(memory_space=pltpu.VMEM)


def normed_rows(values, gain):
    square = jnp.mean(values * values, axis=-1, keepdims=True)
    return values * lax.rsqrt(square + EPS) * gain


def prepare_kernel(prompt_ref, state_ref, gain_ref, *out_refs):
    tokens, width = prompt_ref.shape
    rows = tokens // len(out_refs)
    gain = gain_ref[...].astype(jnp.float32)
    for index, out_ref in enumerate(out_refs):
        part = prompt_ref[index * rows : (index + 1) * rows, :].astype(jnp.float32)
        out_ref[:rows, :] = normed_rows(part, gain).astype(jnp.bfloat16)
    states = normed_rows(state_ref[...].astype(jnp.float32), gain)
    filling = jnp.zeros((out_refs[-1].shape[0] - rows - states.shape[0], width), jnp.float32)
    out_refs[-1][rows:, :] = jnp.concatenate([states, filling], axis=0).astype(jnp.bfloat16)


def prepare(prompts, states, gain, pieces):
    tokens, width = prompts.shape
    rows = [tokens // pieces] * pieces
    rows[-1] += -(-states.shape[0] // LANES) * LANES
    return pl.pallas_call(
        prepare_kernel,
        out_shape=tuple(jax.ShapeDtypeStruct((count, width), jnp.bfloat16) for count in rows),
        in_specs=[whole()] * 3,
        out_specs=tuple(whole() for _ in rows),
        compiler_params=pltpu.CompilerParams(vmem_limit_bytes=VMEM_LIMIT),
        name="prepare",
    )(prompts, states, gain)


def prepare_blocks_kernel(prompt_in, state_in, gain_ref, out_ref, states, prompts, sems):
    each = state_in.shape[0]
    copies = [
        pltpu.make_async_copy(prompt_in, prompts, sems.at[0]),
        pltpu.make_async_copy(state_in, states, sems.at[1]),
    ]
    for copy in copies:
        copy.start()
    gain = gain_ref[...].astype(jnp.float32)
    lanes = gain.shape[1]
    for copy, rows_ref, first in zip(copies, (prompts, states), (0, prompts.shape[0] // each)):
        copy.wait()
        values = rows_ref[...].astype(jnp.float32)
        factor = lax.rsqrt(jnp.mean(values * values, axis=-1, keepdims=True) + EPS)
        for c in range(gain.shape[0]):
            part = slice(c * lanes, (c + 1) * lanes)
            normed = rows_ref[:, part].astype(jnp.float32) * factor * gain[c : c + 1, :]
            for block in range(rows_ref.shape[0] // each):
                rows = normed[block * each : (block + 1) * each, :]
                out_ref[first + block, :, part] = rows.astype(jnp.bfloat16)


def prepare_blocks(prompts, states, gain):
    tokens, width = prompts.shape
    each = states.shape[0]
    hbm = pl.BlockSpec(memory_space=pltpu.HBM)
    return pl.pallas_call(
        prepare_blocks_kernel,
        out_shape=(
            jax.ShapeDtypeStruct((tokens // each + 1, each, width), jnp.bfloat16),
            jax.ShapeDtypeStruct(states.shape, jnp.bfloat16),
        ),
        in_specs=[hbm, hbm, whole()],
        out_specs=(whole(), whole()),
        scratch_shapes=[
            pltpu.VMEM(prompts.shape, jnp.bfloat16),
            pltpu.SemaphoreType.DMA((2,)),
        ],
        compiler_params=pltpu.CompilerParams(vmem_limit_bytes=VMEM_LIMIT),
        name="prepare",
    )(
        pltpu.with_memory_space_constraint(prompts, pltpu.HBM),
        pltpu.with_memory_space_constraint(states, pltpu.HBM),
        gain,
    )


def project_kernel(rows, each, skipped, halves, *refs):
    heads = 2 if halves else 1
    blocks, refs = refs[: -7 - halves - heads], refs[-7 - halves - heads :]
    starts_ref, begins_ref, cos_ref, sin_ref = refs[:4]
    weight_ref, part_refs = refs[4], refs[5 : 5 + halves]
    out_refs = refs[5 + halves : 5 + halves + heads]
    states_ref, staged = refs[-2:]
    depth = weight_ref.shape[0] // CHUNKS

    def stage(span):
        for index, block in enumerate(blocks):
            begin = index * rows
            if block.ndim == 2:
                staged[begin : begin + rows, :] = block[:rows, span].astype(jnp.float32)
                continue
            for piece in range(rows // each):
                here = slice(begin + piece * each, begin + (piece + 1) * each)
                staged[here, :] = block[piece, :, span].astype(jnp.float32)
        return staged[...].astype(jnp.bfloat16)

    totals = [jnp.zeros(out_ref.shape, jnp.float32) for out_ref in out_refs]
    for c in range(CHUNKS):
        span = slice(c * depth, (c + 1) * depth)
        totals[0] += jnp.dot(stage(span), weight_ref[span, :], preferred_element_type=jnp.float32)
    for index, part_ref in enumerate(part_refs):
        for c in range(part_ref.shape[0] // depth):
            begin = pl.multiple_of(begins_ref[index] + c * depth, depth)
            totals[1] += jnp.dot(
                stage(pl.ds(begin, depth)),
                part_ref[c * depth : (c + 1) * depth, :],
                preferred_element_type=jnp.float32,
            )
    for total, out_ref in zip(totals, out_refs):
        out_ref[:, HD:] = total[:, HD:].astype(jnp.bfloat16)
        for index in range(len(blocks)):
            begin = starts_ref[skipped + index] % PLEN
            span = pl.ds(pl.multiple_of(begin, rows), rows)
            here = slice(index * rows, (index + 1) * rows)
            keys = turn(total[here, :HD], cos_ref[span, :], sin_ref[span, :])
            out_ref[here, :HD] = keys.astype(jnp.bfloat16)
    found = 0
    for block in blocks:
        if block.ndim == 3:
            states_ref[found] = block[rows // each]
            found += 1
        elif block.shape[0] > rows:
            states_ref[found] = block[rows:, :].astype(jnp.float32)[:each, :].astype(jnp.bfloat16)
            found += 1


def project(blocks, weight, starts, skipped, rows, each, parts=(), begins=None):
    width = weight.shape[0]
    cosine, sine = rope_tables(np.arange(PLEN), np)
    carrying = sum(block.ndim == 3 or block.shape[0] > rows for block in blocks)
    heads = 2 if parts else 1
    values = jax.ShapeDtypeStruct((len(blocks) * rows, 2 * HD), jnp.bfloat16)
    out_shape = [values] * heads
    out_shape.append(jax.ShapeDtypeStruct((carrying, each, width), jnp.bfloat16))
    smem = pl.BlockSpec(memory_space=pltpu.SMEM)
    begins = jnp.zeros((2,), jnp.int32) if begins is None else begins
    return pl.pallas_call(
        functools.partial(project_kernel, rows, each, skipped, len(parts)),
        out_shape=tuple(out_shape),
        in_specs=[whole()] * len(blocks) + [smem] * 2 + [whole()] * (3 + len(parts)),
        out_specs=tuple(whole() for _ in out_shape),
        scratch_shapes=[pltpu.VMEM((len(blocks) * rows, width // CHUNKS), jnp.float32)],
        compiler_params=pltpu.CompilerParams(vmem_limit_bytes=2 * VMEM_LIMIT),
        cost_estimate=pl.CostEstimate(
            flops=2 * len(blocks) * rows * weight.size * heads,
            bytes_accessed=2 * weight.size * heads,
            transcendentals=0,
        ),
        name="project",
    )(*blocks, starts, begins, cosine, sine, weight, *parts)


def parcels_kernel(heads, table_ref, used_ref, info_ref, pool_ref, sure_ref, more_ref, held, load_sem, store_sem):
    width = sure_ref.shape[-1]
    each, per_request = table_ref.shape
    pages = each * per_request
    sure = sure_ref.shape[1] - 1
    stores = []
    for target in range(len(heads)):
        copy = pltpu.make_async_copy(info_ref, sure_ref.at[target, 0], store_sem.at[0, target])
        copy.start()
        stores.append(copy)
    front = jnp.int32(0)
    back = used_ref[0]
    for r in range(1, each):
        back = back + used_ref[r]
    loads = []
    for r in range(each):
        used = used_ref[r]
        for p in range(per_request):
            spot = jnp.where(p < used, front + p, back + p - used)
            copy = pltpu.make_async_copy(
                pool_ref.at[table_ref[r, p]], held.at[spot], load_sem.at[r * per_request + p]
            )
            copy.start()
            loads.append(copy)
        front = front + used
        back = back + per_request - used
    for copy in loads:
        copy.wait()
    for target, head in enumerate(heads):
        columns = pl.ds(head * width, width)
        for bank, source, goal in (
            (1, held.at[pl.ds(0, sure), :, columns], sure_ref.at[target, pl.ds(1, sure)]),
            (2, held.at[pl.ds(sure, pages - sure), :, columns], more_ref.at[target]),
        ):
            copy = pltpu.make_async_copy(source, goal, store_sem.at[bank, target])
            copy.start()
            stores.append(copy)
    for copy in stores:
        copy.wait()


def make_parcels(table, used, info, pool, heads, width):
    pages, rows, _ = pool.shape
    hbm = pl.BlockSpec(memory_space=pltpu.HBM)
    smem = pl.BlockSpec(memory_space=pltpu.SMEM)
    return pl.pallas_call(
        functools.partial(parcels_kernel, heads),
        out_shape=(
            pltpu.HBM((len(heads), SURE + 1, rows, width), jnp.bfloat16),
            pltpu.HBM((len(heads), pages - SURE, rows, width), jnp.bfloat16),
        ),
        in_specs=[smem, smem, whole(), hbm],
        out_specs=(hbm, hbm),
        scratch_shapes=[
            pltpu.VMEM(pool.shape, jnp.bfloat16),
            pltpu.SemaphoreType.DMA((pages,)),
            pltpu.SemaphoreType.DMA((3, len(heads))),
        ],
        compiler_params=pltpu.CompilerParams(vmem_limit_bytes=VMEM_LIMIT),
        name="parcels",
    )(table, used, info, pltpu.with_memory_space_constraint(pool, pltpu.HBM))


def turn(values, cosine, sine):
    return values * cosine + pltpu.roll(values, HD // 2, 1) * sine


def step_kernel(blocks, iteration, groups, each, *refs):
    x_refs = refs[:blocks]
    order_ref, lens_ref, used_ref, first_ref, cos_ref, sin_ref = refs[blocks : blocks + 6]
    new_refs = refs[blocks + 6 : blocks + 6 + iteration]
    refs = refs[blocks + 6 + iteration :]
    if iteration == 0:
        target_ref, landing_ref, prompt_ref, offset_ref = refs[:4]
        arrived_refs = refs[4 : 4 + groups]
        refs = refs[4 + groups :]
        wq_in, wkv_in, wo_in, sure_in, more_in, out_ref, fresh_ref, wq, wkv, wo, cache = refs[:11]
        x_rows, q_s, score_s, mix_s, new_s, sems, patch_sems = refs[11:]
    else:
        wq, wkv, wo, cache = refs[:4]
        out_ref, fresh_ref, x_rows, q_s, score_s, mix_s, new_s = refs[4:]
    width, q_cols = wq.shape
    owners = cache.shape[0]
    count = owners * each
    span = (cache.shape[1] // PAGE - 1) // each * PAGE
    heads = q_cols // HD
    depth = width // CHUNKS

    waits = {}
    if iteration == 0:
        for c in range(CHUNKS):
            part = pl.ds(c * depth, depth)
            waits[c] = [
                pltpu.make_async_copy(wq_in.at[part, :], wq.at[part, :], sems.at[0, c]),
                pltpu.make_async_copy(wkv_in.at[part, :], wkv.at[part, :], sems.at[1, c]),
            ]
            waits["out", c] = [pltpu.make_async_copy(wo_in.at[:, part], wo.at[:, part], sems.at[2, c])]
        sure = sure_in.shape[1]
        waits["cache"] = [
            pltpu.make_async_copy(sure_in, cache.at[:, pl.ds(0, sure), :], sems.at[3, 0]),
            pltpu.make_async_copy(
                more_in, cache.at[:, pl.ds(sure, more_in.shape[1]), :], sems.at[3, 1]
            ),
        ]
        for name in [0, 1, 2, 3, "cache", 4, 5, 6, 7]:
            for copy in waits[name]:
                copy.start()

    def wait(name):
        for copy in waits.get(name, ()):
            copy.wait()

    def receivers():
        lines = [
            cache[owner, :PAGE, :HD].astype(jnp.float32)[:1, :] for owner in range(owners)
        ]
        firsts = jnp.concatenate(lines, axis=0)
        owner = lax.broadcasted_iota(jnp.int32, firsts.shape, 0)
        slot = lax.broadcasted_iota(jnp.int32, firsts.shape, 1)
        numbers = (owner * each + slot).astype(jnp.float32)
        found = []
        for k in range(target_ref.shape[0]):
            here = (owner == target_ref[k]) & (slot < each)
            here = here & (firsts == landing_ref[k].astype(jnp.float32))
            found.append(jnp.sum(jnp.where(here, numbers, 0.0)).astype(jnp.int32))
        return found

    def window(r, size, page=0):
        return pl.ds(pl.multiple_of((first_ref[r] + page + 1) * PAGE, PAGE), size)

    def patch(requests, action):
        pieces = offset_ref.shape[0]
        rows = sum(ref.shape[0] for ref in arrived_refs) // pieces
        piece = 0
        for ref in arrived_refs:
            for local in range(ref.shape[0] // rows):
                request = jnp.int32(0)
                for k, number in enumerate(requests):
                    request = jnp.where(prompt_ref[piece] == k, number, request)
                for p in range(rows // PAGE):
                    page = offset_ref[piece] // PAGE + p

                    @pl.when(page < used_ref[request])
                    def _():
                        copy = pltpu.make_async_copy(
                            ref.at[pl.ds(local * rows + p * PAGE, PAGE), :],
                            cache.at[request // each, window(request, PAGE, page), :],
                            patch_sems.at[piece, p],
                        )
                        action(copy)

                piece += 1

    place = 0
    for ref in x_refs:
        for rows in [ref[...]] if ref.ndim == 2 else [ref[k] for k in range(ref.shape[0])]:
            x_rows[place : place + each, :] = rows.astype(jnp.float32)
            place += each
    order = order_ref[...]

    query = jnp.zeros((count, q_cols), jnp.float32)
    keyvalue = jnp.zeros((count, 2 * HD), jnp.float32)
    for c in range(CHUNKS):
        part = slice(c * depth, (c + 1) * depth)
        x = jnp.dot(
            order, x_rows[:, part].astype(jnp.bfloat16), preferred_element_type=jnp.float32
        ).astype(jnp.bfloat16)
        wait(c)
        if iteration == 0:
            for copy in waits["out", c]:
                copy.start()
        query += jnp.dot(x, wq[part, :], preferred_element_type=jnp.float32)
        keyvalue += jnp.dot(x, wkv[part, :], preferred_element_type=jnp.float32)
        if iteration == 0 and c == CHUNKS - 2:
            wait("cache")
            requests = receivers()
            patch(requests, lambda copy: copy.start())

    cosine = cos_ref[iteration]
    sine = sin_ref[iteration]
    key = turn(keyvalue[:, :HD], cosine, sine).astype(jnp.bfloat16)
    value = keyvalue[:, HD:].astype(jnp.bfloat16)
    fresh_ref[:, :HD] = key
    fresh_ref[:, HD:] = value
    news = [(ref[:, :HD], ref[:, HD:]) for ref in new_refs] + [(key, value)]
    for j in range(LANES):
        lane = pl.ds(j, count, LANES)
        if j < heads:
            turned = turn(query[:, j * HD : (j + 1) * HD], cosine, sine).astype(jnp.bfloat16)
            q_s[lane, :] = turned.astype(jnp.float32)
        else:
            q_s[lane, :] = jnp.zeros((count, HD), jnp.float32)
        for t, pair in enumerate(news):
            for half in range(2):
                new_s[t, half, lane, :] = pair[half].astype(jnp.float32)

    if iteration == 0:
        patch(requests, lambda copy: copy.wait())
    scale = HD**-0.5
    column = lax.broadcasted_iota(jnp.int32, (LANES, span), 1)
    for r in range(count):
        rows = slice(r * LANES, (r + 1) * LANES)
        found = lax.dot_general(
            q_s[rows, :].astype(jnp.bfloat16),
            cache[r // each, window(r, span), :HD],
            (((1,), (1,)), ((), ())),
            preferred_element_type=jnp.float32,
        )
        score_s[rows, :] = jnp.where(column < lens_ref[r], found * scale, -1e30)

    scores = score_s[...]
    queries = q_s[...]
    fresh_scores = [
        jnp.sum(queries * new_s[t, 0], axis=-1, keepdims=True) * scale for t in range(iteration + 1)
    ]
    top = jnp.max(scores, axis=-1, keepdims=True)
    for s in fresh_scores:
        top = jnp.maximum(top, s)
    weights = jnp.exp(scores - top)
    fresh_weights = [jnp.exp(s - top) for s in fresh_scores]
    total = jnp.sum(weights, axis=-1, keepdims=True)
    for w in fresh_weights:
        total = total + w
    score_s[...] = weights / total
    row = lax.broadcasted_iota(jnp.int32, (span, HD), 0)
    for r in range(count):
        rows = slice(r * LANES, (r + 1) * LANES)
        mix_s[rows, :] = jnp.dot(
            score_s[rows, :].astype(jnp.bfloat16),
            jnp.where(
                row < lens_ref[r],
                cache[r // each, window(r, span), HD:],
                jnp.zeros((), jnp.bfloat16),
            ),
            preferred_element_type=jnp.float32,
        )
    mixed = mix_s[...]
    for t in range(iteration + 1):
        weight = (fresh_weights[t] / total).astype(jnp.bfloat16).astype(jnp.float32)
        mixed = mixed + weight * new_s[t, 1]
    mix_s[...] = mixed
    columns = jnp.concatenate(
        [mix_s[pl.ds(j, count, LANES), :].astype(jnp.bfloat16) for j in range(heads)], axis=1
    )
    for c in range(CHUNKS):
        part = slice(c * depth, (c + 1) * depth)
        wait(("out", c))
        product = jnp.dot(columns, wo[:, part], preferred_element_type=jnp.float32)
        for d in range(owners):
            out_ref[d, :, part] = product[d * each : (d + 1) * each, :].astype(jnp.bfloat16)


def step(x_blocks, order, lengths, used, first, cosine, sine, earlier, held, each, prompts=()):
    width, q_cols = held[0].shape
    owners = held[3].shape[0]
    count = owners * each
    cached = sum(a.shape[1] for a in held[3:])
    span = (cached // PAGE - 1) // each * PAGE
    iteration = len(earlier)
    blocks = len(x_blocks)
    groups = max(len(prompts) - 4, 0)
    smem = pl.BlockSpec(memory_space=pltpu.SMEM)
    hbm = pl.BlockSpec(memory_space=pltpu.HBM)
    anywhere = pl.BlockSpec(memory_space=pl.ANY)
    out_shape = [
        jax.ShapeDtypeStruct((owners, each, width), jnp.bfloat16),
        jax.ShapeDtypeStruct((count, 2 * HD), jnp.bfloat16),
    ]
    in_specs = [whole()] * (blocks + 1) + [smem] * 3 + [whole()] * (2 + iteration)
    scratch = [
        pltpu.VMEM((count, width), jnp.float32),
        pltpu.VMEM((count * LANES, HD), jnp.float32),
        pltpu.VMEM((count * LANES, span), jnp.float32),
        pltpu.VMEM((count * LANES, HD), jnp.float32),
        pltpu.VMEM((iteration + 1, 2, count * LANES, HD), jnp.float32),
    ]
    if iteration == 0:
        in_specs += [smem] * 4 + [whole()] * groups + [hbm] * 3 + [anywhere] * 2
        out_shape += [pltpu.VMEM(a.shape, a.dtype) for a in held[:3]]
        out_shape.append(pltpu.VMEM((owners, cached, 2 * HD), jnp.bfloat16))
        held = [pltpu.with_memory_space_constraint(a, pltpu.HBM) for a in held[:3]] + list(held[3:])
        pieces = prompts[3].shape[0]
        pages = sum(a.shape[0] for a in prompts[4:]) // pieces // PAGE
        scratch.append(pltpu.SemaphoreType.DMA((4, CHUNKS)))
        scratch.append(pltpu.SemaphoreType.DMA((pieces, pages)))
    else:
        in_specs += [whole()] * 4
    return pl.pallas_call(
        functools.partial(step_kernel, blocks, iteration, groups, each),
        out_shape=tuple(out_shape),
        in_specs=in_specs,
        out_specs=tuple(whole() for _ in out_shape),
        scratch_shapes=scratch,
        compiler_params=pltpu.CompilerParams(vmem_limit_bytes=VMEM_LIMIT),
        cost_estimate=pl.CostEstimate(
            flops=2 * count * width * (2 * q_cols + 2 * HD),
            bytes_accessed=2 * sum(a.size for a in held),
            transcendentals=count * LANES * span,
        ),
        name="decode_step",
    )(*x_blocks, order, lengths, used, first, cosine, sine, *earlier, *prompts, *held)


def settle_kernel(parts_ref, state_ref, gain_ref, next_ref, normed_ref):
    total = parts_ref[0].astype(jnp.float32)
    for d in range(1, parts_ref.shape[0]):
        total = total + parts_ref[d].astype(jnp.float32)
    state = (state_ref[...].astype(jnp.float32) + total).astype(jnp.bfloat16)
    next_ref[...] = state
    gain = gain_ref[...].astype(jnp.float32)
    normed_ref[...] = normed_rows(state.astype(jnp.float32), gain).astype(jnp.bfloat16)


def last_kernel(parts_ref, *refs):
    state_refs, out_ref = refs[:-1], refs[-1]
    total = parts_ref[0].astype(jnp.float32)
    for d in range(1, parts_ref.shape[0]):
        total = total + parts_ref[d].astype(jnp.float32)
    for index, state_ref in enumerate(state_refs):
        out_ref[index] = state_ref[...]
    out_ref[len(state_refs)] = (state_refs[-1][...].astype(jnp.float32) + total).astype(jnp.bfloat16)


def last(parts, states):
    return pl.pallas_call(
        last_kernel,
        out_shape=jax.ShapeDtypeStruct((len(states) + 1, *states[0].shape), jnp.bfloat16),
        in_specs=[whole()] * (1 + len(states)),
        out_specs=whole(),
        compiler_params=pltpu.CompilerParams(vmem_limit_bytes=VMEM_LIMIT),
        name="last",
    )(parts, *states)


def settle(parts, state, gain):
    shape = jax.ShapeDtypeStruct(state.shape, jnp.bfloat16)
    return pl.pallas_call(
        settle_kernel,
        out_shape=(shape, shape),
        in_specs=[whole()] * 3,
        out_specs=(whole(), whole()),
        compiler_params=pltpu.CompilerParams(vmem_limit_bytes=VMEM_LIMIT),
        name="settle",
    )(parts, state, gain)


def on_device(
    prompt_states,
    decode_states,
    norm_gain,
    w_query,
    w_keyvalue,
    w_output,
    cache_pages,
    page_table,
    cache_len,
    dest_rank,
    dest_page,
):
    rank = lax.axis_index("tensor")
    section = lax.axis_index("section")
    count = lax.axis_size("tensor")
    pool = cache_pages[0]
    page_size, kv_width = pool.shape[1:]
    own_table = page_table[0]
    lengths = cache_len[0]
    each, width = decode_states.shape[1:]
    tokens = prompt_states.shape[1]
    q_cols = w_query.shape[1]
    kv_heads = kv_width // (2 * HD)
    shared = count // kv_heads if count > kv_heads else 1
    gain = norm_gain[None, :]

    if w_keyvalue.shape[1] < 2 * HD:
        other = swap_xor(w_keyvalue, 1)
        is_key = rank % 2 == 0
        w_pair = jnp.concatenate(
            [jnp.where(is_key, w_keyvalue, other), jnp.where(is_key, other, w_keyvalue)], axis=1
        )
    else:
        w_pair = w_keyvalue

    sections = lax.axis_size("section")
    onward = [(s, (s + 1) % sections) for s in range(sections)]
    grid = count == 8 and sections == 2

    numbers = jnp.arange(count * each, dtype=jnp.int32)
    per_request = own_table.shape[1]
    used = (lengths + page_size - 1) // page_size
    by_owner = used.reshape(count, each)
    first = (jnp.cumsum(by_owner, axis=1) - by_owner).reshape(-1)
    most = jnp.max(jnp.sum(by_owner, axis=1, keepdims=True), keepdims=True)
    for axis in ("section", "groups"):
        for bit in range(lax.axis_size(axis).bit_length() - 1):
            pairs = [(s, s ^ (1 << bit)) for s in range(lax.axis_size(axis))]
            most = jnp.maximum(most, lax.ppermute(most, axis, pairs))
    own_used = lax.dynamic_slice_in_dim(used, rank * each, each)
    heads = tuple(target // shared for target in range(count))
    info = jnp.zeros((page_size, 2 * HD), jnp.bfloat16)
    info = info.at[0, :each].set(own_table[:, 0].astype(jnp.bfloat16))
    ready = make_parcels(own_table, own_used, info, pool, heads, 2 * HD)

    table, halves = grid_arrivals() if grid else ring_arrivals(count)
    parts = 1 if grid else 2
    rows = tokens // parts
    carried = np.array([index for index, piece in enumerate(halves) if piece == parts - 1])
    senders = jnp.asarray(table, jnp.int32)[rank]
    starts = senders * tokens + jnp.asarray(halves, jnp.int32) * rows
    orders = []
    masks = jnp.array([0, 1, 6, 4, 2, 7, 5, 3] if grid else range(count), jnp.int32)
    for owners in (senders[carried], rank ^ masks):
        rows_of = jnp.repeat(owners * each, each) + numbers % each
        orders.append((numbers[:, None] == rows_of[None, :]).astype(jnp.bfloat16))
    times = lengths[None, :] + jnp.arange(STEPS, dtype=jnp.int32)[:, None]
    cosine, sine = rope_tables(times.reshape(-1))
    cosine = cosine.reshape(STEPS, count * each, HD)
    sine = sine.reshape(STEPS, count * each, HD)
    sizes = [size for size in MORE if size < pool.shape[0] - SURE] + [pool.shape[0] - SURE]
    wanted = most[0, 0] - SURE
    choice = jnp.sum((wanted > jnp.array(sizes[:-1], jnp.int32)).astype(jnp.int32))
    ready = (ready, w_pair, choice, starts, orders, cosine, sine)
    if grid:
        lines = norm_gain.reshape(-1, HD)
        *pieces, state = prepare_blocks(prompt_states[0], decode_states[0], lines)
    else:
        state = decode_states[0]
        pieces = prepare(prompt_states[0], decode_states[0], gain, parts)
    known, pending, finish, ready = (along_grid if grid else along_ring)(pieces, ready)
    ready, *_, choice, starts, orders, cosine, sine = ready

    sure, more = ready

    def exchange(pages):
        return lax.all_to_all(
            pages.reshape(count, -1, 2 * HD), "tensor", split_axis=0, concat_axis=0, tiled=True
        )

    extra = more.shape[1]

    def branch(size):
        def run(more):
            if size == 0:
                return jnp.zeros((count, extra * page_size, 2 * HD), jnp.bfloat16)
            pages = exchange(more[:, :size])
            return jnp.pad(pages, ((0, 0), (0, (extra - size) * page_size), (0, 0)))

        return run

    more = lax.switch(choice, [branch(size) for size in sizes], more)
    known, pending, more = lax.optimization_barrier((known, pending, more))
    sure, _ = lax.optimization_barrier((sure, more))
    sure = exchange(sure)

    prompt_kv = []
    blocks = []
    if grid:
        rest, halves_of_other, begins = finish(pending)
        own, other, states = project(
            known[0] + rest, w_pair, starts, 0, rows, each, halves_of_other, begins
        )
        prompt_kv = [own, cross(other)]
        blocks = [states, cross(states)]
    else:
        skipped = 0
        for group in known:
            values, states = project(group, w_pair, starts, skipped, rows, each)
            prompt_kv.append(values)
            blocks.append(states)
            skipped += len(group)
    arrived = tuple(lax.ppermute(part, "section", onward) for part in prompt_kv)
    anchor = (section + 1) % sections
    targets = lax.dynamic_index_in_dim(dest_rank, anchor, 0, keepdims=False)
    landing = lax.dynamic_index_in_dim(dest_page, anchor, 0, keepdims=False)[:, 0]
    prompts = (targets, landing, starts // PLEN, starts % PLEN, *arrived)
    held = (w_query, w_pair, w_output, sure, more)

    blocks, cosine, sine, state, gain = lax.optimization_barrier((blocks, cosine, sine, state, gain))
    outputs = []
    earlier = []
    for iteration in range(STEPS):
        chosen = orders[min(iteration, 1)]
        parts, fresh, *fetched = step(
            blocks, chosen, lengths, used, first, cosine, sine, earlier, held, each, prompts
        )
        if iteration == 0:
            held, prompts = fetched, ()
        earlier.append(fresh)
        parts = lax.all_to_all(parts, "tensor", split_axis=0, concat_axis=0, tiled=True)
        if iteration + 1 < STEPS:
            state, normed = settle(parts, state, gain)
            outputs.append(state)
            if grid:
                along = [swap_xor(normed, bits) for bits in (6, 4, 2)]
                blocks = [normed, cross(normed), *along, *(cross(block) for block in along)]
            else:
                blocks = [normed] + [swap_xor(normed, bits) for bits in range(1, count)]
    return last(parts, outputs)[:, None]


def solution(mesh):
    in_specs = (
        P(("groups", "section"), "tensor", None),
        P(("groups", "section"), "tensor", None),
        P(),
        P(None, "tensor"),
        P(None, "tensor"),
        P("tensor", None),
        P(("groups", "section"), "tensor", None, None),
        P(("groups", "section"), "tensor", None),
        P(("groups", "section"), None),
        P("groups", None),
        P("groups", None, None),
    )
    out_specs = P(None, ("groups", "section"), "tensor", None)
    return jax.shard_map(
        on_device, mesh=mesh, in_specs=in_specs, out_specs=out_specs, check_vma=False
    )
```

```python
import functools

import jax
import jax.numpy as jnp
import numpy as np
from jax import lax
from jax.experimental import pallas as pl
from jax.experimental.pallas import tpu as pltpu
from jax.sharding import PartitionSpec as P

HD = 128
PLEN = 128
STEPS = 4
EPS = 1e-05
ROPE_BASE = 500000.0
LANES = 8
CHUNKS = 8
PAGE = 16
SURE = 16
MORE = (0, 12, 16, 20, 22, 24, 26, 28, 30, 32, 36, 40)
VMEM_LIMIT = 10 * 1024 * 1024


def ring_shift(value, steps):
    count = lax.axis_size("tensor")
    return lax.ppermute(value, "tensor", [(s, (s + steps) % count) for s in range(count)])


def swap_xor(value, mask):
    count = lax.axis_size("tensor")
    return lax.ppermute(value, "tensor", [(s, s ^ mask) for s in range(count)])


def ring_arrivals(count):
    table, halves = [np.arange(count)] * 2, [0, 1]
    for hop in range(1, count // 2 + 1):
        for piece in range(2):
            for way in range(2):
                if hop < count // 2 or piece == way:
                    table.append((np.arange(count) - (1 - 2 * way) * hop) % count)
                    halves.append(piece)
    return np.stack(table, axis=1), halves


def along_ring(pieces, ready):
    count = lax.axis_size("tensor")
    blocks = list(pieces)
    going = [[rows, rows] for rows in pieces]
    for hop in range(1, count // 2 + 1):
        for piece in range(2):
            for way in range(2):
                if hop < count // 2 or piece == way:
                    going[piece][way] = ring_shift(going[piece][way], 1 - 2 * way)
                    blocks.append(going[piece][way])
        if hop == 1:
            going, ready = lax.optimization_barrier((going, ready))
    return [blocks[at : at + 8] for at in range(0, len(blocks), 8)], (), lambda pending: [], ready


def cross(value):
    return lax.ppermute(value, "tensor", [(r, r ^ 1) for r in range(8)])


def grid_arrivals():
    table = []
    for across in (0, 1):
        for origin in ((0, 1, 2, 3), (1, 0, 3, 2), (2, 2, 1, 1), (3, 3, 0, 0)):
            table.append(np.array([(2 * origin[r // 2] + r % 2) ^ across for r in range(8)]))
    return np.stack(table, axis=1), [0] * 8


def along_grid(pieces, ready):
    z = lax.axis_index("tensor") // 2

    def shift(rows, steps, starts):
        pairs = [(2 * s + c, 2 * (s + steps) + c) for s in starts for c in range(2)]
        return lax.ppermute(rows, "tensor", pairs)

    def pick(*rows):
        return jnp.where(z == 0, rows[0], jnp.where(z == 1, rows[1], jnp.where(z == 2, rows[2], rows[3])))

    (rows,) = pieces
    up, down = shift(rows, 1, (0, 1, 2)), shift(rows, -1, (1, 2, 3))
    up, down, parcels, weight = lax.optimization_barrier((up, down, *ready[:2]))
    section = lax.axis_index("section")
    half = weight.shape[0] // 2
    brought = cross(lax.dynamic_slice_in_dim(weight, section * half, half))
    ready = (parcels, *ready[2:])
    up2, down2 = shift(up, 1, (1, 2)), shift(down, -1, (1, 2))
    up2, down2, ready = lax.optimization_barrier((up2, down2, ready))
    outward = jnp.where(z == 1, down2, up2)
    ends = lax.ppermute(outward, "tensor", [(2, 0), (3, 1), (4, 6), (5, 7)])

    def finish(pending):
        up, down, up2, down2, ends, brought = pending
        given = lax.ppermute(brought, "section", [(0, 1), (1, 0)])
        begins = jnp.stack([section * half, (1 - section) * half]).astype(jnp.int32)
        second = pick(down, up, down, up)
        third = pick(down2, down, up, up2)
        fourth = pick(ends, down2, up2, ends)
        return [second, third, fourth], (brought, given), begins

    return [[rows]], (up, down, up2, down2, ends, brought), finish, ready


def rope_tables(positions, lib=jnp):
    half_dim = HD // 2
    freqs = ROPE_BASE ** (-(lib.arange(half_dim, dtype=lib.float32) * 2.0 / HD))
    angles = positions.astype(lib.float32)[:, None] * freqs[None, :].astype(lib.float32)
    cosine = lib.cos(angles)
    sine = lib.sin(angles)
    return (
        lib.concatenate([cosine, cosine], axis=1).astype(lib.float32),
        lib.concatenate([-sine, sine], axis=1).astype(lib.float32),
    )


def whole():
    return pl.BlockSpec(memory_space=pltpu.VMEM)


def normed_rows(values, gain):
    square = jnp.mean(values * values, axis=-1, keepdims=True)
    return values * lax.rsqrt(square + EPS) * gain


def prepare_kernel(prompt_ref, state_ref, gain_ref, *out_refs):
    tokens, width = prompt_ref.shape
    rows = tokens // len(out_refs)
    gain = gain_ref[...].astype(jnp.float32)
    for index, out_ref in enumerate(out_refs):
        part = prompt_ref[index * rows : (index + 1) * rows, :].astype(jnp.float32)
        out_ref[:rows, :] = normed_rows(part, gain).astype(jnp.bfloat16)
    states = normed_rows(state_ref[...].astype(jnp.float32), gain)
    filling = jnp.zeros((out_refs[-1].shape[0] - rows - states.shape[0], width), jnp.float32)
    out_refs[-1][rows:, :] = jnp.concatenate([states, filling], axis=0).astype(jnp.bfloat16)


def prepare(prompts, states, gain, pieces):
    tokens, width = prompts.shape
    rows = [tokens // pieces] * pieces
    rows[-1] += -(-states.shape[0] // LANES) * LANES
    return pl.pallas_call(
        prepare_kernel,
        out_shape=tuple(jax.ShapeDtypeStruct((count, width), jnp.bfloat16) for count in rows),
        in_specs=[whole()] * 3,
        out_specs=tuple(whole() for _ in rows),
        compiler_params=pltpu.CompilerParams(vmem_limit_bytes=VMEM_LIMIT),
        name="prepare",
    )(prompts, states, gain)


def prepare_blocks_kernel(prompt_in, state_in, gain_ref, out_ref, states, prompts, sems):
    each = state_in.shape[0]
    copies = [
        pltpu.make_async_copy(prompt_in, prompts, sems.at[0]),
        pltpu.make_async_copy(state_in, states, sems.at[1]),
    ]
    for copy in copies:
        copy.start()
    gain = gain_ref[...].astype(jnp.float32)
    lanes = gain.shape[1]
    for copy, rows_ref, first in zip(copies, (prompts, states), (0, prompts.shape[0] // each)):
        copy.wait()
        values = rows_ref[...].astype(jnp.float32)
        factor = lax.rsqrt(jnp.mean(values * values, axis=-1, keepdims=True) + EPS)
        for c in range(gain.shape[0]):
            part = slice(c * lanes, (c + 1) * lanes)
            normed = rows_ref[:, part].astype(jnp.float32) * factor * gain[c : c + 1, :]
            for block in range(rows_ref.shape[0] // each):
                rows = normed[block * each : (block + 1) * each, :]
                out_ref[first + block, :, part] = rows.astype(jnp.bfloat16)


def prepare_blocks(prompts, states, gain):
    tokens, width = prompts.shape
    each = states.shape[0]
    hbm = pl.BlockSpec(memory_space=pltpu.HBM)
    return pl.pallas_call(
        prepare_blocks_kernel,
        out_shape=(
            jax.ShapeDtypeStruct((tokens // each + 1, each, width), jnp.bfloat16),
            jax.ShapeDtypeStruct(states.shape, jnp.bfloat16),
        ),
        in_specs=[hbm, hbm, whole()],
        out_specs=(whole(), whole()),
        scratch_shapes=[
            pltpu.VMEM(prompts.shape, jnp.bfloat16),
            pltpu.SemaphoreType.DMA((2,)),
        ],
        compiler_params=pltpu.CompilerParams(vmem_limit_bytes=VMEM_LIMIT),
        name="prepare",
    )(
        pltpu.with_memory_space_constraint(prompts, pltpu.HBM),
        pltpu.with_memory_space_constraint(states, pltpu.HBM),
        gain,
    )


def project_kernel(rows, each, skipped, halves, *refs):
    heads = 2 if halves else 1
    used = 7 + halves + 2 * heads
    blocks, refs = refs[:-used], refs[-used:]
    starts_ref, begins_ref, cos_ref, sin_ref = refs[:4]
    weight_ref, part_refs = refs[4], refs[5 : 5 + halves]
    out_refs = refs[5 + halves : 5 + halves + heads]
    states_ref, staged = refs[-2 - heads : -heads]
    sum_refs = refs[-heads:]
    depth = weight_ref.shape[0] // CHUNKS

    def stage(span):
        for index, block in enumerate(blocks):
            begin = index * rows
            if block.ndim == 2:
                staged[begin : begin + rows, :] = block[:rows, span].astype(jnp.float32)
                continue
            for piece in range(rows // each):
                here = slice(begin + piece * each, begin + (piece + 1) * each)
                staged[here, :] = block[piece, :, span].astype(jnp.float32)
        return staged[...].astype(jnp.bfloat16)

    for sum_ref in sum_refs:
        sum_ref[...] = jnp.zeros_like(sum_ref)

    def add(sum_ref, weights, shift, count):
        @pl.loop(0, count)
        def _(c):
            x = stage(pl.ds(pl.multiple_of(shift + c * depth, depth), depth))
            here = pl.ds(pl.multiple_of(c * depth, depth), depth)
            sum_ref[...] += jnp.dot(x, weights[here, :], preferred_element_type=jnp.float32)

    add(sum_refs[0], weight_ref, 0, CHUNKS)
    for index, part_ref in enumerate(part_refs):
        add(sum_refs[1], part_ref, begins_ref[index], part_ref.shape[0] // depth)
    totals = [sum_ref[...] for sum_ref in sum_refs]
    for total, out_ref in zip(totals, out_refs):
        out_ref[:, HD:] = total[:, HD:].astype(jnp.bfloat16)
        for index in range(len(blocks)):
            begin = starts_ref[skipped + index] % PLEN
            span = pl.ds(pl.multiple_of(begin, rows), rows)
            here = slice(index * rows, (index + 1) * rows)
            keys = turn(total[here, :HD], cos_ref[span, :], sin_ref[span, :])
            out_ref[here, :HD] = keys.astype(jnp.bfloat16)
    found = 0
    for block in blocks:
        if block.ndim == 3:
            states_ref[found] = block[rows // each]
            found += 1
        elif block.shape[0] > rows:
            states_ref[found] = block[rows:, :].astype(jnp.float32)[:each, :].astype(jnp.bfloat16)
            found += 1


def project(blocks, weight, starts, skipped, rows, each, parts=(), begins=None):
    width = weight.shape[0]
    cosine, sine = rope_tables(np.arange(PLEN), np)
    carrying = sum(block.ndim == 3 or block.shape[0] > rows for block in blocks)
    heads = 2 if parts else 1
    values = jax.ShapeDtypeStruct((len(blocks) * rows, 2 * HD), jnp.bfloat16)
    out_shape = [values] * heads
    out_shape.append(jax.ShapeDtypeStruct((carrying, each, width), jnp.bfloat16))
    smem = pl.BlockSpec(memory_space=pltpu.SMEM)
    begins = jnp.zeros((2,), jnp.int32) if begins is None else begins
    return pl.pallas_call(
        functools.partial(project_kernel, rows, each, skipped, len(parts)),
        out_shape=tuple(out_shape),
        in_specs=[whole()] * len(blocks) + [smem] * 2 + [whole()] * (3 + len(parts)),
        out_specs=tuple(whole() for _ in out_shape),
        scratch_shapes=[
            pltpu.VMEM((len(blocks) * rows, width // CHUNKS), jnp.float32),
            *[pltpu.VMEM(values.shape, jnp.float32)] * heads,
        ],
        compiler_params=pltpu.CompilerParams(vmem_limit_bytes=2 * VMEM_LIMIT),
        cost_estimate=pl.CostEstimate(
            flops=2 * len(blocks) * rows * weight.size * heads,
            bytes_accessed=2 * weight.size * heads,
            transcendentals=0,
        ),
        name="project",
    )(*blocks, starts, begins, cosine, sine, weight, *parts)


def parcels_kernel(heads, table_ref, used_ref, info_ref, pool_ref, sure_ref, more_ref, held, load_sem, store_sem):
    width = sure_ref.shape[-1]
    each, per_request = table_ref.shape
    pages = each * per_request
    sure = sure_ref.shape[1] - 1
    stores = []
    for target in range(len(heads)):
        copy = pltpu.make_async_copy(info_ref, sure_ref.at[target, 0], store_sem.at[0, target])
        copy.start()
        stores.append(copy)
    front = jnp.int32(0)
    back = used_ref[0]
    for r in range(1, each):
        back = back + used_ref[r]
    loads = []
    for r in range(each):
        used = used_ref[r]
        for p in range(per_request):
            spot = jnp.where(p < used, front + p, back + p - used)
            copy = pltpu.make_async_copy(
                pool_ref.at[table_ref[r, p]], held.at[spot], load_sem.at[r * per_request + p]
            )
            copy.start()
            loads.append(copy)
        front = front + used
        back = back + per_request - used
    for copy in loads:
        copy.wait()
    for target, head in enumerate(heads):
        columns = pl.ds(head * width, width)
        for bank, source, goal in (
            (1, held.at[pl.ds(0, sure), :, columns], sure_ref.at[target, pl.ds(1, sure)]),
            (2, held.at[pl.ds(sure, pages - sure), :, columns], more_ref.at[target]),
        ):
            copy = pltpu.make_async_copy(source, goal, store_sem.at[bank, target])
            copy.start()
            stores.append(copy)
    for copy in stores:
        copy.wait()


def make_parcels(table, used, info, pool, heads, width):
    pages, rows, _ = pool.shape
    hbm = pl.BlockSpec(memory_space=pltpu.HBM)
    smem = pl.BlockSpec(memory_space=pltpu.SMEM)
    return pl.pallas_call(
        functools.partial(parcels_kernel, heads),
        out_shape=(
            pltpu.HBM((len(heads), SURE + 1, rows, width), jnp.bfloat16),
            pltpu.HBM((len(heads), pages - SURE, rows, width), jnp.bfloat16),
        ),
        in_specs=[smem, smem, whole(), hbm],
        out_specs=(hbm, hbm),
        scratch_shapes=[
            pltpu.VMEM(pool.shape, jnp.bfloat16),
            pltpu.SemaphoreType.DMA((pages,)),
            pltpu.SemaphoreType.DMA((3, len(heads))),
        ],
        compiler_params=pltpu.CompilerParams(vmem_limit_bytes=VMEM_LIMIT),
        name="parcels",
    )(table, used, info, pltpu.with_memory_space_constraint(pool, pltpu.HBM))


def turn(values, cosine, sine):
    return values * cosine + pltpu.roll(values, HD // 2, 1) * sine


def step_kernel(blocks, iteration, groups, each, *refs):
    x_refs = refs[:blocks]
    order_ref, lens_ref, used_ref, first_ref, cos_ref, sin_ref = refs[blocks : blocks + 6]
    new_refs = refs[blocks + 6 : blocks + 6 + iteration]
    refs = refs[blocks + 6 + iteration :]
    if iteration == 0:
        target_ref, landing_ref, prompt_ref, offset_ref = refs[:4]
        arrived_refs = refs[4 : 4 + groups]
        refs = refs[4 + groups :]
        wq_in, wkv_in, wo_in, sure_in, more_in, out_ref, fresh_ref, wq, wkv, wo, cache = refs[:11]
        x_rows, q_s, score_s, mix_s, new_s, sems, patch_sems = refs[11:]
    else:
        wq, wkv, wo, cache = refs[:4]
        out_ref, fresh_ref, x_rows, q_s, score_s, mix_s, new_s = refs[4:]
    width, q_cols = wq.shape
    owners = cache.shape[0]
    count = owners * each
    span = (cache.shape[1] // PAGE - 1) // each * PAGE
    heads = q_cols // HD
    depth = width // CHUNKS

    waits = {}
    if iteration == 0:
        for c in range(CHUNKS):
            part = pl.ds(c * depth, depth)
            waits[c] = [
                pltpu.make_async_copy(wq_in.at[part, :], wq.at[part, :], sems.at[0, c]),
                pltpu.make_async_copy(wkv_in.at[part, :], wkv.at[part, :], sems.at[1, c]),
            ]
            waits["out", c] = [pltpu.make_async_copy(wo_in.at[:, part], wo.at[:, part], sems.at[2, c])]
        sure = sure_in.shape[1]
        waits["cache"] = [
            pltpu.make_async_copy(sure_in, cache.at[:, pl.ds(0, sure), :], sems.at[3, 0]),
            pltpu.make_async_copy(
                more_in, cache.at[:, pl.ds(sure, more_in.shape[1]), :], sems.at[3, 1]
            ),
        ]
        for name in [0, 1, 2, 3, "cache", 4, 5, 6, 7]:
            for copy in waits[name]:
                copy.start()

    def wait(name):
        for copy in waits.get(name, ()):
            copy.wait()

    def receivers():
        lines = [
            cache[owner, :PAGE, :HD].astype(jnp.float32)[:1, :] for owner in range(owners)
        ]
        firsts = jnp.concatenate(lines, axis=0)
        owner = lax.broadcasted_iota(jnp.int32, firsts.shape, 0)
        slot = lax.broadcasted_iota(jnp.int32, firsts.shape, 1)
        numbers = (owner * each + slot).astype(jnp.float32)
        found = []
        for k in range(target_ref.shape[0]):
            here = (owner == target_ref[k]) & (slot < each)
            here = here & (firsts == landing_ref[k].astype(jnp.float32))
            found.append(jnp.sum(jnp.where(here, numbers, 0.0)).astype(jnp.int32))
        return found

    def window(r, size, page=0):
        return pl.ds(pl.multiple_of((first_ref[r] + page + 1) * PAGE, PAGE), size)

    def patch(requests, action):
        pieces = offset_ref.shape[0]
        rows = sum(ref.shape[0] for ref in arrived_refs) // pieces
        piece = 0
        for ref in arrived_refs:
            for local in range(ref.shape[0] // rows):
                request = jnp.int32(0)
                for k, number in enumerate(requests):
                    request = jnp.where(prompt_ref[piece] == k, number, request)
                for p in range(rows // PAGE):
                    page = offset_ref[piece] // PAGE + p

                    @pl.when(page < used_ref[request])
                    def _():
                        copy = pltpu.make_async_copy(
                            ref.at[pl.ds(local * rows + p * PAGE, PAGE), :],
                            cache.at[request // each, window(request, PAGE, page), :],
                            patch_sems.at[piece, p],
                        )
                        action(copy)

                piece += 1

    place = 0
    for ref in x_refs:
        for rows in [ref[...]] if ref.ndim == 2 else [ref[k] for k in range(ref.shape[0])]:
            x_rows[place : place + each, :] = rows.astype(jnp.float32)
            place += each
    order = order_ref[...]

    query = jnp.zeros((count, q_cols), jnp.float32)
    keyvalue = jnp.zeros((count, 2 * HD), jnp.float32)
    for c in range(CHUNKS):
        part = slice(c * depth, (c + 1) * depth)
        x = jnp.dot(
            order, x_rows[:, part].astype(jnp.bfloat16), preferred_element_type=jnp.float32
        ).astype(jnp.bfloat16)
        wait(c)
        if iteration == 0:
            for copy in waits["out", c]:
                copy.start()
        query += jnp.dot(x, wq[part, :], preferred_element_type=jnp.float32)
        keyvalue += jnp.dot(x, wkv[part, :], preferred_element_type=jnp.float32)
        if iteration == 0 and c == CHUNKS - 2:
            wait("cache")
            requests = receivers()
            patch(requests, lambda copy: copy.start())

    cosine = cos_ref[iteration]
    sine = sin_ref[iteration]
    key = turn(keyvalue[:, :HD], cosine, sine).astype(jnp.bfloat16)
    value = keyvalue[:, HD:].astype(jnp.bfloat16)
    fresh_ref[:, :HD] = key
    fresh_ref[:, HD:] = value
    news = [(ref[:, :HD], ref[:, HD:]) for ref in new_refs] + [(key, value)]
    for j in range(LANES):
        lane = pl.ds(j, count, LANES)
        if j < heads:
            turned = turn(query[:, j * HD : (j + 1) * HD], cosine, sine).astype(jnp.bfloat16)
            q_s[lane, :] = turned.astype(jnp.float32)
        else:
            q_s[lane, :] = jnp.zeros((count, HD), jnp.float32)
        for t, pair in enumerate(news):
            for half in range(2):
                new_s[t, half, lane, :] = pair[half].astype(jnp.float32)

    if iteration == 0:
        patch(requests, lambda copy: copy.wait())
    scale = HD**-0.5
    column = lax.broadcasted_iota(jnp.int32, (LANES, span), 1)
    for r in range(count):
        rows = slice(r * LANES, (r + 1) * LANES)
        found = lax.dot_general(
            q_s[rows, :].astype(jnp.bfloat16),
            cache[r // each, window(r, span), :HD],
            (((1,), (1,)), ((), ())),
            preferred_element_type=jnp.float32,
        )
        score_s[rows, :] = jnp.where(column < lens_ref[r], found * scale, -1e30)

    scores = score_s[...]
    queries = q_s[...]
    fresh_scores = [
        jnp.sum(queries * new_s[t, 0], axis=-1, keepdims=True) * scale for t in range(iteration + 1)
    ]
    top = jnp.max(scores, axis=-1, keepdims=True)
    for s in fresh_scores:
        top = jnp.maximum(top, s)
    weights = jnp.exp(scores - top)
    fresh_weights = [jnp.exp(s - top) for s in fresh_scores]
    total = jnp.sum(weights, axis=-1, keepdims=True)
    for w in fresh_weights:
        total = total + w
    score_s[...] = weights / total
    row = lax.broadcasted_iota(jnp.int32, (span, HD), 0)
    for r in range(count):
        rows = slice(r * LANES, (r + 1) * LANES)
        mix_s[rows, :] = jnp.dot(
            score_s[rows, :].astype(jnp.bfloat16),
            jnp.where(
                row < lens_ref[r],
                cache[r // each, window(r, span), HD:],
                jnp.zeros((), jnp.bfloat16),
            ),
            preferred_element_type=jnp.float32,
        )
    mixed = mix_s[...]
    for t in range(iteration + 1):
        weight = (fresh_weights[t] / total).astype(jnp.bfloat16).astype(jnp.float32)
        mixed = mixed + weight * new_s[t, 1]
    mix_s[...] = mixed
    columns = jnp.concatenate(
        [mix_s[pl.ds(j, count, LANES), :].astype(jnp.bfloat16) for j in range(heads)], axis=1
    )
    for c in range(CHUNKS):
        part = slice(c * depth, (c + 1) * depth)
        wait(("out", c))
        product = jnp.dot(columns, wo[:, part], preferred_element_type=jnp.float32)
        for d in range(owners):
            out_ref[d, :, part] = product[d * each : (d + 1) * each, :].astype(jnp.bfloat16)


def step(x_blocks, order, lengths, used, first, cosine, sine, earlier, held, each, prompts=()):
    width, q_cols = held[0].shape
    owners = held[3].shape[0]
    count = owners * each
    cached = sum(a.shape[1] for a in held[3:])
    span = (cached // PAGE - 1) // each * PAGE
    iteration = len(earlier)
    blocks = len(x_blocks)
    groups = max(len(prompts) - 4, 0)
    smem = pl.BlockSpec(memory_space=pltpu.SMEM)
    hbm = pl.BlockSpec(memory_space=pltpu.HBM)
    anywhere = pl.BlockSpec(memory_space=pl.ANY)
    out_shape = [
        jax.ShapeDtypeStruct((owners, each, width), jnp.bfloat16),
        jax.ShapeDtypeStruct((count, 2 * HD), jnp.bfloat16),
    ]
    in_specs = [whole()] * (blocks + 1) + [smem] * 3 + [whole()] * (2 + iteration)
    scratch = [
        pltpu.VMEM((count, width), jnp.float32),
        pltpu.VMEM((count * LANES, HD), jnp.float32),
        pltpu.VMEM((count * LANES, span), jnp.float32),
        pltpu.VMEM((count * LANES, HD), jnp.float32),
        pltpu.VMEM((iteration + 1, 2, count * LANES, HD), jnp.float32),
    ]
    if iteration == 0:
        in_specs += [smem] * 4 + [whole()] * groups + [hbm] * 3 + [anywhere] * 2
        out_shape += [pltpu.VMEM(a.shape, a.dtype) for a in held[:3]]
        out_shape.append(pltpu.VMEM((owners, cached, 2 * HD), jnp.bfloat16))
        held = [pltpu.with_memory_space_constraint(a, pltpu.HBM) for a in held[:3]] + list(held[3:])
        pieces = prompts[3].shape[0]
        pages = sum(a.shape[0] for a in prompts[4:]) // pieces // PAGE
        scratch.append(pltpu.SemaphoreType.DMA((4, CHUNKS)))
        scratch.append(pltpu.SemaphoreType.DMA((pieces, pages)))
    else:
        in_specs += [whole()] * 4
    return pl.pallas_call(
        functools.partial(step_kernel, blocks, iteration, groups, each),
        out_shape=tuple(out_shape),
        in_specs=in_specs,
        out_specs=tuple(whole() for _ in out_shape),
        scratch_shapes=scratch,
        compiler_params=pltpu.CompilerParams(vmem_limit_bytes=VMEM_LIMIT),
        cost_estimate=pl.CostEstimate(
            flops=2 * count * width * (2 * q_cols + 2 * HD),
            bytes_accessed=2 * sum(a.size for a in held),
            transcendentals=count * LANES * span,
        ),
        name="decode_step",
    )(*x_blocks, order, lengths, used, first, cosine, sine, *earlier, *prompts, *held)


def settle_kernel(parts_ref, state_ref, gain_ref, next_ref, normed_ref):
    total = parts_ref[0].astype(jnp.float32)
    for d in range(1, parts_ref.shape[0]):
        total = total + parts_ref[d].astype(jnp.float32)
    state = (state_ref[...].astype(jnp.float32) + total).astype(jnp.bfloat16)
    next_ref[...] = state
    gain = gain_ref[...].astype(jnp.float32)
    normed_ref[...] = normed_rows(state.astype(jnp.float32), gain).astype(jnp.bfloat16)


def last_kernel(parts_ref, *refs):
    state_refs, out_ref = refs[:-1], refs[-1]
    total = parts_ref[0].astype(jnp.float32)
    for d in range(1, parts_ref.shape[0]):
        total = total + parts_ref[d].astype(jnp.float32)
    for index, state_ref in enumerate(state_refs):
        out_ref[index] = state_ref[...]
    out_ref[len(state_refs)] = (state_refs[-1][...].astype(jnp.float32) + total).astype(jnp.bfloat16)


def last(parts, states):
    return pl.pallas_call(
        last_kernel,
        out_shape=jax.ShapeDtypeStruct((len(states) + 1, *states[0].shape), jnp.bfloat16),
        in_specs=[whole()] * (1 + len(states)),
        out_specs=whole(),
        compiler_params=pltpu.CompilerParams(vmem_limit_bytes=VMEM_LIMIT),
        name="last",
    )(parts, *states)


def settle(parts, state, gain):
    shape = jax.ShapeDtypeStruct(state.shape, jnp.bfloat16)
    return pl.pallas_call(
        settle_kernel,
        out_shape=(shape, shape),
        in_specs=[whole()] * 3,
        out_specs=(whole(), whole()),
        compiler_params=pltpu.CompilerParams(vmem_limit_bytes=VMEM_LIMIT),
        name="settle",
    )(parts, state, gain)


def on_device(
    prompt_states,
    decode_states,
    norm_gain,
    w_query,
    w_keyvalue,
    w_output,
    cache_pages,
    page_table,
    cache_len,
    dest_rank,
    dest_page,
):
    rank = lax.axis_index("tensor")
    section = lax.axis_index("section")
    count = lax.axis_size("tensor")
    pool = cache_pages[0]
    page_size, kv_width = pool.shape[1:]
    own_table = page_table[0]
    lengths = cache_len[0]
    each, width = decode_states.shape[1:]
    tokens = prompt_states.shape[1]
    q_cols = w_query.shape[1]
    kv_heads = kv_width // (2 * HD)
    shared = count // kv_heads if count > kv_heads else 1
    gain = norm_gain[None, :]

    if w_keyvalue.shape[1] < 2 * HD:
        other = swap_xor(w_keyvalue, 1)
        is_key = rank % 2 == 0
        w_pair = jnp.concatenate(
            [jnp.where(is_key, w_keyvalue, other), jnp.where(is_key, other, w_keyvalue)], axis=1
        )
    else:
        w_pair = w_keyvalue

    sections = lax.axis_size("section")
    onward = [(s, (s + 1) % sections) for s in range(sections)]
    grid = count == 8 and sections == 2

    numbers = jnp.arange(count * each, dtype=jnp.int32)
    per_request = own_table.shape[1]
    used = (lengths + page_size - 1) // page_size
    by_owner = used.reshape(count, each)
    first = (jnp.cumsum(by_owner, axis=1) - by_owner).reshape(-1)
    most = jnp.max(jnp.sum(by_owner, axis=1, keepdims=True), keepdims=True)
    for axis in ("section", "groups"):
        for bit in range(lax.axis_size(axis).bit_length() - 1):
            pairs = [(s, s ^ (1 << bit)) for s in range(lax.axis_size(axis))]
            most = jnp.maximum(most, lax.ppermute(most, axis, pairs))
    own_used = lax.dynamic_slice_in_dim(used, rank * each, each)
    heads = tuple(target // shared for target in range(count))
    info = jnp.zeros((page_size, 2 * HD), jnp.bfloat16)
    info = info.at[0, :each].set(own_table[:, 0].astype(jnp.bfloat16))
    ready = make_parcels(own_table, own_used, info, pool, heads, 2 * HD)

    table, halves = grid_arrivals() if grid else ring_arrivals(count)
    parts = 1 if grid else 2
    rows = tokens // parts
    carried = np.array([index for index, piece in enumerate(halves) if piece == parts - 1])
    senders = jnp.asarray(table, jnp.int32)[rank]
    starts = senders * tokens + jnp.asarray(halves, jnp.int32) * rows
    orders = []
    masks = jnp.array([0, 1, 6, 4, 2, 7, 5, 3] if grid else range(count), jnp.int32)
    for owners in (senders[carried], rank ^ masks):
        rows_of = jnp.repeat(owners * each, each) + numbers % each
        orders.append((numbers[:, None] == rows_of[None, :]).astype(jnp.bfloat16))
    times = lengths[None, :] + jnp.arange(STEPS, dtype=jnp.int32)[:, None]
    cosine, sine = rope_tables(times.reshape(-1))
    cosine = cosine.reshape(STEPS, count * each, HD)
    sine = sine.reshape(STEPS, count * each, HD)
    sizes = [size for size in MORE if size < pool.shape[0] - SURE] + [pool.shape[0] - SURE]
    wanted = most[0, 0] - SURE
    choice = jnp.sum((wanted > jnp.array(sizes[:-1], jnp.int32)).astype(jnp.int32))
    ready = (ready, w_pair, choice, starts, orders, cosine, sine)
    if grid:
        lines = norm_gain.reshape(-1, HD)
        *pieces, state = prepare_blocks(prompt_states[0], decode_states[0], lines)
    else:
        state = decode_states[0]
        pieces = prepare(prompt_states[0], decode_states[0], gain, parts)
    known, pending, finish, ready = (along_grid if grid else along_ring)(pieces, ready)
    ready, *_, choice, starts, orders, cosine, sine = ready

    sure, more = ready

    def exchange(pages):
        return lax.all_to_all(
            pages.reshape(count, -1, 2 * HD), "tensor", split_axis=0, concat_axis=0, tiled=True
        )

    extra = more.shape[1]

    def branch(size):
        def run(more):
            if size == 0:
                return jnp.zeros((count, extra * page_size, 2 * HD), jnp.bfloat16)
            pages = exchange(more[:, :size])
            return jnp.pad(pages, ((0, 0), (0, (extra - size) * page_size), (0, 0)))

        return run

    more = lax.switch(choice, [branch(size) for size in sizes], more)
    known, pending, more = lax.optimization_barrier((known, pending, more))
    sure, _ = lax.optimization_barrier((sure, more))
    sure = exchange(sure)

    prompt_kv = []
    blocks = []
    if grid:
        rest, halves_of_other, begins = finish(pending)
        own, other, states = project(
            known[0] + rest, w_pair, starts, 0, rows, each, halves_of_other, begins
        )
        prompt_kv = [own, cross(other)]
        blocks = [states, cross(states)]
    else:
        skipped = 0
        for group in known:
            values, states = project(group, w_pair, starts, skipped, rows, each)
            prompt_kv.append(values)
            blocks.append(states)
            skipped += len(group)
    arrived = tuple(lax.ppermute(part, "section", onward) for part in prompt_kv)
    anchor = (section + 1) % sections
    targets = lax.dynamic_index_in_dim(dest_rank, anchor, 0, keepdims=False)
    landing = lax.dynamic_index_in_dim(dest_page, anchor, 0, keepdims=False)[:, 0]
    prompts = (targets, landing, starts // PLEN, starts % PLEN, *arrived)
    held = (w_query, w_pair, w_output, sure, more)

    blocks, cosine, sine, state, gain = lax.optimization_barrier((blocks, cosine, sine, state, gain))
    outputs = []
    earlier = []
    for iteration in range(STEPS):
        chosen = orders[min(iteration, 1)]
        parts, fresh, *fetched = step(
            blocks, chosen, lengths, used, first, cosine, sine, earlier, held, each, prompts
        )
        if iteration == 0:
            held, prompts = fetched, ()
        earlier.append(fresh)
        parts = lax.all_to_all(parts, "tensor", split_axis=0, concat_axis=0, tiled=True)
        if iteration + 1 < STEPS:
            state, normed = settle(parts, state, gain)
            outputs.append(state)
            if grid:
                along = [swap_xor(normed, bits) for bits in (6, 4, 2)]
                blocks = [normed, cross(normed), *along, *(cross(block) for block in along)]
            else:
                blocks = [normed] + [swap_xor(normed, bits) for bits in range(1, count)]
    return last(parts, outputs)[:, None]


def solution(mesh):
    in_specs = (
        P(("groups", "section"), "tensor", None),
        P(("groups", "section"), "tensor", None),
        P(),
        P(None, "tensor"),
        P(None, "tensor"),
        P("tensor", None),
        P(("groups", "section"), "tensor", None, None),
        P(("groups", "section"), "tensor", None),
        P(("groups", "section"), None),
        P("groups", None),
        P("groups", None, None),
    )
    out_specs = P(None, ("groups", "section"), "tensor", None)
    return jax.shard_map(
        on_device, mesh=mesh, in_specs=in_specs, out_specs=out_specs, check_vma=False
    )
```

```python
import functools

import jax
import jax.numpy as jnp
import numpy as np
from jax import lax
from jax.experimental import pallas as pl
from jax.experimental.pallas import tpu as pltpu
from jax.sharding import PartitionSpec as P

HD = 128
PLEN = 128
STEPS = 4
EPS = 1e-05
ROPE_BASE = 500000.0
LANES = 8
CHUNKS = 8
PAGE = 16
SURE = 14
MORE = (0, 14, 18, 22, 24, 26, 28, 30, 32, 34, 38, 42)
VMEM_LIMIT = 10 * 1024 * 1024


def ring_shift(value, steps):
    count = lax.axis_size("tensor")
    return lax.ppermute(value, "tensor", [(s, (s + steps) % count) for s in range(count)])


def swap_xor(value, mask):
    count = lax.axis_size("tensor")
    return lax.ppermute(value, "tensor", [(s, s ^ mask) for s in range(count)])


def ring_arrivals(count):
    table, halves = [np.arange(count)] * 2, [0, 1]
    for hop in range(1, count // 2 + 1):
        for piece in range(2):
            for way in range(2):
                if hop < count // 2 or piece == way:
                    table.append((np.arange(count) - (1 - 2 * way) * hop) % count)
                    halves.append(piece)
    return np.stack(table, axis=1), halves


def along_ring(pieces, ready):
    count = lax.axis_size("tensor")
    blocks = list(pieces)
    going = [[rows, rows] for rows in pieces]
    for hop in range(1, count // 2 + 1):
        for piece in range(2):
            for way in range(2):
                if hop < count // 2 or piece == way:
                    going[piece][way] = ring_shift(going[piece][way], 1 - 2 * way)
                    blocks.append(going[piece][way])
        if hop == 1:
            going, ready = lax.optimization_barrier((going, ready))
    return [blocks[at : at + 8] for at in range(0, len(blocks), 8)], (), lambda pending: [], ready


def cross(value):
    return lax.ppermute(value, "tensor", [(r, r ^ 1) for r in range(8)])


def grid_arrivals():
    table = []
    for across in (0, 1):
        for origin in ((0, 1, 2, 3), (1, 0, 3, 2), (2, 2, 1, 1), (3, 3, 0, 0)):
            table.append(np.array([(2 * origin[r // 2] + r % 2) ^ across for r in range(8)]))
    return np.stack(table, axis=1), [0] * 8


def along_grid(pieces, ready):
    z = lax.axis_index("tensor") // 2

    def shift(rows, steps, starts):
        pairs = [(2 * s + c, 2 * (s + steps) + c) for s in starts for c in range(2)]
        return lax.ppermute(rows, "tensor", pairs)

    def pick(*rows):
        return jnp.where(z == 0, rows[0], jnp.where(z == 1, rows[1], jnp.where(z == 2, rows[2], rows[3])))

    (rows,) = pieces
    up, down = shift(rows, 1, (0, 1, 2)), shift(rows, -1, (1, 2, 3))
    up, down, parcels, weight = lax.optimization_barrier((up, down, *ready[:2]))
    section = lax.axis_index("section")
    half = weight.shape[0] // 2
    brought = cross(lax.dynamic_slice_in_dim(weight, section * half, half))
    ready = (parcels, *ready[2:])
    up2, down2 = shift(up, 1, (1, 2)), shift(down, -1, (1, 2))
    up2, down2, ready = lax.optimization_barrier((up2, down2, ready))
    outward = jnp.where(z == 1, down2, up2)
    ends = lax.ppermute(outward, "tensor", [(2, 0), (3, 1), (4, 6), (5, 7)])

    def finish(pending):
        up, down, up2, down2, ends, brought = pending
        given = lax.ppermute(brought, "section", [(0, 1), (1, 0)])
        begins = jnp.stack([section * half, (1 - section) * half]).astype(jnp.int32)
        second = pick(down, up, down, up)
        third = pick(down2, down, up, up2)
        fourth = pick(ends, down2, up2, ends)
        return [second, third, fourth], (brought, given), begins

    return [[rows]], (up, down, up2, down2, ends, brought), finish, ready


def rope_tables(positions, lib=jnp):
    half_dim = HD // 2
    freqs = ROPE_BASE ** (-(lib.arange(half_dim, dtype=lib.float32) * 2.0 / HD))
    angles = positions.astype(lib.float32)[:, None] * freqs[None, :].astype(lib.float32)
    cosine = lib.cos(angles)
    sine = lib.sin(angles)
    return (
        lib.concatenate([cosine, cosine], axis=1).astype(lib.float32),
        lib.concatenate([-sine, sine], axis=1).astype(lib.float32),
    )


def whole():
    return pl.BlockSpec(memory_space=pltpu.VMEM)


def normed_rows(values, gain):
    square = jnp.mean(values * values, axis=-1, keepdims=True)
    return values * lax.rsqrt(square + EPS) * gain


def prepare_kernel(prompt_ref, state_ref, gain_ref, *out_refs):
    tokens, width = prompt_ref.shape
    rows = tokens // len(out_refs)
    gain = gain_ref[...].astype(jnp.float32)
    for index, out_ref in enumerate(out_refs):
        part = prompt_ref[index * rows : (index + 1) * rows, :].astype(jnp.float32)
        out_ref[:rows, :] = normed_rows(part, gain).astype(jnp.bfloat16)
    states = normed_rows(state_ref[...].astype(jnp.float32), gain)
    filling = jnp.zeros((out_refs[-1].shape[0] - rows - states.shape[0], width), jnp.float32)
    out_refs[-1][rows:, :] = jnp.concatenate([states, filling], axis=0).astype(jnp.bfloat16)


def prepare(prompts, states, gain, pieces):
    tokens, width = prompts.shape
    rows = [tokens // pieces] * pieces
    rows[-1] += -(-states.shape[0] // LANES) * LANES
    return pl.pallas_call(
        prepare_kernel,
        out_shape=tuple(jax.ShapeDtypeStruct((count, width), jnp.bfloat16) for count in rows),
        in_specs=[whole()] * 3,
        out_specs=tuple(whole() for _ in rows),
        compiler_params=pltpu.CompilerParams(vmem_limit_bytes=VMEM_LIMIT),
        name="prepare",
    )(prompts, states, gain)


def prepare_blocks_kernel(prompt_in, state_in, gain_ref, out_ref, states, prompts, sems):
    each = state_in.shape[0]
    copies = [
        pltpu.make_async_copy(prompt_in, prompts, sems.at[0]),
        pltpu.make_async_copy(state_in, states, sems.at[1]),
    ]
    for copy in copies:
        copy.start()
    gain = gain_ref[...].astype(jnp.float32)
    lanes = gain.shape[1]
    for copy, rows_ref, first in zip(copies, (prompts, states), (0, prompts.shape[0] // each)):
        copy.wait()
        values = rows_ref[...].astype(jnp.float32)
        factor = lax.rsqrt(jnp.mean(values * values, axis=-1, keepdims=True) + EPS)
        for c in range(gain.shape[0]):
            part = slice(c * lanes, (c + 1) * lanes)
            normed = rows_ref[:, part].astype(jnp.float32) * factor * gain[c : c + 1, :]
            for block in range(rows_ref.shape[0] // each):
                rows = normed[block * each : (block + 1) * each, :]
                out_ref[first + block, :, part] = rows.astype(jnp.bfloat16)


def prepare_blocks(prompts, states, gain):
    tokens, width = prompts.shape
    each = states.shape[0]
    hbm = pl.BlockSpec(memory_space=pltpu.HBM)
    return pl.pallas_call(
        prepare_blocks_kernel,
        out_shape=(
            jax.ShapeDtypeStruct((tokens // each + 1, each, width), jnp.bfloat16),
            jax.ShapeDtypeStruct(states.shape, jnp.bfloat16),
        ),
        in_specs=[hbm, hbm, whole()],
        out_specs=(whole(), whole()),
        scratch_shapes=[
            pltpu.VMEM(prompts.shape, jnp.bfloat16),
            pltpu.SemaphoreType.DMA((2,)),
        ],
        compiler_params=pltpu.CompilerParams(vmem_limit_bytes=VMEM_LIMIT),
        name="prepare",
    )(
        pltpu.with_memory_space_constraint(prompts, pltpu.HBM),
        pltpu.with_memory_space_constraint(states, pltpu.HBM),
        gain,
    )


def project_kernel(rows, each, skipped, halves, *refs):
    heads = 2 if halves else 1
    used = 7 + halves + 2 * heads
    blocks, refs = refs[:-used], refs[-used:]
    starts_ref, begins_ref, cos_ref, sin_ref = refs[:4]
    weight_ref, part_refs = refs[4], refs[5 : 5 + halves]
    out_refs = refs[5 + halves : 5 + halves + heads]
    states_ref, staged = refs[-2 - heads : -heads]
    sum_refs = refs[-heads:]
    depth = weight_ref.shape[0] // CHUNKS

    def stage(span):
        for index, block in enumerate(blocks):
            begin = index * rows
            if block.ndim == 2:
                staged[begin : begin + rows, :] = block[:rows, span].astype(jnp.float32)
                continue
            for piece in range(rows // each):
                here = slice(begin + piece * each, begin + (piece + 1) * each)
                staged[here, :] = block[piece, :, span].astype(jnp.float32)
        return staged[...].astype(jnp.bfloat16)

    for sum_ref in sum_refs:
        sum_ref[...] = jnp.zeros_like(sum_ref)

    def add(shift, count, part_ref=None):
        @pl.loop(0, count)
        def _(c):
            there = pl.ds(pl.multiple_of(shift + c * depth, depth), depth)
            x = stage(there)
            sum_refs[0][...] += jnp.dot(
                x, weight_ref[there, :], preferred_element_type=jnp.float32
            )
            if part_ref is not None:
                here = pl.ds(pl.multiple_of(c * depth, depth), depth)
                sum_refs[1][...] += jnp.dot(
                    x, part_ref[here, :], preferred_element_type=jnp.float32
                )

    if not halves:
        add(0, CHUNKS)
    for index, part_ref in enumerate(part_refs):
        add(begins_ref[index], part_ref.shape[0] // depth, part_ref)
    totals = [sum_ref[...] for sum_ref in sum_refs]
    for total, out_ref in zip(totals, out_refs):
        out_ref[:, HD:] = total[:, HD:].astype(jnp.bfloat16)
        for index in range(len(blocks)):
            begin = starts_ref[skipped + index] % PLEN
            span = pl.ds(pl.multiple_of(begin, rows), rows)
            here = slice(index * rows, (index + 1) * rows)
            keys = turn(total[here, :HD], cos_ref[span, :], sin_ref[span, :])
            out_ref[here, :HD] = keys.astype(jnp.bfloat16)
    found = 0
    for block in blocks:
        if block.ndim == 3:
            states_ref[found] = block[rows // each]
            found += 1
        elif block.shape[0] > rows:
            states_ref[found] = block[rows:, :].astype(jnp.float32)[:each, :].astype(jnp.bfloat16)
            found += 1


def project(blocks, weight, starts, skipped, rows, each, parts=(), begins=None):
    width = weight.shape[0]
    cosine, sine = rope_tables(np.arange(PLEN), np)
    carrying = sum(block.ndim == 3 or block.shape[0] > rows for block in blocks)
    heads = 2 if parts else 1
    values = jax.ShapeDtypeStruct((len(blocks) * rows, 2 * HD), jnp.bfloat16)
    out_shape = [values] * heads
    out_shape.append(jax.ShapeDtypeStruct((carrying, each, width), jnp.bfloat16))
    smem = pl.BlockSpec(memory_space=pltpu.SMEM)
    begins = jnp.zeros((2,), jnp.int32) if begins is None else begins
    return pl.pallas_call(
        functools.partial(project_kernel, rows, each, skipped, len(parts)),
        out_shape=tuple(out_shape),
        in_specs=[whole()] * len(blocks) + [smem] * 2 + [whole()] * (3 + len(parts)),
        out_specs=tuple(whole() for _ in out_shape),
        scratch_shapes=[
            pltpu.VMEM((len(blocks) * rows, width // CHUNKS), jnp.float32),
            *[pltpu.VMEM(values.shape, jnp.float32)] * heads,
        ],
        compiler_params=pltpu.CompilerParams(vmem_limit_bytes=VMEM_LIMIT),
        cost_estimate=pl.CostEstimate(
            flops=2 * len(blocks) * rows * weight.size * heads,
            bytes_accessed=2 * weight.size * heads,
            transcendentals=0,
        ),
        name="project",
    )(*blocks, starts, begins, cosine, sine, weight, *parts)


def parcels_kernel(heads, table_ref, used_ref, info_ref, pool_ref, sure_ref, more_ref, held, load_sem, store_sem):
    width = sure_ref.shape[-1]
    each, per_request = table_ref.shape
    pages = each * per_request
    sure = sure_ref.shape[1] - 1
    stores = []
    for target in range(len(heads)):
        copy = pltpu.make_async_copy(info_ref, sure_ref.at[target, 0], store_sem.at[0, target])
        copy.start()
        stores.append(copy)
    front = jnp.int32(0)
    back = used_ref[0]
    for r in range(1, each):
        back = back + used_ref[r]
    loads = []
    for r in range(each):
        used = used_ref[r]
        for p in range(per_request):
            spot = jnp.where(p < used, front + p, back + p - used)
            copy = pltpu.make_async_copy(
                pool_ref.at[table_ref[r, p]], held.at[spot], load_sem.at[r * per_request + p]
            )
            copy.start()
            loads.append(copy)
        front = front + used
        back = back + per_request - used
    for copy in loads:
        copy.wait()
    for target, head in enumerate(heads):
        columns = pl.ds(head * width, width)
        for bank, source, goal in (
            (1, held.at[pl.ds(0, sure), :, columns], sure_ref.at[target, pl.ds(1, sure)]),
            (2, held.at[pl.ds(sure, pages - sure), :, columns], more_ref.at[target]),
        ):
            copy = pltpu.make_async_copy(source, goal, store_sem.at[bank, target])
            copy.start()
            stores.append(copy)
    for copy in stores:
        copy.wait()


def make_parcels(table, used, info, pool, heads, width):
    pages, rows, _ = pool.shape
    hbm = pl.BlockSpec(memory_space=pltpu.HBM)
    smem = pl.BlockSpec(memory_space=pltpu.SMEM)
    return pl.pallas_call(
        functools.partial(parcels_kernel, heads),
        out_shape=(
            pltpu.HBM((len(heads), SURE + 1, rows, width), jnp.bfloat16),
            pltpu.HBM((len(heads), pages - SURE, rows, width), jnp.bfloat16),
        ),
        in_specs=[smem, smem, whole(), hbm],
        out_specs=(hbm, hbm),
        scratch_shapes=[
            pltpu.VMEM(pool.shape, jnp.bfloat16),
            pltpu.SemaphoreType.DMA((pages,)),
            pltpu.SemaphoreType.DMA((3, len(heads))),
        ],
        compiler_params=pltpu.CompilerParams(vmem_limit_bytes=VMEM_LIMIT),
        name="parcels",
    )(table, used, info, pltpu.with_memory_space_constraint(pool, pltpu.HBM))


def turn(values, cosine, sine):
    return values * cosine + pltpu.roll(values, HD // 2, 1) * sine


def step_kernel(blocks, iteration, groups, each, *refs):
    x_refs = refs[:blocks]
    order_ref, lens_ref, used_ref, first_ref, cos_ref, sin_ref = refs[blocks : blocks + 6]
    new_refs = refs[blocks + 6 : blocks + 6 + iteration]
    refs = refs[blocks + 6 + iteration :]
    if iteration == 0:
        target_ref, landing_ref, prompt_ref, offset_ref = refs[:4]
        arrived_refs = refs[4 : 4 + groups]
        refs = refs[4 + groups :]
        wq_in, wkv_in, wo_in, sure_in, more_in, out_ref, fresh_ref, wq, wkv, wo, cache = refs[:11]
        x_rows, q_s, score_s, mix_s, new_s, sems, patch_sems = refs[11:]
    else:
        wq, wkv, wo, cache = refs[:4]
        out_ref, fresh_ref, x_rows, q_s, score_s, mix_s, new_s = refs[4:]
    width, q_cols = wq.shape
    owners = cache.shape[0]
    count = owners * each
    span = (cache.shape[1] // PAGE - 1) // each * PAGE
    heads = q_cols // HD
    depth = width // CHUNKS

    waits = {}
    if iteration == 0:
        for c in range(CHUNKS):
            part = pl.ds(c * depth, depth)
            waits[c] = [
                pltpu.make_async_copy(wq_in.at[part, :], wq.at[part, :], sems.at[0, c]),
                pltpu.make_async_copy(wkv_in.at[part, :], wkv.at[part, :], sems.at[1, c]),
            ]
            waits["out", c] = [pltpu.make_async_copy(wo_in.at[:, part], wo.at[:, part], sems.at[2, c])]
        sure = sure_in.shape[1]
        waits["cache"] = [
            pltpu.make_async_copy(sure_in, cache.at[:, pl.ds(0, sure), :], sems.at[3, 0]),
            pltpu.make_async_copy(
                more_in, cache.at[:, pl.ds(sure, more_in.shape[1]), :], sems.at[3, 1]
            ),
        ]
        for name in [0, 1, 2, 3, "cache", 4, 5, 6, 7]:
            for copy in waits[name]:
                copy.start()

    def wait(name):
        for copy in waits.get(name, ()):
            copy.wait()

    def receivers():
        lines = [
            cache[owner, :PAGE, :HD].astype(jnp.float32)[:1, :] for owner in range(owners)
        ]
        firsts = jnp.concatenate(lines, axis=0)
        owner = lax.broadcasted_iota(jnp.int32, firsts.shape, 0)
        slot = lax.broadcasted_iota(jnp.int32, firsts.shape, 1)
        numbers = (owner * each + slot).astype(jnp.float32)
        found = []
        for k in range(target_ref.shape[0]):
            here = (owner == target_ref[k]) & (slot < each)
            here = here & (firsts == landing_ref[k].astype(jnp.float32))
            found.append(jnp.sum(jnp.where(here, numbers, 0.0)).astype(jnp.int32))
        return found

    def window(r, size, page=0):
        return pl.ds(pl.multiple_of((first_ref[r] + page + 1) * PAGE, PAGE), size)

    def patch(requests, action):
        pieces = offset_ref.shape[0]
        rows = sum(ref.shape[0] for ref in arrived_refs) // pieces
        piece = 0
        for ref in arrived_refs:
            for local in range(ref.shape[0] // rows):
                request = jnp.int32(0)
                for k, number in enumerate(requests):
                    request = jnp.where(prompt_ref[piece] == k, number, request)
                for p in range(rows // PAGE):
                    page = offset_ref[piece] // PAGE + p

                    @pl.when(page < used_ref[request])
                    def _():
                        copy = pltpu.make_async_copy(
                            ref.at[pl.ds(local * rows + p * PAGE, PAGE), :],
                            cache.at[request // each, window(request, PAGE, page), :],
                            patch_sems.at[piece, p],
                        )
                        action(copy)

                piece += 1

    place = 0
    for ref in x_refs:
        for rows in [ref[...]] if ref.ndim == 2 else [ref[k] for k in range(ref.shape[0])]:
            x_rows[place : place + each, :] = rows.astype(jnp.float32)
            place += each
    order = order_ref[...]

    query = jnp.zeros((count, q_cols), jnp.float32)
    keyvalue = jnp.zeros((count, 2 * HD), jnp.float32)
    for c in range(CHUNKS):
        part = slice(c * depth, (c + 1) * depth)
        x = jnp.dot(
            order, x_rows[:, part].astype(jnp.bfloat16), preferred_element_type=jnp.float32
        ).astype(jnp.bfloat16)
        wait(c)
        if iteration == 0:
            for copy in waits["out", c]:
                copy.start()
        query += jnp.dot(x, wq[part, :], preferred_element_type=jnp.float32)
        keyvalue += jnp.dot(x, wkv[part, :], preferred_element_type=jnp.float32)
        if iteration == 0 and c == CHUNKS - 2:
            wait("cache")
            requests = receivers()
            patch(requests, lambda copy: copy.start())

    cosine = cos_ref[iteration]
    sine = sin_ref[iteration]
    key = turn(keyvalue[:, :HD], cosine, sine).astype(jnp.bfloat16)
    value = keyvalue[:, HD:].astype(jnp.bfloat16)
    fresh_ref[:, :HD] = key
    fresh_ref[:, HD:] = value
    news = [(ref[:, :HD], ref[:, HD:]) for ref in new_refs] + [(key, value)]
    for j in range(LANES):
        lane = pl.ds(j, count, LANES)
        if j < heads:
            turned = turn(query[:, j * HD : (j + 1) * HD], cosine, sine).astype(jnp.bfloat16)
            q_s[lane, :] = turned.astype(jnp.float32)
        else:
            q_s[lane, :] = jnp.zeros((count, HD), jnp.float32)
        for t, pair in enumerate(news):
            for half in range(2):
                new_s[t, half, lane, :] = pair[half].astype(jnp.float32)

    if iteration == 0:
        patch(requests, lambda copy: copy.wait())
    scale = HD**-0.5
    column = lax.broadcasted_iota(jnp.int32, (LANES, span), 1)
    for r in range(count):
        rows = slice(r * LANES, (r + 1) * LANES)
        found = lax.dot_general(
            q_s[rows, :].astype(jnp.bfloat16),
            cache[r // each, window(r, span), :HD],
            (((1,), (1,)), ((), ())),
            preferred_element_type=jnp.float32,
        )
        score_s[rows, :] = jnp.where(column < lens_ref[r], found * scale, -1e30)

    scores = score_s[...]
    queries = q_s[...]
    fresh_scores = [
        jnp.sum(queries * new_s[t, 0], axis=-1, keepdims=True) * scale for t in range(iteration + 1)
    ]
    top = jnp.max(scores, axis=-1, keepdims=True)
    for s in fresh_scores:
        top = jnp.maximum(top, s)
    weights = jnp.exp(scores - top)
    fresh_weights = [jnp.exp(s - top) for s in fresh_scores]
    total = jnp.sum(weights, axis=-1, keepdims=True)
    for w in fresh_weights:
        total = total + w
    score_s[...] = weights / total
    row = lax.broadcasted_iota(jnp.int32, (span, HD), 0)
    for r in range(count):
        rows = slice(r * LANES, (r + 1) * LANES)
        mix_s[rows, :] = jnp.dot(
            score_s[rows, :].astype(jnp.bfloat16),
            jnp.where(
                row < lens_ref[r],
                cache[r // each, window(r, span), HD:],
                jnp.zeros((), jnp.bfloat16),
            ),
            preferred_element_type=jnp.float32,
        )
    mixed = mix_s[...]
    for t in range(iteration + 1):
        weight = (fresh_weights[t] / total).astype(jnp.bfloat16).astype(jnp.float32)
        mixed = mixed + weight * new_s[t, 1]
    mix_s[...] = mixed
    columns = jnp.concatenate(
        [mix_s[pl.ds(j, count, LANES), :].astype(jnp.bfloat16) for j in range(heads)], axis=1
    )
    for c in range(CHUNKS):
        part = slice(c * depth, (c + 1) * depth)
        wait(("out", c))
        product = jnp.dot(columns, wo[:, part], preferred_element_type=jnp.float32)
        for d in range(owners):
            out_ref[d, :, part] = product[d * each : (d + 1) * each, :].astype(jnp.bfloat16)


def step(x_blocks, order, lengths, used, first, cosine, sine, earlier, held, each, prompts=()):
    width, q_cols = held[0].shape
    owners = held[3].shape[0]
    count = owners * each
    cached = sum(a.shape[1] for a in held[3:])
    span = (cached // PAGE - 1) // each * PAGE
    iteration = len(earlier)
    blocks = len(x_blocks)
    groups = max(len(prompts) - 4, 0)
    smem = pl.BlockSpec(memory_space=pltpu.SMEM)
    hbm = pl.BlockSpec(memory_space=pltpu.HBM)
    anywhere = pl.BlockSpec(memory_space=pl.ANY)
    out_shape = [
        jax.ShapeDtypeStruct((owners, each, width), jnp.bfloat16),
        jax.ShapeDtypeStruct((count, 2 * HD), jnp.bfloat16),
    ]
    in_specs = [whole()] * (blocks + 1) + [smem] * 3 + [whole()] * (2 + iteration)
    scratch = [
        pltpu.VMEM((count, width), jnp.float32),
        pltpu.VMEM((count * LANES, HD), jnp.float32),
        pltpu.VMEM((count * LANES, span), jnp.float32),
        pltpu.VMEM((count * LANES, HD), jnp.float32),
        pltpu.VMEM((iteration + 1, 2, count * LANES, HD), jnp.float32),
    ]
    if iteration == 0:
        in_specs += [smem] * 4 + [whole()] * groups + [hbm] * 3 + [anywhere] * 2
        out_shape += [pltpu.VMEM(a.shape, a.dtype) for a in held[:3]]
        out_shape.append(pltpu.VMEM((owners, cached, 2 * HD), jnp.bfloat16))
        held = [pltpu.with_memory_space_constraint(a, pltpu.HBM) for a in held[:3]] + list(held[3:])
        pieces = prompts[3].shape[0]
        pages = sum(a.shape[0] for a in prompts[4:]) // pieces // PAGE
        scratch.append(pltpu.SemaphoreType.DMA((4, CHUNKS)))
        scratch.append(pltpu.SemaphoreType.DMA((pieces, pages)))
    else:
        in_specs += [whole()] * 4
    return pl.pallas_call(
        functools.partial(step_kernel, blocks, iteration, groups, each),
        out_shape=tuple(out_shape),
        in_specs=in_specs,
        out_specs=tuple(whole() for _ in out_shape),
        scratch_shapes=scratch,
        compiler_params=pltpu.CompilerParams(vmem_limit_bytes=VMEM_LIMIT),
        cost_estimate=pl.CostEstimate(
            flops=2 * count * width * (2 * q_cols + 2 * HD),
            bytes_accessed=2 * sum(a.size for a in held),
            transcendentals=count * LANES * span,
        ),
        name="decode_step",
    )(*x_blocks, order, lengths, used, first, cosine, sine, *earlier, *prompts, *held)


def settle_kernel(parts_ref, state_ref, gain_ref, next_ref, normed_ref):
    total = parts_ref[0].astype(jnp.float32)
    for d in range(1, parts_ref.shape[0]):
        total = total + parts_ref[d].astype(jnp.float32)
    state = (state_ref[...].astype(jnp.float32) + total).astype(jnp.bfloat16)
    next_ref[...] = state
    gain = gain_ref[...].astype(jnp.float32)
    normed_ref[...] = normed_rows(state.astype(jnp.float32), gain).astype(jnp.bfloat16)


def last_kernel(parts_ref, *refs):
    state_refs, out_ref = refs[:-1], refs[-1]
    total = parts_ref[0].astype(jnp.float32)
    for d in range(1, parts_ref.shape[0]):
        total = total + parts_ref[d].astype(jnp.float32)
    for index, state_ref in enumerate(state_refs):
        out_ref[index] = state_ref[...]
    out_ref[len(state_refs)] = (state_refs[-1][...].astype(jnp.float32) + total).astype(jnp.bfloat16)


def last(parts, states):
    return pl.pallas_call(
        last_kernel,
        out_shape=jax.ShapeDtypeStruct((len(states) + 1, *states[0].shape), jnp.bfloat16),
        in_specs=[whole()] * (1 + len(states)),
        out_specs=whole(),
        compiler_params=pltpu.CompilerParams(vmem_limit_bytes=VMEM_LIMIT),
        name="last",
    )(parts, *states)


def settle(parts, state, gain):
    shape = jax.ShapeDtypeStruct(state.shape, jnp.bfloat16)
    return pl.pallas_call(
        settle_kernel,
        out_shape=(shape, shape),
        in_specs=[whole()] * 3,
        out_specs=(whole(), whole()),
        compiler_params=pltpu.CompilerParams(vmem_limit_bytes=VMEM_LIMIT),
        name="settle",
    )(parts, state, gain)


def on_device(
    prompt_states,
    decode_states,
    norm_gain,
    w_query,
    w_keyvalue,
    w_output,
    cache_pages,
    page_table,
    cache_len,
    dest_rank,
    dest_page,
):
    rank = lax.axis_index("tensor")
    section = lax.axis_index("section")
    count = lax.axis_size("tensor")
    pool = cache_pages[0]
    page_size, kv_width = pool.shape[1:]
    own_table = page_table[0]
    lengths = cache_len[0]
    each, width = decode_states.shape[1:]
    tokens = prompt_states.shape[1]
    q_cols = w_query.shape[1]
    kv_heads = kv_width // (2 * HD)
    shared = count // kv_heads if count > kv_heads else 1
    gain = norm_gain[None, :]

    if w_keyvalue.shape[1] < 2 * HD:
        other = swap_xor(w_keyvalue, 1)
        is_key = rank % 2 == 0
        w_pair = jnp.concatenate(
            [jnp.where(is_key, w_keyvalue, other), jnp.where(is_key, other, w_keyvalue)], axis=1
        )
    else:
        w_pair = w_keyvalue

    sections = lax.axis_size("section")
    onward = [(s, (s + 1) % sections) for s in range(sections)]
    grid = count == 8 and sections == 2

    numbers = jnp.arange(count * each, dtype=jnp.int32)
    per_request = own_table.shape[1]
    used = (lengths + page_size - 1) // page_size
    by_owner = used.reshape(count, each)
    first = (jnp.cumsum(by_owner, axis=1) - by_owner).reshape(-1)
    most = jnp.max(jnp.sum(by_owner, axis=1, keepdims=True), keepdims=True)
    for axis in ("section", "groups"):
        for bit in range(lax.axis_size(axis).bit_length() - 1):
            pairs = [(s, s ^ (1 << bit)) for s in range(lax.axis_size(axis))]
            most = jnp.maximum(most, lax.ppermute(most, axis, pairs))
    own_used = lax.dynamic_slice_in_dim(used, rank * each, each)
    heads = tuple(target // shared for target in range(count))
    info = jnp.zeros((page_size, 2 * HD), jnp.bfloat16)
    info = info.at[0, :each].set(own_table[:, 0].astype(jnp.bfloat16))
    ready = make_parcels(own_table, own_used, info, pool, heads, 2 * HD)

    table, halves = grid_arrivals() if grid else ring_arrivals(count)
    parts = 1 if grid else 2
    rows = tokens // parts
    carried = np.array([index for index, piece in enumerate(halves) if piece == parts - 1])
    senders = jnp.asarray(table, jnp.int32)[rank]
    starts = senders * tokens + jnp.asarray(halves, jnp.int32) * rows
    orders = []
    masks = jnp.array([0, 1, 6, 4, 2, 7, 5, 3] if grid else range(count), jnp.int32)
    for owners in (senders[carried], rank ^ masks):
        rows_of = jnp.repeat(owners * each, each) + numbers % each
        orders.append((numbers[:, None] == rows_of[None, :]).astype(jnp.bfloat16))
    times = lengths[None, :] + jnp.arange(STEPS, dtype=jnp.int32)[:, None]
    cosine, sine = rope_tables(times.reshape(-1))
    cosine = cosine.reshape(STEPS, count * each, HD)
    sine = sine.reshape(STEPS, count * each, HD)
    sizes = [size for size in MORE if size < pool.shape[0] - SURE] + [pool.shape[0] - SURE]
    wanted = most[0, 0] - SURE
    choice = jnp.sum((wanted > jnp.array(sizes[:-1], jnp.int32)).astype(jnp.int32))
    ready = (ready, w_pair, choice, starts, orders, cosine, sine)
    if grid:
        lines = norm_gain.reshape(-1, HD)
        *pieces, state = prepare_blocks(prompt_states[0], decode_states[0], lines)
    else:
        state = decode_states[0]
        pieces = prepare(prompt_states[0], decode_states[0], gain, parts)
    known, pending, finish, ready = (along_grid if grid else along_ring)(pieces, ready)
    ready, *_, choice, starts, orders, cosine, sine = ready

    sure, more = ready

    def exchange(pages):
        return lax.all_to_all(
            pages.reshape(count, -1, 2 * HD), "tensor", split_axis=0, concat_axis=0, tiled=True
        )

    extra = more.shape[1]

    def branch(size):
        def run(more):
            if size == 0:
                return jnp.zeros((count, extra * page_size, 2 * HD), jnp.bfloat16)
            pages = exchange(more[:, :size])
            return jnp.pad(pages, ((0, 0), (0, (extra - size) * page_size), (0, 0)))

        return run

    more = lax.switch(choice, [branch(size) for size in sizes], more)
    known, pending, more = lax.optimization_barrier((known, pending, more))
    sure, _ = lax.optimization_barrier((sure, more))
    sure = exchange(sure)

    prompt_kv = []
    blocks = []
    if grid:
        rest, halves_of_other, begins = finish(pending)
        own, other, states = project(
            known[0] + rest, w_pair, starts, 0, rows, each, halves_of_other, begins
        )
        prompt_kv = [own, cross(other)]
        blocks = [states, cross(states)]
    else:
        skipped = 0
        for group in known:
            values, states = project(group, w_pair, starts, skipped, rows, each)
            prompt_kv.append(values)
            blocks.append(states)
            skipped += len(group)
    arrived = tuple(lax.ppermute(part, "section", onward) for part in prompt_kv)
    anchor = (section + 1) % sections
    targets = lax.dynamic_index_in_dim(dest_rank, anchor, 0, keepdims=False)
    landing = lax.dynamic_index_in_dim(dest_page, anchor, 0, keepdims=False)[:, 0]
    prompts = (targets, landing, starts // PLEN, starts % PLEN, *arrived)
    held = (w_query, w_pair, w_output, sure, more)

    blocks, cosine, sine, state, gain = lax.optimization_barrier((blocks, cosine, sine, state, gain))
    outputs = []
    earlier = []
    for iteration in range(STEPS):
        chosen = orders[min(iteration, 1)]
        parts, fresh, *fetched = step(
            blocks, chosen, lengths, used, first, cosine, sine, earlier, held, each, prompts
        )
        if iteration == 0:
            held, prompts = fetched, ()
        earlier.append(fresh)
        parts = lax.all_to_all(parts, "tensor", split_axis=0, concat_axis=0, tiled=True)
        if iteration + 1 < STEPS:
            state, normed = settle(parts, state, gain)
            outputs.append(state)
            if grid:
                along = [swap_xor(normed, bits) for bits in (6, 4, 2)]
                blocks = [normed, cross(normed), *along, *(cross(block) for block in along)]
            else:
                blocks = [normed] + [swap_xor(normed, bits) for bits in range(1, count)]
    return last(parts, outputs)[:, None]


def solution(mesh):
    in_specs = (
        P(("groups", "section"), "tensor", None),
        P(("groups", "section"), "tensor", None),
        P(),
        P(None, "tensor"),
        P(None, "tensor"),
        P("tensor", None),
        P(("groups", "section"), "tensor", None, None),
        P(("groups", "section"), "tensor", None),
        P(("groups", "section"), None),
        P("groups", None),
        P("groups", None, None),
    )
    out_specs = P(None, ("groups", "section"), "tensor", None)
    return jax.shard_map(
        on_device, mesh=mesh, in_specs=in_specs, out_specs=out_specs, check_vma=False
    )
```

```python
import functools

import jax
import jax.numpy as jnp
import numpy as np
from jax import lax
from jax.experimental import pallas as pl
from jax.experimental.pallas import tpu as pltpu
from jax.sharding import PartitionSpec as P

HD = 128
PLEN = 128
STEPS = 4
EPS = 1e-05
ROPE_BASE = 500000.0
LANES = 8
CHUNKS = 8
PAGE = 16
SURE = 14
MORE = (0, 18, 22, 24, 26, 27, 28, 29, 30, 31, 32, 34, 36, 38, 42)
VMEM_LIMIT = 10 * 1024 * 1024


def ring_shift(value, steps):
    count = lax.axis_size("tensor")
    return lax.ppermute(value, "tensor", [(s, (s + steps) % count) for s in range(count)])


def swap_xor(value, mask):
    count = lax.axis_size("tensor")
    return lax.ppermute(value, "tensor", [(s, s ^ mask) for s in range(count)])


def ring_arrivals(count):
    table, halves = [np.arange(count)] * 2, [0, 1]
    for hop in range(1, count // 2 + 1):
        for piece in range(2):
            for way in range(2):
                if hop < count // 2 or piece == way:
                    table.append((np.arange(count) - (1 - 2 * way) * hop) % count)
                    halves.append(piece)
    return np.stack(table, axis=1), halves


def along_ring(pieces, ready):
    count = lax.axis_size("tensor")
    blocks = list(pieces)
    going = [[rows, rows] for rows in pieces]
    for hop in range(1, count // 2 + 1):
        for piece in range(2):
            for way in range(2):
                if hop < count // 2 or piece == way:
                    going[piece][way] = ring_shift(going[piece][way], 1 - 2 * way)
                    blocks.append(going[piece][way])
        if hop == 1:
            going, ready = lax.optimization_barrier((going, ready))
    return [blocks[at : at + 8] for at in range(0, len(blocks), 8)], (), lambda pending: [], ready


def cross(value):
    return lax.ppermute(value, "tensor", [(r, r ^ 1) for r in range(8)])


def grid_arrivals():
    table = []
    for across in (0, 1):
        for origin in ((0, 1, 2, 3), (1, 0, 3, 2), (2, 2, 1, 1), (3, 3, 0, 0)):
            table.append(np.array([(2 * origin[r // 2] + r % 2) ^ across for r in range(8)]))
    return np.stack(table, axis=1), [0] * 8


def along_grid(pieces, ready):
    z = lax.axis_index("tensor") // 2

    def shift(rows, steps, starts):
        pairs = [(2 * s + c, 2 * (s + steps) + c) for s in starts for c in range(2)]
        return lax.ppermute(rows, "tensor", pairs)

    def pick(*rows):
        return jnp.where(z == 0, rows[0], jnp.where(z == 1, rows[1], jnp.where(z == 2, rows[2], rows[3])))

    (rows,) = pieces
    up, down = shift(rows, 1, (0, 1, 2)), shift(rows, -1, (1, 2, 3))
    up, down, parcels, weight = lax.optimization_barrier((up, down, *ready[:2]))
    section = lax.axis_index("section")
    half = weight.shape[0] // 2
    brought = cross(lax.dynamic_slice_in_dim(weight, section * half, half))
    ready = (parcels, *ready[2:])
    up2, down2 = shift(up, 1, (1, 2)), shift(down, -1, (1, 2))
    up2, down2, ready = lax.optimization_barrier((up2, down2, ready))
    outward = jnp.where(z == 1, down2, up2)
    ends = lax.ppermute(outward, "tensor", [(2, 0), (3, 1), (4, 6), (5, 7)])

    def finish(pending):
        up, down, up2, down2, ends, brought = pending
        given = lax.ppermute(brought, "section", [(0, 1), (1, 0)])
        begins = jnp.stack([section * half, (1 - section) * half]).astype(jnp.int32)
        second = pick(down, up, down, up)
        third = pick(down2, down, up, up2)
        fourth = pick(ends, down2, up2, ends)
        return [second, third, fourth], (brought, given), begins

    return [[rows]], (up, down, up2, down2, ends, brought), finish, ready


def rope_tables(positions, lib=jnp):
    half_dim = HD // 2
    freqs = ROPE_BASE ** (-(lib.arange(half_dim, dtype=lib.float32) * 2.0 / HD))
    angles = positions.astype(lib.float32)[:, None] * freqs[None, :].astype(lib.float32)
    cosine = lib.cos(angles)
    sine = lib.sin(angles)
    return (
        lib.concatenate([cosine, cosine], axis=1).astype(lib.float32),
        lib.concatenate([-sine, sine], axis=1).astype(lib.float32),
    )


def whole():
    return pl.BlockSpec(memory_space=pltpu.VMEM)


def normed_rows(values, gain):
    square = jnp.mean(values * values, axis=-1, keepdims=True)
    return values * lax.rsqrt(square + EPS) * gain


def prepare_kernel(prompt_ref, state_ref, gain_ref, *out_refs):
    tokens, width = prompt_ref.shape
    rows = tokens // len(out_refs)
    gain = gain_ref[...].astype(jnp.float32)
    for index, out_ref in enumerate(out_refs):
        part = prompt_ref[index * rows : (index + 1) * rows, :].astype(jnp.float32)
        out_ref[:rows, :] = normed_rows(part, gain).astype(jnp.bfloat16)
    states = normed_rows(state_ref[...].astype(jnp.float32), gain)
    filling = jnp.zeros((out_refs[-1].shape[0] - rows - states.shape[0], width), jnp.float32)
    out_refs[-1][rows:, :] = jnp.concatenate([states, filling], axis=0).astype(jnp.bfloat16)


def prepare(prompts, states, gain, pieces):
    tokens, width = prompts.shape
    rows = [tokens // pieces] * pieces
    rows[-1] += -(-states.shape[0] // LANES) * LANES
    return pl.pallas_call(
        prepare_kernel,
        out_shape=tuple(jax.ShapeDtypeStruct((count, width), jnp.bfloat16) for count in rows),
        in_specs=[whole()] * 3,
        out_specs=tuple(whole() for _ in rows),
        compiler_params=pltpu.CompilerParams(vmem_limit_bytes=VMEM_LIMIT),
        name="prepare",
    )(prompts, states, gain)


def prepare_blocks_kernel(prompt_in, state_in, gain_ref, out_ref, states, prompts, sems):
    each = state_in.shape[0]
    copies = [
        pltpu.make_async_copy(prompt_in, prompts, sems.at[0]),
        pltpu.make_async_copy(state_in, states, sems.at[1]),
    ]
    for copy in copies:
        copy.start()
    gain = gain_ref[...].astype(jnp.float32)
    lanes = gain.shape[1]
    for copy, rows_ref, first in zip(copies, (prompts, states), (0, prompts.shape[0] // each)):
        copy.wait()
        values = rows_ref[...].astype(jnp.float32)
        factor = lax.rsqrt(jnp.mean(values * values, axis=-1, keepdims=True) + EPS)
        for c in range(gain.shape[0]):
            part = slice(c * lanes, (c + 1) * lanes)
            normed = rows_ref[:, part].astype(jnp.float32) * factor * gain[c : c + 1, :]
            for block in range(rows_ref.shape[0] // each):
                rows = normed[block * each : (block + 1) * each, :]
                out_ref[first + block, :, part] = rows.astype(jnp.bfloat16)


def prepare_blocks(prompts, states, gain):
    tokens, width = prompts.shape
    each = states.shape[0]
    hbm = pl.BlockSpec(memory_space=pltpu.HBM)
    return pl.pallas_call(
        prepare_blocks_kernel,
        out_shape=(
            jax.ShapeDtypeStruct((tokens // each + 1, each, width), jnp.bfloat16),
            jax.ShapeDtypeStruct(states.shape, jnp.bfloat16),
        ),
        in_specs=[hbm, hbm, whole()],
        out_specs=(whole(), whole()),
        scratch_shapes=[
            pltpu.VMEM(prompts.shape, jnp.bfloat16),
            pltpu.SemaphoreType.DMA((2,)),
        ],
        compiler_params=pltpu.CompilerParams(vmem_limit_bytes=VMEM_LIMIT),
        name="prepare",
    )(
        pltpu.with_memory_space_constraint(prompts, pltpu.HBM),
        pltpu.with_memory_space_constraint(states, pltpu.HBM),
        gain,
    )


def project_kernel(rows, each, skipped, halves, *refs):
    heads = 2 if halves else 1
    used = 7 + halves + 2 * heads
    blocks, refs = refs[:-used], refs[-used:]
    starts_ref, begins_ref, cos_ref, sin_ref = refs[:4]
    weight_ref, part_refs = refs[4], refs[5 : 5 + halves]
    out_refs = refs[5 + halves : 5 + halves + heads]
    states_ref, staged = refs[-2 - heads : -heads]
    sum_refs = refs[-heads:]
    depth = weight_ref.shape[0] // CHUNKS

    def stage(span):
        for index, block in enumerate(blocks):
            begin = index * rows
            if block.ndim == 2:
                staged[begin : begin + rows, :] = block[:rows, span].astype(jnp.float32)
                continue
            for piece in range(rows // each):
                here = slice(begin + piece * each, begin + (piece + 1) * each)
                staged[here, :] = block[piece, :, span].astype(jnp.float32)
        return staged[...].astype(jnp.bfloat16)

    for sum_ref in sum_refs:
        sum_ref[...] = jnp.zeros_like(sum_ref)

    def add(shift, count, part_ref=None):
        @pl.loop(0, count)
        def _(c):
            there = pl.ds(pl.multiple_of(shift + c * depth, depth), depth)
            x = stage(there)
            sum_refs[0][...] += jnp.dot(
                x, weight_ref[there, :], preferred_element_type=jnp.float32
            )
            if part_ref is not None:
                here = pl.ds(pl.multiple_of(c * depth, depth), depth)
                sum_refs[1][...] += jnp.dot(
                    x, part_ref[here, :], preferred_element_type=jnp.float32
                )

    if not halves:
        add(0, CHUNKS)
    for index, part_ref in enumerate(part_refs):
        add(begins_ref[index], part_ref.shape[0] // depth, part_ref)
    totals = [sum_ref[...] for sum_ref in sum_refs]
    for total, out_ref in zip(totals, out_refs):
        out_ref[:, HD:] = total[:, HD:].astype(jnp.bfloat16)
        for index in range(len(blocks)):
            begin = starts_ref[skipped + index] % PLEN
            span = pl.ds(pl.multiple_of(begin, rows), rows)
            here = slice(index * rows, (index + 1) * rows)
            keys = turn(total[here, :HD], cos_ref[span, :], sin_ref[span, :])
            out_ref[here, :HD] = keys.astype(jnp.bfloat16)
    found = 0
    for block in blocks:
        if block.ndim == 3:
            states_ref[found] = block[rows // each]
            found += 1
        elif block.shape[0] > rows:
            states_ref[found] = block[rows:, :].astype(jnp.float32)[:each, :].astype(jnp.bfloat16)
            found += 1


def project(blocks, weight, starts, skipped, rows, each, parts=(), begins=None):
    width = weight.shape[0]
    cosine, sine = rope_tables(np.arange(PLEN), np)
    carrying = sum(block.ndim == 3 or block.shape[0] > rows for block in blocks)
    heads = 2 if parts else 1
    values = jax.ShapeDtypeStruct((len(blocks) * rows, 2 * HD), jnp.bfloat16)
    out_shape = [values] * heads
    out_shape.append(jax.ShapeDtypeStruct((carrying, each, width), jnp.bfloat16))
    smem = pl.BlockSpec(memory_space=pltpu.SMEM)
    begins = jnp.zeros((2,), jnp.int32) if begins is None else begins
    return pl.pallas_call(
        functools.partial(project_kernel, rows, each, skipped, len(parts)),
        out_shape=tuple(out_shape),
        in_specs=[whole()] * len(blocks) + [smem] * 2 + [whole()] * (3 + len(parts)),
        out_specs=tuple(whole() for _ in out_shape),
        scratch_shapes=[
            pltpu.VMEM((len(blocks) * rows, width // CHUNKS), jnp.float32),
            *[pltpu.VMEM(values.shape, jnp.float32)] * heads,
        ],
        compiler_params=pltpu.CompilerParams(vmem_limit_bytes=VMEM_LIMIT),
        cost_estimate=pl.CostEstimate(
            flops=2 * len(blocks) * rows * weight.size * heads,
            bytes_accessed=2 * weight.size * heads,
            transcendentals=0,
        ),
        name="project",
    )(*blocks, starts, begins, cosine, sine, weight, *parts)


def parcels_kernel(heads, table_ref, used_ref, info_ref, pool_ref, sure_ref, more_ref, held, load_sem, store_sem):
    width = sure_ref.shape[-1]
    each, per_request = table_ref.shape
    pages = each * per_request
    sure = sure_ref.shape[1] - 1
    stores = []
    for target in range(len(heads)):
        copy = pltpu.make_async_copy(info_ref, sure_ref.at[target, 0], store_sem.at[0, target])
        copy.start()
        stores.append(copy)
    front = jnp.int32(0)
    back = used_ref[0]
    for r in range(1, each):
        back = back + used_ref[r]
    loads = []
    for r in range(each):
        used = used_ref[r]
        for p in range(per_request):
            spot = jnp.where(p < used, front + p, back + p - used)
            copy = pltpu.make_async_copy(
                pool_ref.at[table_ref[r, p]], held.at[spot], load_sem.at[r * per_request + p]
            )
            copy.start()
            loads.append(copy)
        front = front + used
        back = back + per_request - used
    for copy in loads:
        copy.wait()
    for target, head in enumerate(heads):
        columns = pl.ds(head * width, width)
        for bank, source, goal in (
            (1, held.at[pl.ds(0, sure), :, columns], sure_ref.at[target, pl.ds(1, sure)]),
            (2, held.at[pl.ds(sure, pages - sure), :, columns], more_ref.at[target]),
        ):
            copy = pltpu.make_async_copy(source, goal, store_sem.at[bank, target])
            copy.start()
            stores.append(copy)
    for copy in stores:
        copy.wait()


def make_parcels(table, used, info, pool, heads, width):
    pages, rows, _ = pool.shape
    hbm = pl.BlockSpec(memory_space=pltpu.HBM)
    smem = pl.BlockSpec(memory_space=pltpu.SMEM)
    return pl.pallas_call(
        functools.partial(parcels_kernel, heads),
        out_shape=(
            pltpu.HBM((len(heads), SURE + 1, rows, width), jnp.bfloat16),
            pltpu.HBM((len(heads), pages - SURE, rows, width), jnp.bfloat16),
        ),
        in_specs=[smem, smem, whole(), hbm],
        out_specs=(hbm, hbm),
        scratch_shapes=[
            pltpu.VMEM(pool.shape, jnp.bfloat16),
            pltpu.SemaphoreType.DMA((pages,)),
            pltpu.SemaphoreType.DMA((3, len(heads))),
        ],
        compiler_params=pltpu.CompilerParams(vmem_limit_bytes=VMEM_LIMIT),
        name="parcels",
    )(table, used, info, pltpu.with_memory_space_constraint(pool, pltpu.HBM))


def turn(values, cosine, sine):
    return values * cosine + pltpu.roll(values, HD // 2, 1) * sine


def step_kernel(blocks, iteration, groups, each, *refs):
    x_refs = refs[:blocks]
    order_ref, lens_ref, used_ref, first_ref, cos_ref, sin_ref = refs[blocks : blocks + 6]
    new_refs = refs[blocks + 6 : blocks + 6 + iteration]
    refs = refs[blocks + 6 + iteration :]
    if iteration == 0:
        target_ref, landing_ref, prompt_ref, offset_ref = refs[:4]
        arrived_refs = refs[4 : 4 + groups]
        refs = refs[4 + groups :]
        wq_in, wkv_in, wo_in, sure_in, more_in, out_ref, fresh_ref, wq, wkv, wo, cache = refs[:11]
        x_rows, q_s, score_s, mix_s, new_s, sems, patch_sems = refs[11:]
    else:
        wq, wkv, wo, cache = refs[:4]
        out_ref, fresh_ref, x_rows, q_s, score_s, mix_s, new_s = refs[4:]
    width, q_cols = wq.shape
    owners = cache.shape[0]
    count = owners * each
    span = (cache.shape[1] // PAGE - 1) // each * PAGE
    heads = q_cols // HD
    depth = width // CHUNKS

    waits = {}
    if iteration == 0:
        for c in range(CHUNKS):
            part = pl.ds(c * depth, depth)
            waits[c] = [
                pltpu.make_async_copy(wq_in.at[part, :], wq.at[part, :], sems.at[0, c]),
                pltpu.make_async_copy(wkv_in.at[part, :], wkv.at[part, :], sems.at[1, c]),
            ]
            waits["out", c] = [pltpu.make_async_copy(wo_in.at[:, part], wo.at[:, part], sems.at[2, c])]
        sure = sure_in.shape[1]
        waits["cache"] = [
            pltpu.make_async_copy(sure_in, cache.at[:, pl.ds(0, sure), :], sems.at[3, 0]),
            pltpu.make_async_copy(
                more_in, cache.at[:, pl.ds(sure, more_in.shape[1]), :], sems.at[3, 1]
            ),
        ]
        for name in [0, 1, 2, 3, "cache", 4, 5, 6, 7]:
            for copy in waits[name]:
                copy.start()

    def wait(name):
        for copy in waits.get(name, ()):
            copy.wait()

    def receivers():
        lines = [
            cache[owner, :PAGE, :HD].astype(jnp.float32)[:1, :] for owner in range(owners)
        ]
        firsts = jnp.concatenate(lines, axis=0)
        owner = lax.broadcasted_iota(jnp.int32, firsts.shape, 0)
        slot = lax.broadcasted_iota(jnp.int32, firsts.shape, 1)
        numbers = (owner * each + slot).astype(jnp.float32)
        found = []
        for k in range(target_ref.shape[0]):
            here = (owner == target_ref[k]) & (slot < each)
            here = here & (firsts == landing_ref[k].astype(jnp.float32))
            found.append(jnp.sum(jnp.where(here, numbers, 0.0)).astype(jnp.int32))
        return found

    def window(r, size, page=0):
        return pl.ds(pl.multiple_of((first_ref[r] + page + 1) * PAGE, PAGE), size)

    def patch(requests, action):
        pieces = offset_ref.shape[0]
        rows = sum(ref.shape[0] for ref in arrived_refs) // pieces
        piece = 0
        for ref in arrived_refs:
            for local in range(ref.shape[0] // rows):
                request = jnp.int32(0)
                for k, number in enumerate(requests):
                    request = jnp.where(prompt_ref[piece] == k, number, request)
                for p in range(rows // PAGE):
                    page = offset_ref[piece] // PAGE + p

                    @pl.when(page < used_ref[request])
                    def _():
                        copy = pltpu.make_async_copy(
                            ref.at[pl.ds(local * rows + p * PAGE, PAGE), :],
                            cache.at[request // each, window(request, PAGE, page), :],
                            patch_sems.at[piece, p],
                        )
                        action(copy)

                piece += 1

    place = 0
    for ref in x_refs:
        for rows in [ref[...]] if ref.ndim == 2 else [ref[k] for k in range(ref.shape[0])]:
            x_rows[place : place + each, :] = rows.astype(jnp.float32)
            place += each
    order = order_ref[...]

    query = jnp.zeros((count, q_cols), jnp.float32)
    keyvalue = jnp.zeros((count, 2 * HD), jnp.float32)
    for c in range(CHUNKS):
        part = slice(c * depth, (c + 1) * depth)
        x = jnp.dot(
            order, x_rows[:, part].astype(jnp.bfloat16), preferred_element_type=jnp.float32
        ).astype(jnp.bfloat16)
        wait(c)
        if iteration == 0:
            for copy in waits["out", c]:
                copy.start()
        query += jnp.dot(x, wq[part, :], preferred_element_type=jnp.float32)
        keyvalue += jnp.dot(x, wkv[part, :], preferred_element_type=jnp.float32)
        if iteration == 0 and c == CHUNKS - 2:
            wait("cache")
            requests = receivers()
            patch(requests, lambda copy: copy.start())

    cosine = cos_ref[iteration]
    sine = sin_ref[iteration]
    key = turn(keyvalue[:, :HD], cosine, sine).astype(jnp.bfloat16)
    value = keyvalue[:, HD:].astype(jnp.bfloat16)
    fresh_ref[:, :HD] = key
    fresh_ref[:, HD:] = value
    news = [(ref[:, :HD], ref[:, HD:]) for ref in new_refs] + [(key, value)]
    for j in range(LANES):
        lane = pl.ds(j, count, LANES)
        if j < heads:
            turned = turn(query[:, j * HD : (j + 1) * HD], cosine, sine).astype(jnp.bfloat16)
            q_s[lane, :] = turned.astype(jnp.float32)
        else:
            q_s[lane, :] = jnp.zeros((count, HD), jnp.float32)
        for t, pair in enumerate(news):
            for half in range(2):
                new_s[t, half, lane, :] = pair[half].astype(jnp.float32)

    if iteration == 0:
        patch(requests, lambda copy: copy.wait())
    scale = HD**-0.5
    column = lax.broadcasted_iota(jnp.int32, (LANES, span), 1)
    for r in range(count):
        rows = slice(r * LANES, (r + 1) * LANES)
        found = lax.dot_general(
            q_s[rows, :].astype(jnp.bfloat16),
            cache[r // each, window(r, span), :HD],
            (((1,), (1,)), ((), ())),
            preferred_element_type=jnp.float32,
        )
        score_s[rows, :] = jnp.where(column < lens_ref[r], found * scale, -1e30)

    scores = score_s[...]
    queries = q_s[...]
    fresh_scores = [
        jnp.sum(queries * new_s[t, 0], axis=-1, keepdims=True) * scale for t in range(iteration + 1)
    ]
    top = jnp.max(scores, axis=-1, keepdims=True)
    for s in fresh_scores:
        top = jnp.maximum(top, s)
    weights = jnp.exp(scores - top)
    fresh_weights = [jnp.exp(s - top) for s in fresh_scores]
    total = jnp.sum(weights, axis=-1, keepdims=True)
    for w in fresh_weights:
        total = total + w
    score_s[...] = weights / total
    row = lax.broadcasted_iota(jnp.int32, (span, HD), 0)
    for r in range(count):
        rows = slice(r * LANES, (r + 1) * LANES)
        mix_s[rows, :] = jnp.dot(
            score_s[rows, :].astype(jnp.bfloat16),
            jnp.where(
                row < lens_ref[r],
                cache[r // each, window(r, span), HD:],
                jnp.zeros((), jnp.bfloat16),
            ),
            preferred_element_type=jnp.float32,
        )
    mixed = mix_s[...]
    for t in range(iteration + 1):
        weight = (fresh_weights[t] / total).astype(jnp.bfloat16).astype(jnp.float32)
        mixed = mixed + weight * new_s[t, 1]
    mix_s[...] = mixed
    columns = jnp.concatenate(
        [mix_s[pl.ds(j, count, LANES), :].astype(jnp.bfloat16) for j in range(heads)], axis=1
    )
    for c in range(CHUNKS):
        part = slice(c * depth, (c + 1) * depth)
        wait(("out", c))
        product = jnp.dot(columns, wo[:, part], preferred_element_type=jnp.float32)
        for d in range(owners):
            out_ref[d, :, part] = product[d * each : (d + 1) * each, :].astype(jnp.bfloat16)


def step(x_blocks, order, lengths, used, first, cosine, sine, earlier, held, each, prompts=()):
    width, q_cols = held[0].shape
    owners = held[3].shape[0]
    count = owners * each
    cached = sum(a.shape[1] for a in held[3:])
    span = (cached // PAGE - 1) // each * PAGE
    iteration = len(earlier)
    blocks = len(x_blocks)
    groups = max(len(prompts) - 4, 0)
    smem = pl.BlockSpec(memory_space=pltpu.SMEM)
    hbm = pl.BlockSpec(memory_space=pltpu.HBM)
    anywhere = pl.BlockSpec(memory_space=pl.ANY)
    out_shape = [
        jax.ShapeDtypeStruct((owners, each, width), jnp.bfloat16),
        jax.ShapeDtypeStruct((count, 2 * HD), jnp.bfloat16),
    ]
    in_specs = [whole()] * (blocks + 1) + [smem] * 3 + [whole()] * (2 + iteration)
    scratch = [
        pltpu.VMEM((count, width), jnp.float32),
        pltpu.VMEM((count * LANES, HD), jnp.float32),
        pltpu.VMEM((count * LANES, span), jnp.float32),
        pltpu.VMEM((count * LANES, HD), jnp.float32),
        pltpu.VMEM((iteration + 1, 2, count * LANES, HD), jnp.float32),
    ]
    if iteration == 0:
        in_specs += [smem] * 4 + [whole()] * groups + [hbm] * 3 + [anywhere] * 2
        out_shape += [pltpu.VMEM(a.shape, a.dtype) for a in held[:3]]
        out_shape.append(pltpu.VMEM((owners, cached, 2 * HD), jnp.bfloat16))
        held = [pltpu.with_memory_space_constraint(a, pltpu.HBM) for a in held[:3]] + list(held[3:])
        pieces = prompts[3].shape[0]
        pages = sum(a.shape[0] for a in prompts[4:]) // pieces // PAGE
        scratch.append(pltpu.SemaphoreType.DMA((4, CHUNKS)))
        scratch.append(pltpu.SemaphoreType.DMA((pieces, pages)))
    else:
        in_specs += [whole()] * 4
    return pl.pallas_call(
        functools.partial(step_kernel, blocks, iteration, groups, each),
        out_shape=tuple(out_shape),
        in_specs=in_specs,
        out_specs=tuple(whole() for _ in out_shape),
        scratch_shapes=scratch,
        compiler_params=pltpu.CompilerParams(vmem_limit_bytes=VMEM_LIMIT),
        cost_estimate=pl.CostEstimate(
            flops=2 * count * width * (2 * q_cols + 2 * HD),
            bytes_accessed=2 * sum(a.size for a in held),
            transcendentals=count * LANES * span,
        ),
        name="decode_step",
    )(*x_blocks, order, lengths, used, first, cosine, sine, *earlier, *prompts, *held)


def settle_kernel(parts_ref, state_ref, gain_ref, next_ref, normed_ref):
    total = parts_ref[0].astype(jnp.float32)
    for d in range(1, parts_ref.shape[0]):
        total = total + parts_ref[d].astype(jnp.float32)
    state = (state_ref[...].astype(jnp.float32) + total).astype(jnp.bfloat16)
    next_ref[...] = state
    gain = gain_ref[...].astype(jnp.float32)
    normed_ref[...] = normed_rows(state.astype(jnp.float32), gain).astype(jnp.bfloat16)


def last_kernel(parts_ref, *refs):
    state_refs, out_ref = refs[:-1], refs[-1]
    total = parts_ref[0].astype(jnp.float32)
    for d in range(1, parts_ref.shape[0]):
        total = total + parts_ref[d].astype(jnp.float32)
    for index, state_ref in enumerate(state_refs):
        out_ref[index] = state_ref[...]
    out_ref[len(state_refs)] = (state_refs[-1][...].astype(jnp.float32) + total).astype(jnp.bfloat16)


def last(parts, states):
    return pl.pallas_call(
        last_kernel,
        out_shape=jax.ShapeDtypeStruct((len(states) + 1, *states[0].shape), jnp.bfloat16),
        in_specs=[whole()] * (1 + len(states)),
        out_specs=whole(),
        compiler_params=pltpu.CompilerParams(vmem_limit_bytes=VMEM_LIMIT),
        name="last",
    )(parts, *states)


def settle(parts, state, gain):
    shape = jax.ShapeDtypeStruct(state.shape, jnp.bfloat16)
    return pl.pallas_call(
        settle_kernel,
        out_shape=(shape, shape),
        in_specs=[whole()] * 3,
        out_specs=(whole(), whole()),
        compiler_params=pltpu.CompilerParams(vmem_limit_bytes=VMEM_LIMIT),
        name="settle",
    )(parts, state, gain)


def on_device(
    prompt_states,
    decode_states,
    norm_gain,
    w_query,
    w_keyvalue,
    w_output,
    cache_pages,
    page_table,
    cache_len,
    dest_rank,
    dest_page,
):
    rank = lax.axis_index("tensor")
    section = lax.axis_index("section")
    count = lax.axis_size("tensor")
    pool = cache_pages[0]
    page_size, kv_width = pool.shape[1:]
    own_table = page_table[0]
    lengths = cache_len[0]
    each, width = decode_states.shape[1:]
    tokens = prompt_states.shape[1]
    q_cols = w_query.shape[1]
    kv_heads = kv_width // (2 * HD)
    shared = count // kv_heads if count > kv_heads else 1
    gain = norm_gain[None, :]

    if w_keyvalue.shape[1] < 2 * HD:
        other = swap_xor(w_keyvalue, 1)
        is_key = rank % 2 == 0
        w_pair = jnp.concatenate(
            [jnp.where(is_key, w_keyvalue, other), jnp.where(is_key, other, w_keyvalue)], axis=1
        )
    else:
        w_pair = w_keyvalue

    sections = lax.axis_size("section")
    onward = [(s, (s + 1) % sections) for s in range(sections)]
    grid = count == 8 and sections == 2

    numbers = jnp.arange(count * each, dtype=jnp.int32)
    per_request = own_table.shape[1]
    used = (lengths + page_size - 1) // page_size
    by_owner = used.reshape(count, each)
    first = (jnp.cumsum(by_owner, axis=1) - by_owner).reshape(-1)
    most = jnp.max(jnp.sum(by_owner, axis=1, keepdims=True), keepdims=True)
    for axis in ("section", "groups"):
        for bit in range(lax.axis_size(axis).bit_length() - 1):
            pairs = [(s, s ^ (1 << bit)) for s in range(lax.axis_size(axis))]
            most = jnp.maximum(most, lax.ppermute(most, axis, pairs))
    own_used = lax.dynamic_slice_in_dim(used, rank * each, each)
    heads = tuple(target // shared for target in range(count))
    info = jnp.zeros((page_size, 2 * HD), jnp.bfloat16)
    info = info.at[0, :each].set(own_table[:, 0].astype(jnp.bfloat16))
    ready = make_parcels(own_table, own_used, info, pool, heads, 2 * HD)

    table, halves = grid_arrivals() if grid else ring_arrivals(count)
    parts = 1 if grid else 2
    rows = tokens // parts
    carried = np.array([index for index, piece in enumerate(halves) if piece == parts - 1])
    senders = jnp.asarray(table, jnp.int32)[rank]
    starts = senders * tokens + jnp.asarray(halves, jnp.int32) * rows
    orders = []
    masks = jnp.array([0, 1, 6, 4, 2, 7, 5, 3] if grid else range(count), jnp.int32)
    for owners in (senders[carried], rank ^ masks):
        rows_of = jnp.repeat(owners * each, each) + numbers % each
        orders.append((numbers[:, None] == rows_of[None, :]).astype(jnp.bfloat16))
    times = lengths[None, :] + jnp.arange(STEPS, dtype=jnp.int32)[:, None]
    cosine, sine = rope_tables(times.reshape(-1))
    cosine = cosine.reshape(STEPS, count * each, HD)
    sine = sine.reshape(STEPS, count * each, HD)
    sizes = [size for size in MORE if size < pool.shape[0] - SURE] + [pool.shape[0] - SURE]
    wanted = most[0, 0] - SURE
    choice = jnp.sum((wanted > jnp.array(sizes[:-1], jnp.int32)).astype(jnp.int32))
    ready = (ready, w_pair, choice, starts, orders, cosine, sine)
    if grid:
        lines = norm_gain.reshape(-1, HD)
        *pieces, state = prepare_blocks(prompt_states[0], decode_states[0], lines)
    else:
        state = decode_states[0]
        pieces = prepare(prompt_states[0], decode_states[0], gain, parts)
    known, pending, finish, ready = (along_grid if grid else along_ring)(pieces, ready)
    ready, *_, choice, starts, orders, cosine, sine = ready

    sure, more = ready

    def exchange(pages):
        return lax.all_to_all(
            pages.reshape(count, -1, 2 * HD), "tensor", split_axis=0, concat_axis=0, tiled=True
        )

    extra = more.shape[1]

    def branch(size):
        def run(more):
            if size == 0:
                return jnp.zeros((count, extra * page_size, 2 * HD), jnp.bfloat16)
            pages = exchange(more[:, :size])
            return jnp.pad(pages, ((0, 0), (0, (extra - size) * page_size), (0, 0)))

        return run

    more = lax.switch(choice, [branch(size) for size in sizes], more)
    known, pending, more = lax.optimization_barrier((known, pending, more))
    sure, _ = lax.optimization_barrier((sure, more))
    sure = exchange(sure)

    prompt_kv = []
    blocks = []
    if grid:
        rest, halves_of_other, begins = finish(pending)
        own, other, states = project(
            known[0] + rest, w_pair, starts, 0, rows, each, halves_of_other, begins
        )
        prompt_kv = [own, cross(other)]
        blocks = [states, cross(states)]
    else:
        skipped = 0
        for group in known:
            values, states = project(group, w_pair, starts, skipped, rows, each)
            prompt_kv.append(values)
            blocks.append(states)
            skipped += len(group)
    arrived = tuple(lax.ppermute(part, "section", onward) for part in prompt_kv)
    anchor = (section + 1) % sections
    targets = lax.dynamic_index_in_dim(dest_rank, anchor, 0, keepdims=False)
    landing = lax.dynamic_index_in_dim(dest_page, anchor, 0, keepdims=False)[:, 0]
    prompts = (targets, landing, starts // PLEN, starts % PLEN, *arrived)
    held = (w_query, w_pair, w_output, sure, more)

    blocks, cosine, sine, state, gain = lax.optimization_barrier((blocks, cosine, sine, state, gain))
    outputs = []
    earlier = []
    for iteration in range(STEPS):
        chosen = orders[min(iteration, 1)]
        parts, fresh, *fetched = step(
            blocks, chosen, lengths, used, first, cosine, sine, earlier, held, each, prompts
        )
        if iteration == 0:
            held, prompts = fetched, ()
        earlier.append(fresh)
        parts = lax.all_to_all(parts, "tensor", split_axis=0, concat_axis=0, tiled=True)
        if iteration + 1 < STEPS:
            state, normed = settle(parts, state, gain)
            outputs.append(state)
            if grid:
                along = [swap_xor(normed, bits) for bits in (6, 4, 2)]
                blocks = [normed, cross(normed), *along, *(cross(block) for block in along)]
            else:
                blocks = [normed] + [swap_xor(normed, bits) for bits in range(1, count)]
    return last(parts, outputs)[:, None]


def solution(mesh):
    in_specs = (
        P(("groups", "section"), "tensor", None),
        P(("groups", "section"), "tensor", None),
        P(),
        P(None, "tensor"),
        P(None, "tensor"),
        P("tensor", None),
        P(("groups", "section"), "tensor", None, None),
        P(("groups", "section"), "tensor", None),
        P(("groups", "section"), None),
        P("groups", None),
        P("groups", None, None),
    )
    out_specs = P(None, ("groups", "section"), "tensor", None)
    return jax.shard_map(
        on_device, mesh=mesh, in_specs=in_specs, out_specs=out_specs, check_vma=False
    )
```
